32 devices in a mesh: fsdp: 32 (over z, y, x, core).
Axes of the slice: x: 2, y: 2, z: 4, core: 2. Of those that a mesh axis runs over, the one named last changes fastest.
Arguments:
- latents_in: bfloat16 [128, 256, 384], P('fsdp'), may hold values from -6 to 6
- condition: bfloat16 [128, 384], P('fsdp'), may hold values from -6 to 6
- counts: int32 [32], P('fsdp'), may hold values from 3 to 4, as said below
- ada_weight: bfloat16 [2, 884736], P(None, 'fsdp'), may hold values from -0.3125 to 0.3125
- qkv_weight: bfloat16 [2, 442368], P(None, 'fsdp'), may hold values from -0.3125 to 0.3125
- proj_weight: bfloat16 [2, 147456], P(None, 'fsdp'), may hold values from -2.5 to 2.5
- fc1_weight: bfloat16 [2, 589824], P(None, 'fsdp'), may hold values from -0.3125 to 0.3125
- fc2_weight: bfloat16 [2, 589824], P(None, 'fsdp'), may hold values from -0.15625 to 0.15625
- biases: bfloat16 [2, 8192], P(None, 'fsdp'), may hold values from -3 to 3
- cotangent: bfloat16 [128, 256, 384], P('fsdp'), may hold values from -6 to 6
Outputs:
- latents_out: float32 [128, 256, 384], P('fsdp')
- latents_grad: float32 [128, 256, 384], P('fsdp')
- condition_grad: float32 [128, 384], P('fsdp')
- ada_grad: float32 [2, 884736], P(None, 'fsdp')
- qkv_grad: float32 [2, 442368], P(None, 'fsdp')
- proj_grad: float32 [2, 147456], P(None, 'fsdp')
- fc1_grad: float32 [2, 589824], P(None, 'fsdp')
- fc2_grad: float32 [2, 589824], P(None, 'fsdp')
- bias_grad: float32 [2, 8192], P(None, 'fsdp')
The draws below stay inside these ranges and needn't reach their ends.
Inputs may be any that keep to these rules, and one draw needn't show every extreme that they name: Each device holds 3 or 4 latents, in its first slots; both counts occur in every draw.
All inputs are finite; a program needn't handle non-finite values.
Results may differ from the reference program's by a relative error of at most 0.022.
The reference program's roundings to bfloat16 on the way count: a program that leaves them out, or rounds other values in their place, can miss the bound.
Values may be sent and summed in bfloat16 or wider, within the bound.
No kernel may reach another device: no remote copies, remote signals or barrier semaphores. Data moves between devices by JAX's collectives and lax.ppermute only.
A program may use at most 192 MiB of HBM per device.

```python
import math
import jax
import jax.numpy as jnp
from jax import lax

D = 384
HEADS = 6
HEAD = 64
FF = 1536
SEQ = 256
LAYERS = 2
CAP = 4
SHARDS = 32
SLOTS = 128
ADA_PAD = 884736
QKV_PAD = 442368
PROJ_PAD = 147456
FC1_PAD = 589824
FC2_PAD = 589824
BIAS_PAD = 8192


def draw_counts(key, part):
    key = jax.random.fold_in(key, 11)
    key_base, key_full, key_gap = jax.random.split(key, 3)
    counted = jax.random.randint(key_base, (SHARDS,), CAP - 1, CAP + 1)
    fullest = jax.random.randint(key_full, (), 0, SHARDS)
    lightest = (fullest + 1 + jax.random.randint(key_gap, (), 0, SHARDS - 1)) % SHARDS
    positions = jnp.arange(SHARDS)
    counted = jnp.where(positions == fullest, CAP, counted)
    counted = jnp.where(positions == lightest, CAP - 1, counted)
    return counted.astype(jnp.int32)


def block_levels(own_key, extent, pieces, low, top_value):
    gain, own = 1.0, jax.random.fold_in(own_key, 6)
    for dim, shards_of in pieces:
        draws = jnp.exp(jax.random.uniform(jax.random.fold_in(own, dim), (shards_of,), jnp.float32, low / len(pieces), top_value / len(pieces)))
        gain = gain * jnp.repeat(draws, extent[dim] // shards_of).reshape([-1 if axis == dim else 1 for axis in range(len(extent))])
    return gain


def bell_draw(rng, dims, scale, reach, shards=(), held_as=jnp.bfloat16):
    factor_of = block_levels(rng, dims, shards, -0.22, 0.18) if shards else 1.0
    array = jax.random.normal(rng, dims, jnp.float32) * scale * factor_of
    return jnp.minimum(jnp.maximum(array, -reach), reach).astype(held_as)


def setup_inputs(seed: int = 0) -> dict:
    key_of = jax.random.split(jax.random.key(seed), 11)
    latents_in = bell_draw(key_of[0], (SLOTS, SEQ, D), 1.0, 6.0, ((0, 32),))
    condition = bell_draw(key_of[1], (SLOTS, D), 1.0, 6.0, ((0, 32),))
    counts = draw_counts(jax.random.fold_in(key_of[10], 71), 0)
    ada_weight = bell_draw(key_of[3], (LAYERS, ADA_PAD), D ** -0.5, 0.3125, ((1, 32),))
    qkv_weight = bell_draw(key_of[4], (LAYERS, QKV_PAD), D ** -0.5, 0.3125, ((1, 32),))
    proj_weight = bell_draw(key_of[5], (LAYERS, PROJ_PAD), (D * 4 // SEQ) ** -0.5, 2.5, ((1, 32),))
    fc1_weight = bell_draw(key_of[6], (LAYERS, FC1_PAD), D ** -0.5, 0.3125, ((1, 32),))
    fc2_weight = bell_draw(key_of[7], (LAYERS, FC2_PAD), FF ** -0.5, 0.15625, ((1, 32),))
    biases = bell_draw(key_of[8], (LAYERS, BIAS_PAD), 0.5, 3.0, ((1, 32),))
    cotangent = bell_draw(key_of[9], (SLOTS, SEQ, D), 1.0, 6.0, ((0, 32),))
    return dict(latents_in=latents_in, condition=condition, counts=counts, ada_weight=ada_weight, qkv_weight=qkv_weight, proj_weight=proj_weight, fc1_weight=fc1_weight, fc2_weight=fc2_weight, biases=biases, cotangent=cotangent)


@jax.custom_vjp
def low(v):
    return lax.optimization_barrier(v.astype(jnp.bfloat16)).astype(jnp.float32)

@jax.custom_vjp
def low_back(v):
    return v

def low_keep(v):
    return (low(v), None)

def low_pass(kept, grad):
    return (grad,)

def back_keep(v):
    return (v, None)

def back_low(kept, grad):
    return (low(grad),)
low.defvjp(low_keep, low_pass)
low_back.defvjp(back_keep, back_low)
HIGHEST = lax.Precision.HIGHEST
EPSILON = 1e-06

def modulate_norm(values_in, shift_add, scale_mul):
    centred = values_in - lax.optimization_barrier(jnp.mean(values_in, axis=-1, keepdims=True))
    variance = lax.optimization_barrier(jnp.mean(centred * centred, axis=-1, keepdims=True))
    normed = centred * lax.rsqrt(variance + EPSILON)
    return normed * (1.0 + scale_mul[:, None, :]) + shift_add[:, None, :]

def matmul(left, right):
    return jnp.dot(left, right, precision=HIGHEST, preferred_element_type=jnp.float32)

def unpack(ada_row, qkv_row, proj_row, fc1_row, fc2_row, bias_row):
    w_ada = ada_row[:6 * D * D].reshape(D, 6 * D)
    w_qkv = qkv_row[:3 * D * D].reshape(D, 3 * D)
    w_proj = proj_row[:D * D].reshape(D, D)
    w_fc1 = fc1_row[:D * FF].reshape(D, FF)
    w_fc2 = fc2_row[:FF * D].reshape(FF, D)
    b_ada = bias_row[:6 * D]
    b_query = bias_row[6 * D:7 * D]
    b_value = bias_row[7 * D:8 * D]
    b_proj = bias_row[8 * D:9 * D]
    b_fc1 = bias_row[9 * D:9 * D + FF]
    b_fc2 = bias_row[9 * D + FF:10 * D + FF]
    return (w_ada, w_qkv, w_proj, w_fc1, w_fc2, b_ada, b_query, b_value, b_proj, b_fc1, b_fc2)

def block(hidden, cond_act, params):
    w_ada, w_qkv, w_proj, w_fc1, w_fc2, b_ada, b_query, b_value, b_proj, b_fc1, b_fc2 = params
    group_size = hidden.shape[0]
    seq_len = hidden.shape[1]
    modulation = low_back(matmul(cond_act, w_ada)) + b_ada
    shift_attn = modulation[:, 0:D]
    scale_attn = modulation[:, D:2 * D]
    gate_attn = modulation[:, 2 * D:3 * D]
    shift_ffn = modulation[:, 3 * D:4 * D]
    scale_ffn = modulation[:, 4 * D:5 * D]
    gate_ffn = modulation[:, 5 * D:6 * D]
    normed_attn = low(modulate_norm(hidden, shift_attn, scale_attn)).reshape(-1, D)
    mixed_qkv = low_back(matmul(normed_attn, w_qkv))
    queries = low(mixed_qkv[:, 0:D] + b_query).reshape(group_size, seq_len, HEADS, HEAD)
    key_heads = low(mixed_qkv[:, D:2 * D]).reshape(group_size, seq_len, HEADS, HEAD)
    value_heads = low(mixed_qkv[:, 2 * D:3 * D] + b_value).reshape(group_size, seq_len, HEADS, HEAD)
    scores = low_back(jnp.einsum('bqhd,bkhd->bhqk', queries, key_heads, precision=HIGHEST)) * (1.0 / math.sqrt(HEAD))
    attn_probs = jax.nn.softmax(scores, axis=-1)
    attended = jnp.einsum('bhqk,bkhd->bqhd', low(attn_probs), value_heads, precision=HIGHEST)
    attended = low(low_back(attended)).reshape(-1, D)
    projected = (low_back(matmul(attended, w_proj)) + b_proj).reshape(group_size, seq_len, D)
    middle = hidden + gate_attn[:, None, :] * projected
    normed_ffn = low(modulate_norm(middle, shift_ffn, scale_ffn)).reshape(-1, D)
    pre_act = low_back(matmul(normed_ffn, w_fc1)) + b_fc1
    activation = low(jax.nn.gelu(pre_act, approximate=True))
    branch = (low_back(matmul(activation, w_fc2)) + b_fc2).reshape(group_size, seq_len, D)
    return middle + gate_ffn[:, None, :] * branch

def reference(latents_in, condition, counts, ada_weight, qkv_weight, proj_weight, fc1_weight, fc2_weight, biases, cotangent):
    occupied = (jnp.tile(jnp.arange(CAP, dtype=jnp.int32), SHARDS) < jnp.repeat(counts, CAP)).astype(jnp.float32)

    def forward(hidden, cond, ada_all, qkv_all, proj_all, fc1_all, fc2_all, bias_all):
        cond_act = low(jax.nn.silu(cond))
        layer_params = [unpack(ada_all[layer_index], qkv_all[layer_index], proj_all[layer_index], fc1_all[layer_index], fc2_all[layer_index], bias_all[layer_index]) for layer_index in range(LAYERS)]
        group_size = math.gcd(hidden.shape[0], 16)

        def run_group(pair):
            group_hidden, group_cond = pair
            for params in layer_params:
                group_hidden = block(group_hidden, group_cond, params)
            return group_hidden
        grouped = lax.map(jax.checkpoint(run_group), (hidden.reshape(-1, group_size, SEQ, D), cond_act.reshape(-1, group_size, D)))
        return grouped.reshape(hidden.shape)
    inputs = (latents_in.astype(jnp.float32), condition.astype(jnp.float32), ada_weight.astype(jnp.float32), qkv_weight.astype(jnp.float32), proj_weight.astype(jnp.float32), fc1_weight.astype(jnp.float32), fc2_weight.astype(jnp.float32), biases.astype(jnp.float32))
    result, pullback = jax.vjp(forward, *inputs)
    grads = pullback(cotangent.astype(jnp.float32) * occupied[:, None, None])
    return (result * occupied[:, None, None], grads[0], grads[1], grads[2], grads[3], grads[4], grads[5], grads[6], grads[7])
```

```python
import functools
import math

import jax
import jax.numpy as jnp
from jax import lax
from jax.experimental import pallas as pl
from jax.experimental.pallas import tpu as pltpu
from jax.sharding import PartitionSpec as P

D = 384
HEADS = 6
HEAD = 64
FF = 1536


EPSILON = 1e-06


def modulate_norm(values_in, shift_add, scale_mul):
    centred = values_in - jnp.mean(values_in, axis=-1, keepdims=True)
    variance = jnp.mean(centred * centred, axis=-1, keepdims=True)
    normed = centred * lax.rsqrt(variance + EPSILON)
    return normed * (1.0 + scale_mul[:, None, :]) + shift_add[:, None, :]


def gelu_tanh(values_in):
    return jax.nn.gelu(values_in, approximate=True)


def left_product(left, right):
    return lax.dot_general(
        left, right, (((0,), (0,)), ((), ())), preferred_element_type=jnp.float32
    )


def right_product(left, right):
    return lax.dot_general(
        left, right, (((1,), (1,)), ((), ())), preferred_element_type=jnp.float32
    )


def unpack(gathered):
    ada_flat, qkv_flat, proj_flat, fc1_flat, fc2_flat, bias_flat = gathered
    bias_wide = bias_flat.astype(jnp.float32)
    return (
        ada_flat.reshape(D, 6 * D),
        qkv_flat[: 3 * D * D].reshape(D, 3 * D),
        proj_flat[: D * D].reshape(D, D),
        fc1_flat.reshape(D, FF),
        fc2_flat.reshape(FF, D),
        bias_wide[: 6 * D],
        bias_wide[6 * D : 7 * D],
        bias_wide[7 * D : 8 * D],
        bias_wide[8 * D : 9 * D],
        bias_wide[9 * D : 9 * D + FF],
        bias_wide[9 * D + FF : 10 * D + FF],
    )


def split_modulation(modulation):
    return [modulation[:, part_index * D : (part_index + 1) * D] for part_index in range(6)]


def layer_forward(hidden, cond_act, params):
    w_ada, w_qkv, w_proj, w_fc1, w_fc2, b_ada, b_query, b_value, b_proj, b_fc1, b_fc2 = params
    slot_count, seq_len = (hidden.shape[0], hidden.shape[1])
    modulation = jnp.dot(cond_act, w_ada, preferred_element_type=jnp.float32) + b_ada
    shift_attn, scale_attn, gate_attn, shift_ffn, scale_ffn, gate_ffn = split_modulation(modulation)
    normed_attn = modulate_norm(hidden, shift_attn, scale_attn).astype(jnp.bfloat16).reshape(-1, D)
    mixed_qkv = jnp.dot(normed_attn, w_qkv, preferred_element_type=jnp.float32)
    queries = (
        (mixed_qkv[:, 0:D] + b_query).astype(jnp.bfloat16).reshape(slot_count, seq_len, HEADS, HEAD)
    )
    key_heads = (
        mixed_qkv[:, D : 2 * D].astype(jnp.bfloat16).reshape(slot_count, seq_len, HEADS, HEAD)
    )
    value_heads = (
        (mixed_qkv[:, 2 * D : 3 * D] + b_value)
        .astype(jnp.bfloat16)
        .reshape(slot_count, seq_len, HEADS, HEAD)
    )
    scores = jnp.einsum(
        "bqhd,bkhd->bhqk", queries, key_heads, preferred_element_type=jnp.float32
    ) * (1.0 / math.sqrt(HEAD))
    peak_score = jnp.max(scores, axis=-1, keepdims=True)
    exp_scores = jnp.exp(scores - peak_score)
    exp_total = jnp.sum(exp_scores, axis=-1, keepdims=True)
    logsum = peak_score + jnp.log(exp_total)
    attn_probs = (exp_scores / exp_total).astype(jnp.bfloat16)
    attended = jnp.einsum(
        "bhqk,bkhd->bqhd", attn_probs, value_heads, preferred_element_type=jnp.float32
    )
    attended = attended.astype(jnp.bfloat16).reshape(-1, D)
    projected = (jnp.dot(attended, w_proj, preferred_element_type=jnp.float32) + b_proj).reshape(
        slot_count, seq_len, D
    )
    middle = hidden + gate_attn[:, None, :] * projected
    normed_ffn = modulate_norm(middle, shift_ffn, scale_ffn).astype(jnp.bfloat16).reshape(-1, D)
    pre_act = jnp.dot(normed_ffn, w_fc1, preferred_element_type=jnp.float32) + b_fc1
    activation = gelu_tanh(pre_act).astype(jnp.bfloat16)
    branch = (jnp.dot(activation, w_fc2, preferred_element_type=jnp.float32) + b_fc2).reshape(
        slot_count, seq_len, D
    )
    result = middle + gate_ffn[:, None, :] * branch
    record = (
        hidden,
        modulation,
        normed_attn,
        queries,
        key_heads,
        value_heads,
        logsum,
        attended,
        projected,
        middle,
        normed_ffn,
        pre_act,
        activation,
        branch,
    )
    return (result, record)


def layer_backward(upstream, params, record):
    w_ada, w_qkv, w_proj, w_fc1, w_fc2, b_ada, b_query, b_value, b_proj, b_fc1, b_fc2 = params
    (
        hidden,
        modulation,
        normed_attn,
        queries,
        key_heads,
        value_heads,
        logsum,
        attended,
        projected,
        middle,
        normed_ffn,
        pre_act,
        activation,
        branch,
    ) = record
    slot_count, seq_len = (hidden.shape[0], hidden.shape[1])
    shift_attn, scale_attn, gate_attn, shift_ffn, scale_ffn, gate_ffn = split_modulation(modulation)
    d_branch = (upstream * gate_ffn[:, None, :]).reshape(-1, D)
    d_gate_ffn = jnp.sum(upstream * branch, axis=1)
    grad_b_fc2 = jnp.sum(d_branch, axis=0)
    branch_low = d_branch.astype(jnp.bfloat16)
    grad_w_fc2 = left_product(activation, branch_low)
    d_act = right_product(branch_low, w_fc2)
    gelu_out, gelu_pull = jax.vjp(gelu_tanh, pre_act)
    (d_pre,) = gelu_pull(d_act)
    grad_b_fc1 = jnp.sum(d_pre, axis=0)
    pre_low = d_pre.astype(jnp.bfloat16)
    grad_w_fc1 = left_product(normed_ffn, pre_low)
    d_normed_ffn = right_product(pre_low, w_fc1).reshape(slot_count, seq_len, D)
    norm_out, norm_pull = jax.vjp(modulate_norm, middle, shift_ffn, scale_ffn)
    middle_part, d_shift_ffn, d_scale_ffn = norm_pull(d_normed_ffn)
    d_middle = upstream + middle_part
    d_proj = (d_middle * gate_attn[:, None, :]).reshape(-1, D)
    d_gate_attn = jnp.sum(d_middle * projected, axis=1)
    grad_b_proj = jnp.sum(d_proj, axis=0)
    proj_low = d_proj.astype(jnp.bfloat16)
    grad_w_proj = left_product(attended, proj_low)
    d_attended = (
        right_product(proj_low, w_proj)
        .astype(jnp.bfloat16)
        .reshape(slot_count, seq_len, HEADS, HEAD)
    )
    scores = jnp.einsum(
        "bqhd,bkhd->bhqk", queries, key_heads, preferred_element_type=jnp.float32
    ) * (1.0 / math.sqrt(HEAD))
    attn_probs = jnp.exp(scores - logsum)
    d_probs = jnp.einsum(
        "bqhd,bkhd->bhqk", d_attended, value_heads, preferred_element_type=jnp.float32
    )
    d_values = jnp.einsum(
        "bhqk,bqhd->bkhd",
        attn_probs.astype(jnp.bfloat16),
        d_attended,
        preferred_element_type=jnp.float32,
    )
    row_inner = jnp.sum(attn_probs * d_probs, axis=-1, keepdims=True)
    d_scores = (attn_probs * (d_probs - row_inner) * (1.0 / math.sqrt(HEAD))).astype(jnp.bfloat16)
    d_query = jnp.einsum(
        "bhqk,bkhd->bqhd", d_scores, key_heads, preferred_element_type=jnp.float32
    ).reshape(-1, D)
    d_keys = jnp.einsum(
        "bhqk,bqhd->bkhd", d_scores, queries, preferred_element_type=jnp.float32
    ).reshape(-1, D)
    d_values = d_values.reshape(-1, D)
    grad_b_query = jnp.sum(d_query, axis=0)
    grad_b_value = jnp.sum(d_values, axis=0)
    mixed_low = jnp.concatenate([d_query, d_keys, d_values], axis=1).astype(jnp.bfloat16)
    grad_w_qkv = left_product(normed_attn, mixed_low)
    d_normed_attn = right_product(mixed_low, w_qkv).reshape(slot_count, seq_len, D)
    attn_out, attn_pull = jax.vjp(modulate_norm, hidden, shift_attn, scale_attn)
    hidden_part, d_shift_attn, d_scale_attn = attn_pull(d_normed_attn)
    d_hidden = d_middle + hidden_part
    d_mod = jnp.concatenate(
        [d_shift_attn, d_scale_attn, d_gate_attn, d_shift_ffn, d_scale_ffn, d_gate_ffn], axis=1
    )
    grad_b_ada = jnp.sum(d_mod, axis=0)
    mod_low = d_mod.astype(jnp.bfloat16)
    d_cond = right_product(mod_low, w_ada)
    grad_bias = jnp.concatenate(
        [grad_b_ada, grad_b_query, grad_b_value, grad_b_proj, grad_b_fc1, grad_b_fc2]
    )
    return (d_hidden, d_cond, mod_low, (grad_w_qkv, grad_w_proj, grad_w_fc1, grad_w_fc2, grad_bias))


def pad_flat(values_in, length):
    flat = values_in.reshape(-1)
    return jnp.pad(flat, (0, length - flat.shape[0]))


def body(
    latents_in,
    condition,
    counts,
    ada_weight,
    qkv_weight,
    proj_weight,
    fc1_weight,
    fc2_weight,
    biases,
    cotangent,
):
    slot_count = latents_in.shape[0]
    layer_total = ada_weight.shape[0]
    device_count = lax.axis_size("fsdp")
    rest_list = (qkv_weight, proj_weight, fc1_weight, fc2_weight, biases)
    rest_lengths = [piece.shape[1] * device_count for piece in rest_list]
    ada_shard = ada_weight.shape[1]
    occupied = (jnp.arange(slot_count) < counts[0]).astype(jnp.float32)
    cond_wide = condition.astype(jnp.float32)
    silu_out, silu_pull = jax.vjp(jax.nn.silu, cond_wide)
    cond_act = silu_out.astype(jnp.bfloat16)
    hidden = latents_in.astype(jnp.float32)
    records = []
    for layer_index in range(layer_total):
        gathered = (
            lax.all_gather(ada_weight[layer_index], "fsdp", axis=0, tiled=True),
            lax.all_gather(qkv_weight[layer_index], "fsdp", axis=0, tiled=True),
            lax.all_gather(proj_weight[layer_index], "fsdp", axis=0, tiled=True),
            lax.all_gather(fc1_weight[layer_index], "fsdp", axis=0, tiled=True),
            lax.all_gather(fc2_weight[layer_index], "fsdp", axis=0, tiled=True),
            lax.all_gather(biases[layer_index], "fsdp", axis=0, tiled=True),
        )
        params = unpack(gathered)
        hidden, record = layer_forward(hidden, cond_act, params)
        records.append(record)
    latents_out = hidden * occupied[:, None, None]
    upstream = cotangent.astype(jnp.float32) * occupied[:, None, None]
    cond_total = jnp.zeros(cond_wide.shape, jnp.float32)
    layer_sums = [None] * layer_total
    mod_lows = [None] * layer_total
    for layer_index in reversed(range(layer_total)):
        gathered = (
            lax.all_gather(ada_weight[layer_index], "fsdp", axis=0, tiled=True),
            lax.all_gather(qkv_weight[layer_index], "fsdp", axis=0, tiled=True),
            lax.all_gather(proj_weight[layer_index], "fsdp", axis=0, tiled=True),
            lax.all_gather(fc1_weight[layer_index], "fsdp", axis=0, tiled=True),
            lax.all_gather(fc2_weight[layer_index], "fsdp", axis=0, tiled=True),
            lax.all_gather(biases[layer_index], "fsdp", axis=0, tiled=True),
        )
        params = unpack(gathered)
        upstream, d_cond, mod_low, grad_parts = layer_backward(
            upstream, params, records[layer_index]
        )
        mod_lows[layer_index] = mod_low
        cond_total = cond_total + d_cond
        padded = [
            pad_flat(grad_parts[part_index], rest_lengths[part_index]) for part_index in range(5)
        ]
        layer_sums[layer_index] = (
            lax.psum_scatter(padded[0], "fsdp", scatter_dimension=0, tiled=True),
            lax.psum_scatter(padded[1], "fsdp", scatter_dimension=0, tiled=True),
            lax.psum_scatter(padded[2], "fsdp", scatter_dimension=0, tiled=True),
            lax.psum_scatter(padded[3], "fsdp", scatter_dimension=0, tiled=True),
            lax.psum_scatter(padded[4], "fsdp", scatter_dimension=0, tiled=True),
        )
    grad_rest = [
        jnp.stack([layer_sums[layer_index][part_index] for layer_index in range(layer_total)])
        for part_index in range(5)
    ]
    mod_joined = jnp.concatenate(mod_lows, axis=1)
    ada_full = left_product(
        lax.all_gather(cond_act, "fsdp", axis=0, tiled=True),
        lax.all_gather(mod_joined, "fsdp", axis=0, tiled=True),
    )
    own_start = lax.axis_index("fsdp") * ada_shard
    ada_rows = []
    for layer_index in range(layer_total):
        flat_layer = pad_flat(
            ada_full[:, layer_index * 6 * D : (layer_index + 1) * 6 * D], ada_shard * device_count
        )
        ada_rows.append(lax.dynamic_slice_in_dim(flat_layer, own_start, ada_shard))
    ada_grad = jnp.stack(ada_rows)
    (condition_grad,) = silu_pull(cond_total)
    return (
        latents_out,
        upstream,
        condition_grad,
        ada_grad,
        grad_rest[0],
        grad_rest[1],
        grad_rest[2],
        grad_rest[3],
        grad_rest[4],
    )


BF16 = jnp.bfloat16
F32 = jnp.float32
SLOT = 4
SEQ = 256
HALF = 7 * D
WIRE = HALF + 2 * D + 128
BIAS = 10 * D + FF
VMEM = pl.BlockSpec(memory_space=pltpu.VMEM)
SMEM = pl.BlockSpec(memory_space=pltpu.SMEM)


def params_of(grid_rank=0):
    semantics = ("arbitrary",) * grid_rank if grid_rank else None
    return pltpu.CompilerParams(vmem_limit_bytes=50 * 2**20, dimension_semantics=semantics)


def dot_nn(left, right):
    return lax.dot_general(
        left, right, (((1,), (0,)), ((), ())), preferred_element_type=jnp.float32
    )


def pack_kernel(rows, ada, qkv, proj, fc1, fc2, bias, cond, out, wide):
    wide[:, :, WIRE - 128 :] = jnp.zeros((2, 2 * rows, 128), F32)

    def put(source, start, width, row, column):
        values = source[:, start : start + width].astype(F32)
        for layer in range(2):
            wide[layer, row : row + 1, column : column + width] = values[layer : layer + 1]

    for row in range(rows):
        put(ada, row * 6 * D, 6 * D, row, 0)
        put(qkv, row * 3 * D, D, row, 6 * D)
        put(qkv, row * 3 * D + D, 2 * D, rows + row, 0)
        put(proj, row * D, D, rows + row, 2 * D)
        put(fc1, row * FF, FF, rows + row, 3 * D)
    for row in range(4 * rows):
        put(fc2, row * D, D, row % (2 * rows), HALF + D * (row // (2 * rows)))
    put(bias, 0, 128, 0, WIRE - 128)
    put(bias, 128, 128, 1, WIRE - 128)
    wide_cond = cond[...].astype(F32)
    act = (wide_cond / (1.0 + jnp.exp(-wide_cond))).astype(BF16).astype(F32)
    for part in range(3):
        wide[0, 8 + 4 * part : 12 + 4 * part, WIRE - 128 :] = act[:, part * 128 : part * 128 + 128]
    out[...] = wide[...].astype(BF16)


def pack(ada, qkv, proj, fc1, fc2, bias, cond, rows):
    return pl.pallas_call(
        functools.partial(pack_kernel, rows),
        out_shape=jax.ShapeDtypeStruct((2, 2 * rows, WIRE), BF16),
        in_specs=[VMEM] * 7,
        out_specs=VMEM,
        scratch_shapes=[pltpu.VMEM((2, 2 * rows, WIRE), F32)],
        compiler_params=params_of(),
        name="pack",
    )(ada, qkv, proj, fc1, fc2, bias, cond)


def unpack_kernel(rows, devices, wire, left, right, down, bias, cond):
    for group in range(devices // 4):
        for half, target in ((0, left), (1, right)):
            target[4 * rows * group : 4 * rows * (group + 1), :] = jnp.concatenate(
                [
                    wire[4 * group + member, half * rows : (half + 1) * rows, :HALF]
                    for member in range(4)
                ],
                axis=0,
            )
    for device in range(devices):
        for part in range(2):
            start = 4 * rows * device + 2 * rows * part
            column = HALF + D * part
            down[start : start + 2 * rows, :] = wire[device, :, column : column + D]
        tail = wire[device, :, WIRE - 128 :].astype(F32)
        for part in range(2):
            chunk = 2 * device + part
            if chunk < BIAS // 128:
                bias[0:1, chunk * 128 : chunk * 128 + 128] = tail[part : part + 1]
        for part in range(3):
            cond[device % 2, 4 * (device // 2) : 4 * (device // 2) + 4, part * 128 : part * 128 + 128] = tail[
                8 + 4 * part : 12 + 4 * part
            ]


def unpack_wire(wire):
    devices, rows = wire.shape[0], wire.shape[1] // 2
    return pl.pallas_call(
        functools.partial(unpack_kernel, rows, devices),
        out_shape=(
            jax.ShapeDtypeStruct((D, HALF), BF16),
            jax.ShapeDtypeStruct((D, HALF), BF16),
            jax.ShapeDtypeStruct((FF, D), BF16),
            jax.ShapeDtypeStruct((1, BIAS), F32),
            jax.ShapeDtypeStruct((2, SLOT * devices // 2, D), F32),
        ),
        in_specs=[VMEM],
        out_specs=(VMEM,) * 5,
        compiler_params=params_of(),
        name="unpack",
    )(wire)


def norm_stats(values):
    centred = values - jnp.mean(values, axis=-1, keepdims=True)
    rstd = lax.rsqrt(jnp.mean(centred * centred, axis=-1, keepdims=True) + EPSILON)
    return centred * rstd, rstd


def mod_part(mod, slot, part):
    return mod[pl.ds(slot, 1), part * D : (part + 1) * D]


def gelu_parts(pre):
    inner = 0.7978845608028654 * (pre + 0.044715 * (pre * pre * pre))
    return jnp.tanh(inner)


def forward_kernel(counts, hidden, cond, left, right, down, bias, out, mod, qkv, attended, projected, middle, pre_act, branch, *, last):
    slot = pl.program_id(0)

    @pl.when(slot == 0)
    def _():
        wide_cond = cond[...].astype(F32)
        act = (wide_cond / (1.0 + jnp.exp(-wide_cond))).astype(BF16)
        mod[...] = dot_nn(act, left[:, : 6 * D]) + bias[:, : 6 * D]

    values = hidden[0].astype(F32)
    normed, _ = norm_stats(values)
    normed = (normed * (1.0 + mod_part(mod, slot, 1)) + mod_part(mod, slot, 0)).astype(BF16)
    queries = (dot_nn(normed, left[:, 6 * D :]) + bias[:, 6 * D : 7 * D]).astype(BF16)
    keys = dot_nn(normed, right[:, :D]).astype(BF16)
    heads_in = (dot_nn(normed, right[:, D : 2 * D]) + bias[:, 7 * D : 8 * D]).astype(BF16)
    qkv[0, :, :D] = queries
    qkv[0, :, D : 2 * D] = keys
    qkv[0, :, 2 * D :] = heads_in
    scaled = queries * jnp.asarray(1.0 / math.sqrt(HEAD), BF16)
    joined = []
    for head in range(HEADS):
        span = slice(head * HEAD, (head + 1) * HEAD)
        scores = right_product(scaled[:, span], keys[:, span])
        raised = jnp.exp(scores - jnp.max(scores, axis=-1, keepdims=True))
        probs = (raised * (1.0 / jnp.sum(raised, axis=-1, keepdims=True))).astype(BF16)
        joined.append(dot_nn(probs, heads_in[:, span]).astype(BF16))
    joined = jnp.concatenate(joined, axis=1)
    attended[0] = joined
    proj = dot_nn(joined, right[:, 2 * D : 3 * D]) + bias[:, 8 * D : 9 * D]
    projected[0] = proj
    mid = values + mod_part(mod, slot, 2) * proj
    middle[0] = mid
    normed, _ = norm_stats(mid)
    normed = (normed * (1.0 + mod_part(mod, slot, 4)) + mod_part(mod, slot, 3)).astype(BF16)
    pre = dot_nn(normed, right[:, 3 * D :]) + bias[:, 9 * D : 9 * D + FF]
    pre_act[0] = pre
    act = (0.5 * pre * (1.0 + gelu_parts(pre))).astype(BF16)
    ffn = dot_nn(act, down[...]) + bias[:, 9 * D + FF :]
    branch[0] = ffn
    result = mid + mod_part(mod, slot, 5) * ffn
    if last:
        result = result * jnp.where(slot < counts[0], 1.0, 0.0)
    out[0] = result


def per_slot(width):
    return pl.BlockSpec((1, SEQ, width), lambda slot: (slot, 0, 0))


def whole(*shape):
    return pl.BlockSpec(shape, lambda slot: (0,) * len(shape))


def tokens(width, dtype):
    return jax.ShapeDtypeStruct((SLOT, SEQ, width), dtype)


def cost(flops, moved):
    return pl.CostEstimate(flops=flops, bytes_accessed=moved, transcendentals=0)


def forward_block(counts, hidden, cond, weights, last):
    left, right, down, bias = weights
    return pl.pallas_call(
        functools.partial(forward_kernel, last=last),
        grid=(SLOT,),
        out_shape=(
            tokens(D, F32),
            jax.ShapeDtypeStruct((SLOT, 6 * D), F32),
            tokens(3 * D, BF16),
            tokens(D, BF16),
            tokens(D, F32),
            tokens(D, F32),
            tokens(FF, F32),
            tokens(D, F32),
        ),
        in_specs=[
            SMEM,
            per_slot(D),
            whole(SLOT, D),
            whole(D, HALF),
            whole(D, HALF),
            whole(FF, D),
            whole(1, BIAS),
        ],
        out_specs=(
            per_slot(D),
            whole(SLOT, 6 * D),
            per_slot(3 * D),
            per_slot(D),
            per_slot(D),
            per_slot(D),
            per_slot(FF),
            per_slot(D),
        ),
        compiler_params=params_of(1),
        cost_estimate=cost(5 * 10**9, 20 * 2**20),
        name="forward_block",
    )(counts, hidden, cond, left, right, down, bias)


def norm_backward(d_normed, normed, rstd, scale):
    inner = d_normed * (1.0 + scale)
    along = jnp.mean(inner * normed, axis=-1, keepdims=True)
    return rstd * (inner - jnp.mean(inner, axis=-1, keepdims=True) - normed * along)


def row_sum(values):
    return jnp.sum(values, axis=0, keepdims=True)


def ffn_kernel(chips, counts, upstream, branch, pre_act, middle, mod, right, down, d_middle, d_mod, bias, wire, acc_up, acc_down, *, last):
    slot = pl.program_id(0)

    @pl.when(slot == 0)
    def _():
        acc_up[...] = jnp.zeros_like(acc_up)
        acc_down[...] = jnp.zeros_like(acc_down)
        bias[...] = jnp.zeros_like(bias)
        d_mod[...] = jnp.zeros_like(d_mod)

    up = upstream[0].astype(F32)
    if last:
        up = up * jnp.where(slot < counts[0], 1.0, 0.0)
    d_branch = up * mod_part(mod, slot, 5)
    d_mod[pl.ds(20 + slot, 1), :] = row_sum(up * branch[0])
    bias[:, FF:] += row_sum(d_branch)
    low = d_branch.astype(BF16)
    pre = pre_act[0]
    curve = gelu_parts(pre)
    act = (0.5 * pre * (1.0 + curve)).astype(BF16)
    acc_down[...] += left_product(act, low)
    slope = 0.5 * (1.0 + curve) + (0.5 * 0.7978845608028654) * pre * (1.0 - curve * curve) * (
        1.0 + (3 * 0.044715) * (pre * pre)
    )
    d_pre = right_product(low, down[...]) * slope
    bias[:, :FF] += row_sum(d_pre)
    low = d_pre.astype(BF16)
    normed, rstd = norm_stats(middle[0])
    scale = mod_part(mod, slot, 4)
    shifted = (normed * (1.0 + scale) + mod_part(mod, slot, 3)).astype(BF16)
    acc_up[...] += left_product(shifted, low)
    d_normed = right_product(low, right[:, 3 * D :])
    d_mod[pl.ds(12 + slot, 1), :] = row_sum(d_normed)
    d_mod[pl.ds(16 + slot, 1), :] = row_sum(d_normed * normed)
    d_middle[0] = up + norm_backward(d_normed, normed, rstd, scale)

    @pl.when(slot == SLOT - 1)
    def _():
        rows = D // chips
        for chip in range(chips):
            for half in range(2):
                wire[half, chip, :, : 2 * D] = acc_up[rows * chip : rows * (chip + 1), 2 * D * half : 2 * D * (half + 1)].astype(BF16)
                for part in range(2):
                    start = rows * (4 * chip + 2 * half + part)
                    wire[half, chip, :, (2 + part) * D : (3 + part) * D] = acc_down[start : start + rows, :].astype(BF16)


def ffn_backward(counts, upstream, record, weights, chips, last):
    _, mod, _, _, _, middle, pre_act, branch = record
    _, right, down, _ = weights
    rows = D // chips
    return pl.pallas_call(
        functools.partial(ffn_kernel, chips, last=last),
        grid=(SLOT,),
        out_shape=(
            tokens(D, F32),
            jax.ShapeDtypeStruct((24, D), F32),
            jax.ShapeDtypeStruct((1, FF + D), F32),
            jax.ShapeDtypeStruct((2, chips, rows, 4 * D), BF16),
        ),
        in_specs=[
            SMEM,
            per_slot(D),
            per_slot(D),
            per_slot(FF),
            per_slot(D),
            whole(SLOT, 6 * D),
            whole(D, HALF),
            whole(FF, D),
        ],
        out_specs=(
            per_slot(D),
            whole(24, D),
            whole(1, FF + D),
            whole(2, chips, rows, 4 * D),
        ),
        scratch_shapes=[pltpu.VMEM((D, FF), F32), pltpu.VMEM((FF, D), F32)],
        compiler_params=params_of(1),
        cost_estimate=cost(8 * 10**9, 20 * 2**20),
        name="ffn_backward",
    )(counts, upstream, branch, pre_act, middle, mod, right, down)


def attention_kernel(chips, d_middle, hidden, qkv, attended, projected, mod, left, right, d_mod_in, bias_in, cond, d_cond_in, d_hidden, d_cond, wire, acc, acc_proj, d_mod, bias, *, first):
    slot = pl.program_id(0)

    @pl.when(slot == 0)
    def _():
        acc[...] = jnp.zeros_like(acc)
        acc_proj[...] = jnp.zeros_like(acc_proj)
        bias[...] = jnp.zeros_like(bias)
        d_mod[...] = d_mod_in[...]

    d_mid = d_middle[0]
    d_proj = d_mid * mod_part(mod, slot, 2)
    d_mod[pl.ds(8 + slot, 1), :] = row_sum(d_mid * projected[0])
    bias[:, 8 * D : 9 * D] += row_sum(d_proj)
    low = d_proj.astype(BF16)
    acc_proj[...] += left_product(attended[0], low)
    d_heads = right_product(low, right[:, 2 * D : 3 * D]).astype(BF16)
    factor = 1.0 / math.sqrt(HEAD)
    scaled = qkv[0, :, :D] * jnp.asarray(factor, BF16)
    keys = qkv[0, :, D : 2 * D]
    heads_in = qkv[0, :, 2 * D :]
    d_query, d_keys, d_values = [], [], []
    for head in range(HEADS):
        span = slice(head * HEAD, (head + 1) * HEAD)
        scores = right_product(keys[:, span], scaled[:, span])
        raised = jnp.exp(scores - jnp.max(scores, axis=0, keepdims=True))
        probs = raised * (1.0 / jnp.sum(raised, axis=0, keepdims=True))
        d_probs = right_product(heads_in[:, span], d_heads[:, span])
        d_values.append(dot_nn(probs.astype(BF16), d_heads[:, span]))
        weighted = probs * d_probs
        d_scores = (weighted - probs * jnp.sum(weighted, axis=0, keepdims=True)).astype(BF16)
        d_keys.append(dot_nn(d_scores, scaled[:, span]))
        d_query.append(left_product(d_scores, keys[:, span]) * factor)
    d_query = jnp.concatenate(d_query, axis=1)
    d_values = jnp.concatenate(d_values, axis=1)
    bias[:, 6 * D : 7 * D] += row_sum(d_query)
    bias[:, 7 * D : 8 * D] += row_sum(d_values)
    mixed = jnp.concatenate(
        [d_query.astype(BF16), jnp.concatenate(d_keys, axis=1).astype(BF16), d_values.astype(BF16)], axis=1
    )
    normed, rstd = norm_stats(hidden[0].astype(F32))
    scale = mod_part(mod, slot, 1)
    shifted = (normed * (1.0 + scale) + mod_part(mod, slot, 0)).astype(BF16)
    acc[...] += left_product(shifted, mixed)
    d_normed = right_product(mixed[:, :D], left[:, 6 * D :]) + right_product(mixed[:, D:], right[:, : 2 * D])
    d_mod[pl.ds(slot, 1), :] = row_sum(d_normed)
    d_mod[pl.ds(4 + slot, 1), :] = row_sum(d_normed * normed)
    d_hidden[0] = d_mid + norm_backward(d_normed, normed, rstd, scale)

    @pl.when(slot == SLOT - 1)
    def _():
        rows = D // chips
        bias[:, 9 * D :] = bias_in[...]
        total = d_cond_in[...]
        for part in range(6):
            grads = d_mod[SLOT * part : SLOT * (part + 1), :]
            bias[:, part * D : (part + 1) * D] = row_sum(grads)
            total = total + right_product(grads.astype(BF16), left[:, part * D : (part + 1) * D])
        if first:
            wide_cond = cond[...].astype(F32)
            gate = 1.0 / (1.0 + jnp.exp(-wide_cond))
            total = total * (gate * (1.0 + wide_cond * (1.0 - gate)))
        d_cond[...] = total
        low_mod = d_mod[...].astype(BF16)
        for chip in range(chips):
            span = slice(rows * chip, rows * (chip + 1))
            wire[0, chip, :, : 2 * D] = acc[span, : 2 * D].astype(BF16)
            wire[1, chip, :, :D] = acc[span, 2 * D :].astype(BF16)
            wire[1, chip, :, D : 2 * D] = acc_proj[span, :].astype(BF16)
            for half in range(2):
                pieces = []
                for part in range(2):
                    chunk = 4 * chip + 2 * half + part
                    if chunk < BIAS // 128:
                        pieces.append(bias[:, chunk * 128 : (chunk + 1) * 128])
                    else:
                        pieces.append(jnp.zeros((1, 128), F32))
                pieces.append(jnp.zeros((rows - 2, 128), F32))
                wire[half, chip, :, 2 * D : 2 * D + 128] = jnp.concatenate(pieces, axis=0).astype(BF16)
                wire[half, chip, :, 2 * D + 128 :] = low_mod


def attention_backward(d_middle, hidden, record, weights, d_mod, bias, cond, d_cond, chips, first):
    _, mod, qkv, attended, projected, _, _, _ = record
    left, right, _, _ = weights
    rows = D // chips
    return pl.pallas_call(
        functools.partial(attention_kernel, chips, first=first),
        grid=(SLOT,),
        out_shape=(
            tokens(D, F32),
            jax.ShapeDtypeStruct((SLOT, D), F32),
            jax.ShapeDtypeStruct((2, chips, rows, 3 * D + 128), BF16),
        ),
        in_specs=[
            per_slot(D),
            per_slot(D),
            per_slot(3 * D),
            per_slot(D),
            per_slot(D),
            whole(SLOT, 6 * D),
            whole(D, HALF),
            whole(D, HALF),
            whole(24, D),
            whole(1, FF + D),
            whole(SLOT, D),
            whole(SLOT, D),
        ],
        out_specs=(
            per_slot(D),
            whole(SLOT, D),
            whole(2, chips, rows, 3 * D + 128),
        ),
        scratch_shapes=[
            pltpu.VMEM((D, 3 * D), F32),
            pltpu.VMEM((D, D), F32),
            pltpu.VMEM((24, D), F32),
            pltpu.VMEM((1, BIAS), F32),
        ],
        compiler_params=params_of(1),
        cost_estimate=cost(6 * 10**9, 20 * 2**20),
        name="attention_backward",
    )(d_middle, hidden, qkv, attended, projected, mod, left, right, d_mod, bias, cond, d_cond)


def finish_kernel(chips, core, own_ffn, own_attn, got_ffn, got_attn, own_mod, got_mod, cond, chip, ada_out, qkv_out, proj_out, fc1_out, fc2_out, bias_out):
    rows = D // (2 * chips)
    is_odd = core[0] == 1
    mine = 2 * chip[0] + core[0]
    take = lax.broadcasted_iota(jnp.int32, (16, D), 0)
    column = lax.broadcasted_iota(jnp.int32, (16, D), 1)
    pick = ((column == rows * mine + take) & (take < rows)).astype(F32).astype(BF16)
    chosen = [right_product(pick, cond[side].astype(BF16)).astype(BF16) for side in range(2)]
    slots = SLOT * chips
    source = lax.broadcasted_iota(jnp.int32, (slots, 24 * chips), 0)
    target = lax.broadcasted_iota(jnp.int32, (slots, 24 * chips), 1)
    places = []
    for part in range(6):
        place = (target == 24 * (source // SLOT) + SLOT * part + source % SLOT).astype(F32).astype(BF16)
        places.append([dot_nn(chosen[side], place).astype(BF16) for side in range(2)])
    for layer in range(2):
        even = jnp.where(is_odd, got_mod[layer], own_mod[layer])
        odd = jnp.where(is_odd, own_mod[layer], got_mod[layer])
        for part in range(6):
            block = dot_nn(places[part][0], even) + dot_nn(places[part][1], odd)
            for row in range(rows):
                start = row * 6 * D + part * D
                ada_out[layer : layer + 1, start : start + D] = block[row : row + 1]
        own = jnp.where(is_odd, own_ffn[layer, rows:, :], own_ffn[layer, :rows, :])
        got = got_ffn[layer]
        first = jnp.where(is_odd, got, own[:, : 2 * D])
        second = jnp.where(is_odd, own[:, : 2 * D], got)
        for row in range(rows):
            fc1_out[layer : layer + 1, row * FF : row * FF + 2 * D] = first[row : row + 1]
            fc1_out[layer : layer + 1, row * FF + 2 * D : (row + 1) * FF] = second[row : row + 1]
        for row in range(4 * rows):
            column_start = (2 + row // (2 * rows)) * D
            fc2_out[layer : layer + 1, row * D : (row + 1) * D] = own_ffn[
                layer, row % (2 * rows) : row % (2 * rows) + 1, column_start : column_start + D
            ]
        own = jnp.where(is_odd, own_attn[layer, rows:, :], own_attn[layer, :rows, :])
        got = got_attn[layer]
        first = jnp.where(is_odd, got, own[:, : 2 * D])
        second = jnp.where(is_odd, own[:, : 2 * D], got)
        for row in range(rows):
            qkv_out[layer : layer + 1, row * 3 * D : row * 3 * D + 2 * D] = first[row : row + 1]
            qkv_out[layer : layer + 1, row * 3 * D + 2 * D : (row + 1) * 3 * D] = second[row : row + 1, :D]
            proj_out[layer : layer + 1, row * D : (row + 1) * D] = second[row : row + 1, D:]
        for part in range(2):
            bias_out[layer : layer + 1, part * 128 : (part + 1) * 128] = own_attn[
                layer, part : part + 1, 2 * D : 2 * D + 128
            ]


def finish(core, chip, own_ffn, own_attn, got_ffn, got_attn, own_mod, got_mod, cond, shapes, chips):
    return pl.pallas_call(
        functools.partial(finish_kernel, chips),
        out_shape=tuple(jax.ShapeDtypeStruct(shape, F32) for shape in shapes),
        in_specs=[SMEM] + [VMEM] * 7 + [SMEM],
        out_specs=(VMEM,) * 6,
        compiler_params=params_of(),
        name="finish",
    )(core, own_ffn, own_attn, got_ffn, got_attn, own_mod, got_mod, cond, chip)


def fast_body(
    latents_in, condition, counts, ada_weight, qkv_weight, proj_weight, fc1_weight, fc2_weight, biases, cotangent
):
    devices = lax.axis_size("fsdp")
    chips = devices // 2
    rows = D // devices
    index = lax.axis_index("fsdp")
    core, chip = (index % 2).reshape(1), (index // 2).reshape(1)
    pairs = [[2 * one, 2 * one + 1] for one in range(chips)]
    across = [[2 * one + side for one in range(chips)] for side in range(2)]
    swap = [(one, one ^ 1) for one in range(devices)]

    packed = pack(ada_weight, qkv_weight, proj_weight, fc1_weight, fc2_weight, biases, condition, rows)
    gathered = lax.all_gather(packed, "fsdp", axis=0, tiled=False)
    weights, conds = [], []
    for layer in range(2):
        *layer_weights, cond_all = unpack_wire(gathered[:, layer])
        weights.append(layer_weights)
        conds.append(cond_all)
    hidden = [latents_in]
    records = []
    for layer in range(2):
        record = forward_block(counts, hidden[-1], condition, weights[layer], layer == 1)
        records.append(record)
        hidden.append(record[0])
    upstream = cotangent
    d_cond = jnp.zeros((SLOT, D), F32)
    reduced = [None, None]

    def summed(wire, width):
        pair = lax.all_to_all(wire, "fsdp", 0, 0, axis_index_groups=pairs, tiled=True)
        both = (pair[0].astype(F32) + pair[1].astype(F32))[:, :, :width].astype(BF16)
        if width < wire.shape[-1]:
            both = jnp.concatenate([both, wire[0, :, :, width:]], axis=2)
        spread = lax.all_to_all(both, "fsdp", 0, 0, axis_index_groups=across, tiled=True)
        return jnp.sum(spread[:, :, :width].astype(F32), axis=0), spread[:, :, width:]

    for layer in (1, 0):
        d_middle, d_mod, bias, ffn_wire = ffn_backward(
            counts, upstream, records[layer], weights[layer], chips, layer == 1
        )
        ffn_sum, _ = summed(ffn_wire, 4 * D)
        upstream, d_cond, attn_wire = attention_backward(
            d_middle, hidden[layer], records[layer], weights[layer], d_mod, bias, condition, d_cond, chips, layer == 0
        )
        attn_sum, mods = summed(attn_wire, 2 * D + 128)
        reduced[layer] = (ffn_sum, attn_sum, mods.reshape(24 * chips, D))
    own_ffn = jnp.stack([reduced[layer][0] for layer in range(2)])
    own_attn = jnp.stack([reduced[layer][1] for layer in range(2)])
    own_mod = jnp.stack([reduced[layer][2] for layer in range(2)])
    start = (1 - index % 2) * rows
    to_send = jnp.concatenate([own_ffn[:, :, : 2 * D], own_attn[:, :, : 2 * D]], axis=2)
    got = lax.ppermute(lax.dynamic_slice_in_dim(to_send, start, rows, axis=1), "fsdp", swap)
    got_mod = lax.ppermute(own_mod, "fsdp", swap)
    shapes = [array.shape for array in (ada_weight, qkv_weight, proj_weight, fc1_weight, fc2_weight, biases)]
    grads = finish(
        core, chip, own_ffn, own_attn, got[:, :, : 2 * D], got[:, :, 2 * D :], own_mod, got_mod, conds[0], shapes, chips
    )
    return (hidden[2], upstream, d_cond, *grads)


def choose_body(
    latents_in, condition, counts, ada_weight, qkv_weight, proj_weight, fc1_weight, fc2_weight, biases, cotangent
):
    devices = lax.axis_size("fsdp")
    rows = D // devices
    fits = (
        D % devices == 0
        and devices == 32
        and latents_in.shape == (SLOT, SEQ, D)
        and ada_weight.shape == (2, rows * 6 * D)
        and qkv_weight.shape == (2, rows * 3 * D)
        and proj_weight.shape == (2, rows * D)
        and fc1_weight.shape == (2, rows * FF)
        and fc2_weight.shape == (2, rows * FF)
        and biases.shape == (2, 256)
    )
    chosen = fast_body if fits else body
    return chosen(
        latents_in, condition, counts, ada_weight, qkv_weight, proj_weight, fc1_weight, fc2_weight, biases, cotangent
    )


def solution(mesh):
    return jax.shard_map(
        choose_body,
        mesh=mesh,
        in_specs=(
            P("fsdp", None, None),
            P("fsdp", None),
            P("fsdp"),
            P(None, "fsdp"),
            P(None, "fsdp"),
            P(None, "fsdp"),
            P(None, "fsdp"),
            P(None, "fsdp"),
            P(None, "fsdp"),
            P("fsdp", None, None),
        ),
        out_specs=(
            P("fsdp", None, None),
            P("fsdp", None, None),
            P("fsdp", None),
            P(None, "fsdp"),
            P(None, "fsdp"),
            P(None, "fsdp"),
            P(None, "fsdp"),
            P(None, "fsdp"),
            P(None, "fsdp"),
        ),
        check_vma=False,
    )
```

```python
import functools
import math

import jax
import jax.numpy as jnp
from jax import lax
from jax.experimental import pallas as pl
from jax.experimental.pallas import tpu as pltpu
from jax.sharding import PartitionSpec as P

D = 384
HEADS = 6
HEAD = 64
FF = 1536


EPSILON = 1e-06


def modulate_norm(values_in, shift_add, scale_mul):
    centred = values_in - jnp.mean(values_in, axis=-1, keepdims=True)
    variance = jnp.mean(centred * centred, axis=-1, keepdims=True)
    normed = centred * lax.rsqrt(variance + EPSILON)
    return normed * (1.0 + scale_mul[:, None, :]) + shift_add[:, None, :]


def gelu_tanh(values_in):
    return jax.nn.gelu(values_in, approximate=True)


def left_product(left, right):
    return lax.dot_general(
        left, right, (((0,), (0,)), ((), ())), preferred_element_type=jnp.float32
    )


def right_product(left, right):
    return lax.dot_general(
        left, right, (((1,), (1,)), ((), ())), preferred_element_type=jnp.float32
    )


def unpack(gathered):
    ada_flat, qkv_flat, proj_flat, fc1_flat, fc2_flat, bias_flat = gathered
    bias_wide = bias_flat.astype(jnp.float32)
    return (
        ada_flat.reshape(D, 6 * D),
        qkv_flat[: 3 * D * D].reshape(D, 3 * D),
        proj_flat[: D * D].reshape(D, D),
        fc1_flat.reshape(D, FF),
        fc2_flat.reshape(FF, D),
        bias_wide[: 6 * D],
        bias_wide[6 * D : 7 * D],
        bias_wide[7 * D : 8 * D],
        bias_wide[8 * D : 9 * D],
        bias_wide[9 * D : 9 * D + FF],
        bias_wide[9 * D + FF : 10 * D + FF],
    )


def split_modulation(modulation):
    return [modulation[:, part_index * D : (part_index + 1) * D] for part_index in range(6)]


def layer_forward(hidden, cond_act, params):
    w_ada, w_qkv, w_proj, w_fc1, w_fc2, b_ada, b_query, b_value, b_proj, b_fc1, b_fc2 = params
    slot_count, seq_len = (hidden.shape[0], hidden.shape[1])
    modulation = jnp.dot(cond_act, w_ada, preferred_element_type=jnp.float32) + b_ada
    shift_attn, scale_attn, gate_attn, shift_ffn, scale_ffn, gate_ffn = split_modulation(modulation)
    normed_attn = modulate_norm(hidden, shift_attn, scale_attn).astype(jnp.bfloat16).reshape(-1, D)
    mixed_qkv = jnp.dot(normed_attn, w_qkv, preferred_element_type=jnp.float32)
    queries = (
        (mixed_qkv[:, 0:D] + b_query).astype(jnp.bfloat16).reshape(slot_count, seq_len, HEADS, HEAD)
    )
    key_heads = (
        mixed_qkv[:, D : 2 * D].astype(jnp.bfloat16).reshape(slot_count, seq_len, HEADS, HEAD)
    )
    value_heads = (
        (mixed_qkv[:, 2 * D : 3 * D] + b_value)
        .astype(jnp.bfloat16)
        .reshape(slot_count, seq_len, HEADS, HEAD)
    )
    scores = jnp.einsum(
        "bqhd,bkhd->bhqk", queries, key_heads, preferred_element_type=jnp.float32
    ) * (1.0 / math.sqrt(HEAD))
    peak_score = jnp.max(scores, axis=-1, keepdims=True)
    exp_scores = jnp.exp(scores - peak_score)
    exp_total = jnp.sum(exp_scores, axis=-1, keepdims=True)
    logsum = peak_score + jnp.log(exp_total)
    attn_probs = (exp_scores / exp_total).astype(jnp.bfloat16)
    attended = jnp.einsum(
        "bhqk,bkhd->bqhd", attn_probs, value_heads, preferred_element_type=jnp.float32
    )
    attended = attended.astype(jnp.bfloat16).reshape(-1, D)
    projected = (jnp.dot(attended, w_proj, preferred_element_type=jnp.float32) + b_proj).reshape(
        slot_count, seq_len, D
    )
    middle = hidden + gate_attn[:, None, :] * projected
    normed_ffn = modulate_norm(middle, shift_ffn, scale_ffn).astype(jnp.bfloat16).reshape(-1, D)
    pre_act = jnp.dot(normed_ffn, w_fc1, preferred_element_type=jnp.float32) + b_fc1
    activation = gelu_tanh(pre_act).astype(jnp.bfloat16)
    branch = (jnp.dot(activation, w_fc2, preferred_element_type=jnp.float32) + b_fc2).reshape(
        slot_count, seq_len, D
    )
    result = middle + gate_ffn[:, None, :] * branch
    record = (
        hidden,
        modulation,
        normed_attn,
        queries,
        key_heads,
        value_heads,
        logsum,
        attended,
        projected,
        middle,
        normed_ffn,
        pre_act,
        activation,
        branch,
    )
    return (result, record)


def layer_backward(upstream, params, record):
    w_ada, w_qkv, w_proj, w_fc1, w_fc2, b_ada, b_query, b_value, b_proj, b_fc1, b_fc2 = params
    (
        hidden,
        modulation,
        normed_attn,
        queries,
        key_heads,
        value_heads,
        logsum,
        attended,
        projected,
        middle,
        normed_ffn,
        pre_act,
        activation,
        branch,
    ) = record
    slot_count, seq_len = (hidden.shape[0], hidden.shape[1])
    shift_attn, scale_attn, gate_attn, shift_ffn, scale_ffn, gate_ffn = split_modulation(modulation)
    d_branch = (upstream * gate_ffn[:, None, :]).reshape(-1, D)
    d_gate_ffn = jnp.sum(upstream * branch, axis=1)
    grad_b_fc2 = jnp.sum(d_branch, axis=0)
    branch_low = d_branch.astype(jnp.bfloat16)
    grad_w_fc2 = left_product(activation, branch_low)
    d_act = right_product(branch_low, w_fc2)
    gelu_out, gelu_pull = jax.vjp(gelu_tanh, pre_act)
    (d_pre,) = gelu_pull(d_act)
    grad_b_fc1 = jnp.sum(d_pre, axis=0)
    pre_low = d_pre.astype(jnp.bfloat16)
    grad_w_fc1 = left_product(normed_ffn, pre_low)
    d_normed_ffn = right_product(pre_low, w_fc1).reshape(slot_count, seq_len, D)
    norm_out, norm_pull = jax.vjp(modulate_norm, middle, shift_ffn, scale_ffn)
    middle_part, d_shift_ffn, d_scale_ffn = norm_pull(d_normed_ffn)
    d_middle = upstream + middle_part
    d_proj = (d_middle * gate_attn[:, None, :]).reshape(-1, D)
    d_gate_attn = jnp.sum(d_middle * projected, axis=1)
    grad_b_proj = jnp.sum(d_proj, axis=0)
    proj_low = d_proj.astype(jnp.bfloat16)
    grad_w_proj = left_product(attended, proj_low)
    d_attended = (
        right_product(proj_low, w_proj)
        .astype(jnp.bfloat16)
        .reshape(slot_count, seq_len, HEADS, HEAD)
    )
    scores = jnp.einsum(
        "bqhd,bkhd->bhqk", queries, key_heads, preferred_element_type=jnp.float32
    ) * (1.0 / math.sqrt(HEAD))
    attn_probs = jnp.exp(scores - logsum)
    d_probs = jnp.einsum(
        "bqhd,bkhd->bhqk", d_attended, value_heads, preferred_element_type=jnp.float32
    )
    d_values = jnp.einsum(
        "bhqk,bqhd->bkhd",
        attn_probs.astype(jnp.bfloat16),
        d_attended,
        preferred_element_type=jnp.float32,
    )
    row_inner = jnp.sum(attn_probs * d_probs, axis=-1, keepdims=True)
    d_scores = (attn_probs * (d_probs - row_inner) * (1.0 / math.sqrt(HEAD))).astype(jnp.bfloat16)
    d_query = jnp.einsum(
        "bhqk,bkhd->bqhd", d_scores, key_heads, preferred_element_type=jnp.float32
    ).reshape(-1, D)
    d_keys = jnp.einsum(
        "bhqk,bqhd->bkhd", d_scores, queries, preferred_element_type=jnp.float32
    ).reshape(-1, D)
    d_values = d_values.reshape(-1, D)
    grad_b_query = jnp.sum(d_query, axis=0)
    grad_b_value = jnp.sum(d_values, axis=0)
    mixed_low = jnp.concatenate([d_query, d_keys, d_values], axis=1).astype(jnp.bfloat16)
    grad_w_qkv = left_product(normed_attn, mixed_low)
    d_normed_attn = right_product(mixed_low, w_qkv).reshape(slot_count, seq_len, D)
    attn_out, attn_pull = jax.vjp(modulate_norm, hidden, shift_attn, scale_attn)
    hidden_part, d_shift_attn, d_scale_attn = attn_pull(d_normed_attn)
    d_hidden = d_middle + hidden_part
    d_mod = jnp.concatenate(
        [d_shift_attn, d_scale_attn, d_gate_attn, d_shift_ffn, d_scale_ffn, d_gate_ffn], axis=1
    )
    grad_b_ada = jnp.sum(d_mod, axis=0)
    mod_low = d_mod.astype(jnp.bfloat16)
    d_cond = right_product(mod_low, w_ada)
    grad_bias = jnp.concatenate(
        [grad_b_ada, grad_b_query, grad_b_value, grad_b_proj, grad_b_fc1, grad_b_fc2]
    )
    return (d_hidden, d_cond, mod_low, (grad_w_qkv, grad_w_proj, grad_w_fc1, grad_w_fc2, grad_bias))


def pad_flat(values_in, length):
    flat = values_in.reshape(-1)
    return jnp.pad(flat, (0, length - flat.shape[0]))


def body(
    latents_in,
    condition,
    counts,
    ada_weight,
    qkv_weight,
    proj_weight,
    fc1_weight,
    fc2_weight,
    biases,
    cotangent,
):
    slot_count = latents_in.shape[0]
    layer_total = ada_weight.shape[0]
    device_count = lax.axis_size("fsdp")
    rest_list = (qkv_weight, proj_weight, fc1_weight, fc2_weight, biases)
    rest_lengths = [piece.shape[1] * device_count for piece in rest_list]
    ada_shard = ada_weight.shape[1]
    occupied = (jnp.arange(slot_count) < counts[0]).astype(jnp.float32)
    cond_wide = condition.astype(jnp.float32)
    silu_out, silu_pull = jax.vjp(jax.nn.silu, cond_wide)
    cond_act = silu_out.astype(jnp.bfloat16)
    hidden = latents_in.astype(jnp.float32)
    records = []
    for layer_index in range(layer_total):
        gathered = (
            lax.all_gather(ada_weight[layer_index], "fsdp", axis=0, tiled=True),
            lax.all_gather(qkv_weight[layer_index], "fsdp", axis=0, tiled=True),
            lax.all_gather(proj_weight[layer_index], "fsdp", axis=0, tiled=True),
            lax.all_gather(fc1_weight[layer_index], "fsdp", axis=0, tiled=True),
            lax.all_gather(fc2_weight[layer_index], "fsdp", axis=0, tiled=True),
            lax.all_gather(biases[layer_index], "fsdp", axis=0, tiled=True),
        )
        params = unpack(gathered)
        hidden, record = layer_forward(hidden, cond_act, params)
        records.append(record)
    latents_out = hidden * occupied[:, None, None]
    upstream = cotangent.astype(jnp.float32) * occupied[:, None, None]
    cond_total = jnp.zeros(cond_wide.shape, jnp.float32)
    layer_sums = [None] * layer_total
    mod_lows = [None] * layer_total
    for layer_index in reversed(range(layer_total)):
        gathered = (
            lax.all_gather(ada_weight[layer_index], "fsdp", axis=0, tiled=True),
            lax.all_gather(qkv_weight[layer_index], "fsdp", axis=0, tiled=True),
            lax.all_gather(proj_weight[layer_index], "fsdp", axis=0, tiled=True),
            lax.all_gather(fc1_weight[layer_index], "fsdp", axis=0, tiled=True),
            lax.all_gather(fc2_weight[layer_index], "fsdp", axis=0, tiled=True),
            lax.all_gather(biases[layer_index], "fsdp", axis=0, tiled=True),
        )
        params = unpack(gathered)
        upstream, d_cond, mod_low, grad_parts = layer_backward(
            upstream, params, records[layer_index]
        )
        mod_lows[layer_index] = mod_low
        cond_total = cond_total + d_cond
        padded = [
            pad_flat(grad_parts[part_index], rest_lengths[part_index]) for part_index in range(5)
        ]
        layer_sums[layer_index] = (
            lax.psum_scatter(padded[0], "fsdp", scatter_dimension=0, tiled=True),
            lax.psum_scatter(padded[1], "fsdp", scatter_dimension=0, tiled=True),
            lax.psum_scatter(padded[2], "fsdp", scatter_dimension=0, tiled=True),
            lax.psum_scatter(padded[3], "fsdp", scatter_dimension=0, tiled=True),
            lax.psum_scatter(padded[4], "fsdp", scatter_dimension=0, tiled=True),
        )
    grad_rest = [
        jnp.stack([layer_sums[layer_index][part_index] for layer_index in range(layer_total)])
        for part_index in range(5)
    ]
    mod_joined = jnp.concatenate(mod_lows, axis=1)
    ada_full = left_product(
        lax.all_gather(cond_act, "fsdp", axis=0, tiled=True),
        lax.all_gather(mod_joined, "fsdp", axis=0, tiled=True),
    )
    own_start = lax.axis_index("fsdp") * ada_shard
    ada_rows = []
    for layer_index in range(layer_total):
        flat_layer = pad_flat(
            ada_full[:, layer_index * 6 * D : (layer_index + 1) * 6 * D], ada_shard * device_count
        )
        ada_rows.append(lax.dynamic_slice_in_dim(flat_layer, own_start, ada_shard))
    ada_grad = jnp.stack(ada_rows)
    (condition_grad,) = silu_pull(cond_total)
    return (
        latents_out,
        upstream,
        condition_grad,
        ada_grad,
        grad_rest[0],
        grad_rest[1],
        grad_rest[2],
        grad_rest[3],
        grad_rest[4],
    )


BF16 = jnp.bfloat16
F32 = jnp.float32
SLOT = 4
SEQ = 256
HALF = 7 * D
WIRE = HALF + 2 * D + 128
BIAS = 10 * D + FF
VMEM = pl.BlockSpec(memory_space=pltpu.VMEM)
SMEM = pl.BlockSpec(memory_space=pltpu.SMEM)


def params_of(grid_rank=0):
    semantics = ("arbitrary",) * grid_rank if grid_rank else None
    return pltpu.CompilerParams(vmem_limit_bytes=50 * 2**20, dimension_semantics=semantics)


def dot_nn(left, right):
    return lax.dot_general(
        left, right, (((1,), (0,)), ((), ())), preferred_element_type=jnp.float32
    )


def pack_kernel(rows, ada_in, qkv_in, proj_in, fc1_in, fc2_in, bias_in, cond, out_first, out_last, ada, qkv, proj, fc1, fc2, bias, sems, wide):
    copies = [
        pltpu.make_async_copy(source, target, sems.at[place])
        for place, (source, target) in enumerate(
            ((ada_in, ada), (qkv_in, qkv), (proj_in, proj), (fc1_in, fc1), (fc2_in, fc2), (bias_in, bias))
        )
    ]
    for copy in copies:
        copy.start()
    wide[:, :, WIRE - 128 :] = jnp.zeros((2, 2 * rows, 128), F32)
    wide_cond = cond[...].astype(F32)
    act = (wide_cond / (1.0 + jnp.exp(-wide_cond))).astype(BF16).astype(F32)
    for part in range(3):
        wide[0, 8 + 4 * part : 12 + 4 * part, WIRE - 128 :] = act[:, part * 128 : part * 128 + 128]
    for copy in copies:
        copy.wait()

    def put(source, start, width, row, column):
        values = source[:, start : start + width].astype(F32)
        for layer in range(2):
            wide[layer, row : row + 1, column : column + width] = values[layer : layer + 1]

    for row in range(rows):
        put(ada, row * 6 * D, 6 * D, row, 0)
        put(qkv, row * 3 * D, D, row, 6 * D)
        put(qkv, row * 3 * D + D, 2 * D, rows + row, 0)
        put(proj, row * D, D, rows + row, 2 * D)
        put(fc1, row * FF, FF, rows + row, 3 * D)
    for row in range(4 * rows):
        put(fc2, row * D, D, row % (2 * rows), HALF + D * (row // (2 * rows)))
    put(bias, 0, 128, 0, WIRE - 128)
    put(bias, 128, 128, 1, WIRE - 128)
    for layer, out in enumerate((out_first, out_last)):
        low = wide[layer].astype(BF16)
        for copy_index in range(out.shape[0]):
            out[copy_index] = low


def pack(ada, qkv, proj, fc1, fc2, bias, cond, rows, copies):
    flat = (ada, qkv, proj, fc1, fc2, bias)
    return pl.pallas_call(
        functools.partial(pack_kernel, rows),
        out_shape=(jax.ShapeDtypeStruct((copies, 2 * rows, WIRE), BF16),) * 2,
        in_specs=[pl.BlockSpec(memory_space=pl.ANY)] * 6 + [VMEM],
        out_specs=(VMEM, VMEM),
        scratch_shapes=[pltpu.VMEM(array.shape, BF16) for array in flat]
        + [pltpu.SemaphoreType.DMA((6,)), pltpu.VMEM((2, 2 * rows, WIRE), F32)],
        compiler_params=params_of(),
        name="pack",
    )(*flat, cond)


def unpack_kernel(rows, place, *refs):
    blocks, (left, right, down, bias, cond, wire, sems) = refs[:16], refs[16:]
    copies = []
    for side in range(2):
        for step in range(4):
            for half in range(2):
                number = 8 * side + 2 * step + half
                target = wire.at[(place[0] + side) % 2, place[1] ^ step, pl.ds(2 * half, 2)]
                copies.append(pltpu.make_async_copy(blocks[number], target, sems.at[number]))
    for copy in copies:
        copy.start()
    for copy in copies:
        copy.wait()

    def of(device):
        return wire.at[device % 2, (device // 2) % 4, device // 8]

    for group in range(8):
        for half, target in ((0, left), (1, right)):
            target[4 * rows * group : 4 * rows * (group + 1), :] = jnp.concatenate(
                [of(4 * group + member)[half * rows : (half + 1) * rows, :HALF] for member in range(4)], axis=0
            )
    for device in range(32):
        for part in range(2):
            start = 4 * rows * device + 2 * rows * part
            column = HALF + D * part
            down[start : start + 2 * rows, :] = of(device)[:, column : column + D]
        tail = of(device)[:, WIRE - 128 :].astype(F32)
        for part in range(2):
            chunk = 2 * device + part
            if chunk < BIAS // 128:
                bias[0:1, chunk * 128 : chunk * 128 + 128] = tail[part : part + 1]
        for part in range(3):
            cond[device % 2, 4 * (device // 2) : 4 * (device // 2) + 4, part * 128 : part * 128 + 128] = tail[
                8 + 4 * part : 12 + 4 * part
            ]


def unpack_wire(place, blocks):
    rows = blocks[0].shape[1] // 2
    return pl.pallas_call(
        functools.partial(unpack_kernel, rows),
        out_shape=(
            jax.ShapeDtypeStruct((D, HALF), BF16),
            jax.ShapeDtypeStruct((D, HALF), BF16),
            jax.ShapeDtypeStruct((FF, D), BF16),
            jax.ShapeDtypeStruct((1, BIAS), F32),
            jax.ShapeDtypeStruct((2, SLOT * 16, D), F32),
        ),
        in_specs=[SMEM] + [pl.BlockSpec(memory_space=pl.ANY)] * 16,
        out_specs=(VMEM,) * 5,
        scratch_shapes=[pltpu.VMEM((2, 4, 4, 2 * rows, WIRE), BF16), pltpu.SemaphoreType.DMA((16,))],
        compiler_params=params_of(),
        name="unpack",
    )(place, *blocks)


def norm_stats(values):
    centred = values - jnp.mean(values, axis=-1, keepdims=True)
    rstd = lax.rsqrt(jnp.mean(centred * centred, axis=-1, keepdims=True) + EPSILON)
    return centred * rstd, rstd


def mod_part(mod, slot, part):
    return mod[pl.ds(slot, 1), part * D : (part + 1) * D]


def gelu_parts(pre):
    inner = 0.7978845608028654 * (pre + 0.044715 * (pre * pre * pre))
    return jnp.tanh(inner)


def forward_kernel(counts, hidden, cond, left, right, down, bias, out, mod, qkv, attended, projected, middle, pre_act, branch, *, last):
    slot = pl.program_id(0)

    @pl.when(slot == 0)
    def _():
        wide_cond = cond[...].astype(F32)
        act = (wide_cond / (1.0 + jnp.exp(-wide_cond))).astype(BF16)
        mod[...] = dot_nn(act, left[:, : 6 * D]) + bias[:, : 6 * D]

    values = hidden[0].astype(F32)
    normed, _ = norm_stats(values)
    normed = (normed * (1.0 + mod_part(mod, slot, 1)) + mod_part(mod, slot, 0)).astype(BF16)
    queries = (dot_nn(normed, left[:, 6 * D :]) + bias[:, 6 * D : 7 * D]).astype(BF16)
    keys = dot_nn(normed, right[:, :D]).astype(BF16)
    heads_in = (dot_nn(normed, right[:, D : 2 * D]) + bias[:, 7 * D : 8 * D]).astype(BF16)
    qkv[0, :, :D] = queries
    qkv[0, :, D : 2 * D] = keys
    qkv[0, :, 2 * D :] = heads_in
    scaled = queries * jnp.asarray(1.0 / math.sqrt(HEAD), BF16)
    joined = []
    for head in range(HEADS):
        span = slice(head * HEAD, (head + 1) * HEAD)
        scores = right_product(scaled[:, span], keys[:, span])
        raised = jnp.exp(scores - jnp.max(scores, axis=-1, keepdims=True))
        probs = (raised * (1.0 / jnp.sum(raised, axis=-1, keepdims=True))).astype(BF16)
        joined.append(dot_nn(probs, heads_in[:, span]).astype(BF16))
    joined = jnp.concatenate(joined, axis=1)
    attended[0] = joined
    proj = dot_nn(joined, right[:, 2 * D : 3 * D]) + bias[:, 8 * D : 9 * D]
    projected[0] = proj
    mid = values + mod_part(mod, slot, 2) * proj
    middle[0] = mid
    normed, _ = norm_stats(mid)
    normed = (normed * (1.0 + mod_part(mod, slot, 4)) + mod_part(mod, slot, 3)).astype(BF16)
    pre = dot_nn(normed, right[:, 3 * D :]) + bias[:, 9 * D : 9 * D + FF]
    pre_act[0] = pre
    act = (0.5 * pre * (1.0 + gelu_parts(pre))).astype(BF16)
    ffn = dot_nn(act, down[...]) + bias[:, 9 * D + FF :]
    branch[0] = ffn
    result = mid + mod_part(mod, slot, 5) * ffn
    if last:
        result = result * jnp.where(slot < counts[0], 1.0, 0.0)
    out[0] = result


def per_slot(width):
    return pl.BlockSpec((1, SEQ, width), lambda slot: (slot, 0, 0))


def whole(*shape):
    return pl.BlockSpec(shape, lambda slot: (0,) * len(shape))


def tokens(width, dtype):
    return jax.ShapeDtypeStruct((SLOT, SEQ, width), dtype)


def cost(flops, moved):
    return pl.CostEstimate(flops=flops, bytes_accessed=moved, transcendentals=0)


def forward_block(counts, hidden, cond, weights, last):
    left, right, down, bias = weights
    return pl.pallas_call(
        functools.partial(forward_kernel, last=last),
        grid=(SLOT,),
        out_shape=(
            tokens(D, F32),
            jax.ShapeDtypeStruct((SLOT, 6 * D), F32),
            tokens(3 * D, BF16),
            tokens(D, BF16),
            tokens(D, F32),
            tokens(D, F32),
            tokens(FF, F32),
            tokens(D, F32),
        ),
        in_specs=[
            SMEM,
            per_slot(D),
            whole(SLOT, D),
            whole(D, HALF),
            whole(D, HALF),
            whole(FF, D),
            whole(1, BIAS),
        ],
        out_specs=(
            per_slot(D),
            whole(SLOT, 6 * D),
            per_slot(3 * D),
            per_slot(D),
            per_slot(D),
            per_slot(D),
            per_slot(FF),
            per_slot(D),
        ),
        compiler_params=params_of(1),
        cost_estimate=cost(5 * 10**9, 20 * 2**20),
        name="forward_block",
    )(counts, hidden, cond, left, right, down, bias)


def norm_backward(d_normed, normed, rstd, scale):
    inner = d_normed * (1.0 + scale)
    along = jnp.mean(inner * normed, axis=-1, keepdims=True)
    return rstd * (inner - jnp.mean(inner, axis=-1, keepdims=True) - normed * along)


def row_sum(values):
    return jnp.sum(values, axis=0, keepdims=True)


def ffn_kernel(chips, core, counts, upstream, branch, pre_act, middle, mod, right, down, d_middle, d_mod, bias, wire, acc_up, acc_down, *, last):
    slot = pl.program_id(0)

    @pl.when(slot == 0)
    def _():
        acc_up[...] = jnp.zeros_like(acc_up)
        acc_down[...] = jnp.zeros_like(acc_down)
        bias[...] = jnp.zeros_like(bias)
        d_mod[...] = jnp.zeros_like(d_mod)

    up = upstream[0].astype(F32)
    if last:
        up = up * jnp.where(slot < counts[0], 1.0, 0.0)
    d_branch = up * mod_part(mod, slot, 5)
    d_mod[pl.ds(20 + slot, 1), :] = row_sum(up * branch[0])
    bias[:, FF:] += row_sum(d_branch)
    low = d_branch.astype(BF16)
    pre = pre_act[0]
    curve = gelu_parts(pre)
    act = (0.5 * pre * (1.0 + curve)).astype(BF16)
    acc_down[...] += left_product(act, low)
    slope = 0.5 * (1.0 + curve) + (0.5 * 0.7978845608028654) * pre * (1.0 - curve * curve) * (
        1.0 + (3 * 0.044715) * (pre * pre)
    )
    d_pre = right_product(low, down[...]) * slope
    bias[:, :FF] += row_sum(d_pre)
    low = d_pre.astype(BF16)
    normed, rstd = norm_stats(middle[0])
    scale = mod_part(mod, slot, 4)
    shifted = (normed * (1.0 + scale) + mod_part(mod, slot, 3)).astype(BF16)
    acc_up[...] += left_product(shifted, low)
    d_normed = right_product(low, right[:, 3 * D :])
    d_mod[pl.ds(12 + slot, 1), :] = row_sum(d_normed)
    d_mod[pl.ds(16 + slot, 1), :] = row_sum(d_normed * normed)
    d_middle[0] = up + norm_backward(d_normed, normed, rstd, scale)

    @pl.when(slot == SLOT - 1)
    def _():
        rows = D // chips
        for chip in range(chips):
            for half in range(2):
                side = (half + core[0]) % 2
                wire[side, chip, :, : 2 * D] = acc_up[rows * chip : rows * (chip + 1), 2 * D * half : 2 * D * (half + 1)].astype(BF16)
                for part in range(2):
                    start = rows * (4 * chip + 2 * half + part)
                    wire[side, chip, :, (2 + part) * D : (3 + part) * D] = acc_down[start : start + rows, :].astype(BF16)


def ffn_backward(core, counts, upstream, record, weights, chips, last):
    _, mod, _, _, _, middle, pre_act, branch = record
    _, right, down, _ = weights
    rows = D // chips
    return pl.pallas_call(
        functools.partial(ffn_kernel, chips, last=last),
        grid=(SLOT,),
        out_shape=(
            tokens(D, F32),
            jax.ShapeDtypeStruct((24, D), F32),
            jax.ShapeDtypeStruct((1, FF + D), F32),
            jax.ShapeDtypeStruct((2, chips, rows, 4 * D), BF16),
        ),
        in_specs=[
            SMEM,
            SMEM,
            per_slot(D),
            per_slot(D),
            per_slot(FF),
            per_slot(D),
            whole(SLOT, 6 * D),
            whole(D, HALF),
            whole(FF, D),
        ],
        out_specs=(
            per_slot(D),
            whole(24, D),
            whole(1, FF + D),
            whole(2, chips, rows, 4 * D),
        ),
        scratch_shapes=[pltpu.VMEM((D, FF), F32), pltpu.VMEM((FF, D), F32)],
        compiler_params=params_of(1),
        cost_estimate=cost(8 * 10**9, 20 * 2**20),
        name="ffn_backward",
    )(core, counts, upstream, branch, pre_act, middle, mod, right, down)


def attention_kernel(chips, core, d_middle, hidden, qkv, attended, projected, mod, left, right, d_mod_in, bias_in, cond, d_cond_in, d_hidden, d_cond, wire, acc, acc_proj, d_mod, bias, *, first):
    slot = pl.program_id(0)

    @pl.when(slot == 0)
    def _():
        acc[...] = jnp.zeros_like(acc)
        acc_proj[...] = jnp.zeros_like(acc_proj)
        bias[...] = jnp.zeros_like(bias)
        d_mod[...] = d_mod_in[...]

    d_mid = d_middle[0]
    d_proj = d_mid * mod_part(mod, slot, 2)
    d_mod[pl.ds(8 + slot, 1), :] = row_sum(d_mid * projected[0])
    bias[:, 8 * D : 9 * D] += row_sum(d_proj)
    low = d_proj.astype(BF16)
    acc_proj[...] += left_product(attended[0], low)
    d_heads = right_product(low, right[:, 2 * D : 3 * D]).astype(BF16)
    factor = 1.0 / math.sqrt(HEAD)
    scaled = qkv[0, :, :D] * jnp.asarray(factor, BF16)
    keys = qkv[0, :, D : 2 * D]
    heads_in = qkv[0, :, 2 * D :]
    d_query, d_keys, d_values = [], [], []
    for head in range(HEADS):
        span = slice(head * HEAD, (head + 1) * HEAD)
        scores = right_product(keys[:, span], scaled[:, span])
        raised = jnp.exp(scores - jnp.max(scores, axis=0, keepdims=True))
        probs = raised * (1.0 / jnp.sum(raised, axis=0, keepdims=True))
        d_probs = right_product(heads_in[:, span], d_heads[:, span])
        d_values.append(dot_nn(probs.astype(BF16), d_heads[:, span]))
        weighted = probs * d_probs
        d_scores = (weighted - probs * jnp.sum(weighted, axis=0, keepdims=True)).astype(BF16)
        d_keys.append(dot_nn(d_scores, scaled[:, span]))
        d_query.append(left_product(d_scores, keys[:, span]) * factor)
    d_query = jnp.concatenate(d_query, axis=1)
    d_values = jnp.concatenate(d_values, axis=1)
    bias[:, 6 * D : 7 * D] += row_sum(d_query)
    bias[:, 7 * D : 8 * D] += row_sum(d_values)
    mixed = jnp.concatenate(
        [d_query.astype(BF16), jnp.concatenate(d_keys, axis=1).astype(BF16), d_values.astype(BF16)], axis=1
    )
    normed, rstd = norm_stats(hidden[0].astype(F32))
    scale = mod_part(mod, slot, 1)
    shifted = (normed * (1.0 + scale) + mod_part(mod, slot, 0)).astype(BF16)
    acc[...] += left_product(shifted, mixed)
    d_normed = right_product(mixed[:, :D], left[:, 6 * D :]) + right_product(mixed[:, D:], right[:, : 2 * D])
    d_mod[pl.ds(slot, 1), :] = row_sum(d_normed)
    d_mod[pl.ds(4 + slot, 1), :] = row_sum(d_normed * normed)
    d_hidden[0] = d_mid + norm_backward(d_normed, normed, rstd, scale)

    @pl.when(slot == SLOT - 1)
    def _():
        rows = D // chips
        bias[:, 9 * D :] = bias_in[...]
        total = d_cond_in[...]
        for part in range(6):
            grads = d_mod[SLOT * part : SLOT * (part + 1), :]
            bias[:, part * D : (part + 1) * D] = row_sum(grads)
            total = total + right_product(grads.astype(BF16), left[:, part * D : (part + 1) * D])
        if first:
            wide_cond = cond[...].astype(F32)
            gate = 1.0 / (1.0 + jnp.exp(-wide_cond))
            total = total * (gate * (1.0 + wide_cond * (1.0 - gate)))
        d_cond[...] = total
        low_mod = d_mod[...].astype(BF16)
        for chip in range(chips):
            span = slice(rows * chip, rows * (chip + 1))
            wire[core[0], chip, :, : 2 * D] = acc[span, : 2 * D].astype(BF16)
            wire[1 - core[0], chip, :, :D] = acc[span, 2 * D :].astype(BF16)
            wire[1 - core[0], chip, :, D : 2 * D] = acc_proj[span, :].astype(BF16)
            for half in range(2):
                pieces = []
                for part in range(2):
                    chunk = 4 * chip + 2 * half + part
                    if chunk < BIAS // 128:
                        pieces.append(bias[:, chunk * 128 : (chunk + 1) * 128])
                    else:
                        pieces.append(jnp.zeros((1, 128), F32))
                pieces.append(jnp.zeros((rows - 2, 128), F32))
                side = (half + core[0]) % 2
                wire[side, chip, :, 2 * D : 2 * D + 128] = jnp.concatenate(pieces, axis=0).astype(BF16)
                wire[side, chip, :, 2 * D + 128 :] = low_mod


def attention_backward(core, d_middle, hidden, record, weights, d_mod, bias, cond, d_cond, chips, first):
    _, mod, qkv, attended, projected, _, _, _ = record
    left, right, _, _ = weights
    rows = D // chips
    return pl.pallas_call(
        functools.partial(attention_kernel, chips, first=first),
        grid=(SLOT,),
        out_shape=(
            tokens(D, F32),
            jax.ShapeDtypeStruct((SLOT, D), F32),
            jax.ShapeDtypeStruct((2, chips, rows, 3 * D + 128), BF16),
        ),
        in_specs=[
            SMEM,
            per_slot(D),
            per_slot(D),
            per_slot(3 * D),
            per_slot(D),
            per_slot(D),
            whole(SLOT, 6 * D),
            whole(D, HALF),
            whole(D, HALF),
            whole(24, D),
            whole(1, FF + D),
            whole(SLOT, D),
            whole(SLOT, D),
        ],
        out_specs=(
            per_slot(D),
            whole(SLOT, D),
            whole(2, chips, rows, 3 * D + 128),
        ),
        scratch_shapes=[
            pltpu.VMEM((D, 3 * D), F32),
            pltpu.VMEM((D, D), F32),
            pltpu.VMEM((24, D), F32),
            pltpu.VMEM((1, BIAS), F32),
        ],
        compiler_params=params_of(1),
        cost_estimate=cost(6 * 10**9, 20 * 2**20),
        name="attention_backward",
    )(core, d_middle, hidden, qkv, attended, projected, mod, left, right, d_mod, bias, cond, d_cond)


def finish_kernel(chips, core, own_ffn, own_attn, got_ffn, got_attn, own_mod, got_mod, cond, chip, ada_out, qkv_out, proj_out, fc1_out, fc2_out, bias_out):
    rows = D // (2 * chips)
    is_odd = core[0] == 1
    mine = 2 * chip[0] + core[0]
    take = lax.broadcasted_iota(jnp.int32, (16, D), 0)
    column = lax.broadcasted_iota(jnp.int32, (16, D), 1)
    pick = ((column == rows * mine + take) & (take < rows)).astype(F32).astype(BF16)
    chosen = [right_product(pick, cond[side].astype(BF16)).astype(BF16) for side in range(2)]
    slots = SLOT * chips
    source = lax.broadcasted_iota(jnp.int32, (slots, 24 * chips), 0)
    target = lax.broadcasted_iota(jnp.int32, (slots, 24 * chips), 1)
    places = []
    for part in range(6):
        place = (target == 24 * (source // SLOT) + SLOT * part + source % SLOT).astype(F32).astype(BF16)
        places.append([dot_nn(chosen[side], place).astype(BF16) for side in range(2)])
    for layer in range(2):
        even = jnp.where(is_odd, got_mod[layer], own_mod[layer])
        odd = jnp.where(is_odd, own_mod[layer], got_mod[layer])
        for part in range(6):
            block = dot_nn(places[part][0], even) + dot_nn(places[part][1], odd)
            for row in range(rows):
                start = row * 6 * D + part * D
                ada_out[layer : layer + 1, start : start + D] = block[row : row + 1]
        own = jnp.where(is_odd, own_ffn[layer, rows:, :], own_ffn[layer, :rows, :])
        got = got_ffn[layer]
        first = jnp.where(is_odd, got, own[:, : 2 * D])
        second = jnp.where(is_odd, own[:, : 2 * D], got)
        for row in range(rows):
            fc1_out[layer : layer + 1, row * FF : row * FF + 2 * D] = first[row : row + 1]
            fc1_out[layer : layer + 1, row * FF + 2 * D : (row + 1) * FF] = second[row : row + 1]
        for row in range(4 * rows):
            column_start = (2 + row // (2 * rows)) * D
            fc2_out[layer : layer + 1, row * D : (row + 1) * D] = own_ffn[
                layer, row % (2 * rows) : row % (2 * rows) + 1, column_start : column_start + D
            ]
        own = jnp.where(is_odd, own_attn[layer, rows:, :], own_attn[layer, :rows, :])
        got = got_attn[layer]
        first = jnp.where(is_odd, got, own[:, : 2 * D])
        second = jnp.where(is_odd, own[:, : 2 * D], got)
        for row in range(rows):
            qkv_out[layer : layer + 1, row * 3 * D : row * 3 * D + 2 * D] = first[row : row + 1]
            qkv_out[layer : layer + 1, row * 3 * D + 2 * D : (row + 1) * 3 * D] = second[row : row + 1, :D]
            proj_out[layer : layer + 1, row * D : (row + 1) * D] = second[row : row + 1, D:]
        for part in range(2):
            bias_out[layer : layer + 1, part * 128 : (part + 1) * 128] = own_attn[
                layer, part : part + 1, 2 * D : 2 * D + 128
            ]


def finish(core, chip, own_ffn, own_attn, got_ffn, got_attn, own_mod, got_mod, cond, shapes, chips):
    return pl.pallas_call(
        functools.partial(finish_kernel, chips),
        out_shape=tuple(jax.ShapeDtypeStruct(shape, F32) for shape in shapes),
        in_specs=[SMEM] + [VMEM] * 7 + [SMEM],
        out_specs=(VMEM,) * 6,
        compiler_params=params_of(),
        name="finish",
    )(core, own_ffn, own_attn, got_ffn, got_attn, own_mod, got_mod, cond, chip)


def fast_body(
    latents_in, condition, counts, ada_weight, qkv_weight, proj_weight, fc1_weight, fc2_weight, biases, cotangent
):
    devices = lax.axis_size("fsdp")
    chips = devices // 2
    rows = D // devices
    index = lax.axis_index("fsdp")
    core, chip = (index % 2).reshape(1), (index // 2).reshape(1)
    pairs = [[2 * one, 2 * one + 1] for one in range(chips)]
    across = [[2 * one + side for one in range(chips)] for side in range(2)]
    swap = [(one, one ^ 1) for one in range(devices)]

    lines = [[8 * level + one for level in range(4)] for one in range(8)]
    place = jnp.stack([index % 2, (index // 2) % 4])
    tie = lax.optimization_barrier

    def along(value, bit):
        return lax.ppermute(value, "fsdp", [(one, one ^ bit) for one in range(devices)])

    def stacked(copies):
        return lax.all_to_all(copies, "fsdp", 0, 0, axis_index_groups=lines, tiled=True)

    def spread_out(stack):
        low, high = stack[:2], stack[2:]
        low_x, high_y = along(low, 2), along(high, 4)
        low_y, high_x = along(low, 4), along(high, 2)
        return low, high, low_x, high_x, low_y, high_y

    def spread_more(held):
        low_x, high_y = held[2], held[5]
        held = (*held, along(low_x, 4), along(high_y, 2))
        return (*held, *[along(value, 1) for value in held])

    copies_first, copies_last = pack(
        ada_weight, qkv_weight, proj_weight, fc1_weight, fc2_weight, biases, condition, rows, 4
    )
    stack_first = stacked(copies_first)
    stack_first, copies_last = tie((stack_first, copies_last))
    stack_last = stacked(copies_last)
    *first_weights, cond_all = unpack_wire(place, spread_more(spread_out(stack_first)))
    held_last = spread_out(stack_last)
    first = forward_block(counts, latents_in, condition, first_weights, False)
    held_last, first = tie((held_last, first))
    *last_weights, _ = unpack_wire(place, spread_more(held_last))
    last = forward_block(counts, first[0], condition, last_weights, True)
    weights, records, hidden = [first_weights, last_weights], [first, last], [latents_in, first[0], last[0]]
    upstream = cotangent
    d_cond = jnp.zeros((SLOT, D), F32)
    reduced = [None, None]

    def paired(wire, width):
        got = lax.ppermute(wire[1], "fsdp", swap)
        both = (wire[0].astype(F32) + got.astype(F32))[:, :, :width].astype(BF16)
        if width < wire.shape[-1]:
            both = jnp.concatenate([both, wire[0, :, :, width:]], axis=2)
        return both

    def summed(both, width):
        spread = lax.all_to_all(both, "fsdp", 0, 0, axis_index_groups=across, tiled=True)
        return jnp.sum(spread[:, :, :width].astype(F32), axis=0), spread[:, :, width:]

    d_middle, d_mod, bias, wire = ffn_backward(core, counts, upstream, records[1], weights[1], chips, True)
    d_middle, both = tie((d_middle, paired(wire, 4 * D)))
    ffn_last, _ = summed(both, 4 * D)
    upstream, d_cond, wire = attention_backward(
        core, d_middle, hidden[1], records[1], weights[1], d_mod, bias, condition, d_cond, chips, False
    )
    wire, ffn_last = tie((wire, ffn_last))
    upstream, both = tie((upstream, paired(wire, 2 * D + 128)))
    attn_last, mods_last = summed(both, 2 * D + 128)
    d_middle, d_mod, bias, wire = ffn_backward(core, counts, upstream, records[0], weights[0], chips, False)
    wire, attn_last, mods_last = tie((wire, attn_last, mods_last))
    d_middle, both = tie((d_middle, paired(wire, 4 * D)))
    ffn_first, _ = summed(both, 4 * D)
    upstream, d_cond, wire = attention_backward(
        core, d_middle, hidden[0], records[0], weights[0], d_mod, bias, condition, d_cond, chips, True
    )
    wire, ffn_first = tie((wire, ffn_first))
    attn_first, mods_first = summed(paired(wire, 2 * D + 128), 2 * D + 128)
    reduced[0] = (ffn_first, attn_first, mods_first.reshape(24 * chips, D))
    reduced[1] = (ffn_last, attn_last, mods_last.reshape(24 * chips, D))
    own_ffn = jnp.stack([reduced[layer][0] for layer in range(2)])
    own_attn = jnp.stack([reduced[layer][1] for layer in range(2)])
    own_mod = jnp.stack([reduced[layer][2] for layer in range(2)])
    start = (1 - index % 2) * rows
    to_send = jnp.concatenate([own_ffn[:, :, : 2 * D], own_attn[:, :, : 2 * D]], axis=2)
    got = lax.ppermute(lax.dynamic_slice_in_dim(to_send, start, rows, axis=1), "fsdp", swap)
    got_mod = lax.ppermute(own_mod, "fsdp", swap)
    shapes = [array.shape for array in (ada_weight, qkv_weight, proj_weight, fc1_weight, fc2_weight, biases)]
    grads = finish(
        core, chip, own_ffn, own_attn, got[:, :, : 2 * D], got[:, :, 2 * D :], own_mod, got_mod, cond_all, shapes, chips
    )
    return (hidden[2], upstream, d_cond, *grads)


def choose_body(
    latents_in, condition, counts, ada_weight, qkv_weight, proj_weight, fc1_weight, fc2_weight, biases, cotangent
):
    devices = lax.axis_size("fsdp")
    rows = D // devices
    fits = (
        D % devices == 0
        and devices == 32
        and latents_in.shape == (SLOT, SEQ, D)
        and ada_weight.shape == (2, rows * 6 * D)
        and qkv_weight.shape == (2, rows * 3 * D)
        and proj_weight.shape == (2, rows * D)
        and fc1_weight.shape == (2, rows * FF)
        and fc2_weight.shape == (2, rows * FF)
        and biases.shape == (2, 256)
    )
    chosen = fast_body if fits else body
    return chosen(
        latents_in, condition, counts, ada_weight, qkv_weight, proj_weight, fc1_weight, fc2_weight, biases, cotangent
    )


def solution(mesh):
    return jax.shard_map(
        choose_body,
        mesh=mesh,
        in_specs=(
            P("fsdp", None, None),
            P("fsdp", None),
            P("fsdp"),
            P(None, "fsdp"),
            P(None, "fsdp"),
            P(None, "fsdp"),
            P(None, "fsdp"),
            P(None, "fsdp"),
            P(None, "fsdp"),
            P("fsdp", None, None),
        ),
        out_specs=(
            P("fsdp", None, None),
            P("fsdp", None, None),
            P("fsdp", None),
            P(None, "fsdp"),
            P(None, "fsdp"),
            P(None, "fsdp"),
            P(None, "fsdp"),
            P(None, "fsdp"),
            P(None, "fsdp"),
        ),
        check_vma=False,
    )
```

```python
import functools
import math

import jax
import jax.numpy as jnp
from jax import lax
from jax.experimental import pallas as pl
from jax.experimental.pallas import tpu as pltpu
from jax.sharding import PartitionSpec as P

D = 384
HEADS = 6
HEAD = 64
FF = 1536


EPSILON = 1e-06


def modulate_norm(values_in, shift_add, scale_mul):
    centred = values_in - jnp.mean(values_in, axis=-1, keepdims=True)
    variance = jnp.mean(centred * centred, axis=-1, keepdims=True)
    normed = centred * lax.rsqrt(variance + EPSILON)
    return normed * (1.0 + scale_mul[:, None, :]) + shift_add[:, None, :]


def gelu_tanh(values_in):
    return jax.nn.gelu(values_in, approximate=True)


def left_product(left, right):
    return lax.dot_general(
        left, right, (((0,), (0,)), ((), ())), preferred_element_type=jnp.float32
    )


def right_product(left, right):
    return lax.dot_general(
        left, right, (((1,), (1,)), ((), ())), preferred_element_type=jnp.float32
    )


def unpack(gathered):
    ada_flat, qkv_flat, proj_flat, fc1_flat, fc2_flat, bias_flat = gathered
    bias_wide = bias_flat.astype(jnp.float32)
    return (
        ada_flat.reshape(D, 6 * D),
        qkv_flat[: 3 * D * D].reshape(D, 3 * D),
        proj_flat[: D * D].reshape(D, D),
        fc1_flat.reshape(D, FF),
        fc2_flat.reshape(FF, D),
        bias_wide[: 6 * D],
        bias_wide[6 * D : 7 * D],
        bias_wide[7 * D : 8 * D],
        bias_wide[8 * D : 9 * D],
        bias_wide[9 * D : 9 * D + FF],
        bias_wide[9 * D + FF : 10 * D + FF],
    )


def split_modulation(modulation):
    return [modulation[:, part_index * D : (part_index + 1) * D] for part_index in range(6)]


def layer_forward(hidden, cond_act, params):
    w_ada, w_qkv, w_proj, w_fc1, w_fc2, b_ada, b_query, b_value, b_proj, b_fc1, b_fc2 = params
    slot_count, seq_len = (hidden.shape[0], hidden.shape[1])
    modulation = jnp.dot(cond_act, w_ada, preferred_element_type=jnp.float32) + b_ada
    shift_attn, scale_attn, gate_attn, shift_ffn, scale_ffn, gate_ffn = split_modulation(modulation)
    normed_attn = modulate_norm(hidden, shift_attn, scale_attn).astype(jnp.bfloat16).reshape(-1, D)
    mixed_qkv = jnp.dot(normed_attn, w_qkv, preferred_element_type=jnp.float32)
    queries = (
        (mixed_qkv[:, 0:D] + b_query).astype(jnp.bfloat16).reshape(slot_count, seq_len, HEADS, HEAD)
    )
    key_heads = (
        mixed_qkv[:, D : 2 * D].astype(jnp.bfloat16).reshape(slot_count, seq_len, HEADS, HEAD)
    )
    value_heads = (
        (mixed_qkv[:, 2 * D : 3 * D] + b_value)
        .astype(jnp.bfloat16)
        .reshape(slot_count, seq_len, HEADS, HEAD)
    )
    scores = jnp.einsum(
        "bqhd,bkhd->bhqk", queries, key_heads, preferred_element_type=jnp.float32
    ) * (1.0 / math.sqrt(HEAD))
    peak_score = jnp.max(scores, axis=-1, keepdims=True)
    exp_scores = jnp.exp(scores - peak_score)
    exp_total = jnp.sum(exp_scores, axis=-1, keepdims=True)
    logsum = peak_score + jnp.log(exp_total)
    attn_probs = (exp_scores / exp_total).astype(jnp.bfloat16)
    attended = jnp.einsum(
        "bhqk,bkhd->bqhd", attn_probs, value_heads, preferred_element_type=jnp.float32
    )
    attended = attended.astype(jnp.bfloat16).reshape(-1, D)
    projected = (jnp.dot(attended, w_proj, preferred_element_type=jnp.float32) + b_proj).reshape(
        slot_count, seq_len, D
    )
    middle = hidden + gate_attn[:, None, :] * projected
    normed_ffn = modulate_norm(middle, shift_ffn, scale_ffn).astype(jnp.bfloat16).reshape(-1, D)
    pre_act = jnp.dot(normed_ffn, w_fc1, preferred_element_type=jnp.float32) + b_fc1
    activation = gelu_tanh(pre_act).astype(jnp.bfloat16)
    branch = (jnp.dot(activation, w_fc2, preferred_element_type=jnp.float32) + b_fc2).reshape(
        slot_count, seq_len, D
    )
    result = middle + gate_ffn[:, None, :] * branch
    record = (
        hidden,
        modulation,
        normed_attn,
        queries,
        key_heads,
        value_heads,
        logsum,
        attended,
        projected,
        middle,
        normed_ffn,
        pre_act,
        activation,
        branch,
    )
    return (result, record)


def layer_backward(upstream, params, record):
    w_ada, w_qkv, w_proj, w_fc1, w_fc2, b_ada, b_query, b_value, b_proj, b_fc1, b_fc2 = params
    (
        hidden,
        modulation,
        normed_attn,
        queries,
        key_heads,
        value_heads,
        logsum,
        attended,
        projected,
        middle,
        normed_ffn,
        pre_act,
        activation,
        branch,
    ) = record
    slot_count, seq_len = (hidden.shape[0], hidden.shape[1])
    shift_attn, scale_attn, gate_attn, shift_ffn, scale_ffn, gate_ffn = split_modulation(modulation)
    d_branch = (upstream * gate_ffn[:, None, :]).reshape(-1, D)
    d_gate_ffn = jnp.sum(upstream * branch, axis=1)
    grad_b_fc2 = jnp.sum(d_branch, axis=0)
    branch_low = d_branch.astype(jnp.bfloat16)
    grad_w_fc2 = left_product(activation, branch_low)
    d_act = right_product(branch_low, w_fc2)
    gelu_out, gelu_pull = jax.vjp(gelu_tanh, pre_act)
    (d_pre,) = gelu_pull(d_act)
    grad_b_fc1 = jnp.sum(d_pre, axis=0)
    pre_low = d_pre.astype(jnp.bfloat16)
    grad_w_fc1 = left_product(normed_ffn, pre_low)
    d_normed_ffn = right_product(pre_low, w_fc1).reshape(slot_count, seq_len, D)
    norm_out, norm_pull = jax.vjp(modulate_norm, middle, shift_ffn, scale_ffn)
    middle_part, d_shift_ffn, d_scale_ffn = norm_pull(d_normed_ffn)
    d_middle = upstream + middle_part
    d_proj = (d_middle * gate_attn[:, None, :]).reshape(-1, D)
    d_gate_attn = jnp.sum(d_middle * projected, axis=1)
    grad_b_proj = jnp.sum(d_proj, axis=0)
    proj_low = d_proj.astype(jnp.bfloat16)
    grad_w_proj = left_product(attended, proj_low)
    d_attended = (
        right_product(proj_low, w_proj)
        .astype(jnp.bfloat16)
        .reshape(slot_count, seq_len, HEADS, HEAD)
    )
    scores = jnp.einsum(
        "bqhd,bkhd->bhqk", queries, key_heads, preferred_element_type=jnp.float32
    ) * (1.0 / math.sqrt(HEAD))
    attn_probs = jnp.exp(scores - logsum)
    d_probs = jnp.einsum(
        "bqhd,bkhd->bhqk", d_attended, value_heads, preferred_element_type=jnp.float32
    )
    d_values = jnp.einsum(
        "bhqk,bqhd->bkhd",
        attn_probs.astype(jnp.bfloat16),
        d_attended,
        preferred_element_type=jnp.float32,
    )
    row_inner = jnp.sum(attn_probs * d_probs, axis=-1, keepdims=True)
    d_scores = (attn_probs * (d_probs - row_inner) * (1.0 / math.sqrt(HEAD))).astype(jnp.bfloat16)
    d_query = jnp.einsum(
        "bhqk,bkhd->bqhd", d_scores, key_heads, preferred_element_type=jnp.float32
    ).reshape(-1, D)
    d_keys = jnp.einsum(
        "bhqk,bqhd->bkhd", d_scores, queries, preferred_element_type=jnp.float32
    ).reshape(-1, D)
    d_values = d_values.reshape(-1, D)
    grad_b_query = jnp.sum(d_query, axis=0)
    grad_b_value = jnp.sum(d_values, axis=0)
    mixed_low = jnp.concatenate([d_query, d_keys, d_values], axis=1).astype(jnp.bfloat16)
    grad_w_qkv = left_product(normed_attn, mixed_low)
    d_normed_attn = right_product(mixed_low, w_qkv).reshape(slot_count, seq_len, D)
    attn_out, attn_pull = jax.vjp(modulate_norm, hidden, shift_attn, scale_attn)
    hidden_part, d_shift_attn, d_scale_attn = attn_pull(d_normed_attn)
    d_hidden = d_middle + hidden_part
    d_mod = jnp.concatenate(
        [d_shift_attn, d_scale_attn, d_gate_attn, d_shift_ffn, d_scale_ffn, d_gate_ffn], axis=1
    )
    grad_b_ada = jnp.sum(d_mod, axis=0)
    mod_low = d_mod.astype(jnp.bfloat16)
    d_cond = right_product(mod_low, w_ada)
    grad_bias = jnp.concatenate(
        [grad_b_ada, grad_b_query, grad_b_value, grad_b_proj, grad_b_fc1, grad_b_fc2]
    )
    return (d_hidden, d_cond, mod_low, (grad_w_qkv, grad_w_proj, grad_w_fc1, grad_w_fc2, grad_bias))


def pad_flat(values_in, length):
    flat = values_in.reshape(-1)
    return jnp.pad(flat, (0, length - flat.shape[0]))


def body(
    latents_in,
    condition,
    counts,
    ada_weight,
    qkv_weight,
    proj_weight,
    fc1_weight,
    fc2_weight,
    biases,
    cotangent,
):
    slot_count = latents_in.shape[0]
    layer_total = ada_weight.shape[0]
    device_count = lax.axis_size("fsdp")
    rest_list = (qkv_weight, proj_weight, fc1_weight, fc2_weight, biases)
    rest_lengths = [piece.shape[1] * device_count for piece in rest_list]
    ada_shard = ada_weight.shape[1]
    occupied = (jnp.arange(slot_count) < counts[0]).astype(jnp.float32)
    cond_wide = condition.astype(jnp.float32)
    silu_out, silu_pull = jax.vjp(jax.nn.silu, cond_wide)
    cond_act = silu_out.astype(jnp.bfloat16)
    hidden = latents_in.astype(jnp.float32)
    records = []
    for layer_index in range(layer_total):
        gathered = (
            lax.all_gather(ada_weight[layer_index], "fsdp", axis=0, tiled=True),
            lax.all_gather(qkv_weight[layer_index], "fsdp", axis=0, tiled=True),
            lax.all_gather(proj_weight[layer_index], "fsdp", axis=0, tiled=True),
            lax.all_gather(fc1_weight[layer_index], "fsdp", axis=0, tiled=True),
            lax.all_gather(fc2_weight[layer_index], "fsdp", axis=0, tiled=True),
            lax.all_gather(biases[layer_index], "fsdp", axis=0, tiled=True),
        )
        params = unpack(gathered)
        hidden, record = layer_forward(hidden, cond_act, params)
        records.append(record)
    latents_out = hidden * occupied[:, None, None]
    upstream = cotangent.astype(jnp.float32) * occupied[:, None, None]
    cond_total = jnp.zeros(cond_wide.shape, jnp.float32)
    layer_sums = [None] * layer_total
    mod_lows = [None] * layer_total
    for layer_index in reversed(range(layer_total)):
        gathered = (
            lax.all_gather(ada_weight[layer_index], "fsdp", axis=0, tiled=True),
            lax.all_gather(qkv_weight[layer_index], "fsdp", axis=0, tiled=True),
            lax.all_gather(proj_weight[layer_index], "fsdp", axis=0, tiled=True),
            lax.all_gather(fc1_weight[layer_index], "fsdp", axis=0, tiled=True),
            lax.all_gather(fc2_weight[layer_index], "fsdp", axis=0, tiled=True),
            lax.all_gather(biases[layer_index], "fsdp", axis=0, tiled=True),
        )
        params = unpack(gathered)
        upstream, d_cond, mod_low, grad_parts = layer_backward(
            upstream, params, records[layer_index]
        )
        mod_lows[layer_index] = mod_low
        cond_total = cond_total + d_cond
        padded = [
            pad_flat(grad_parts[part_index], rest_lengths[part_index]) for part_index in range(5)
        ]
        layer_sums[layer_index] = (
            lax.psum_scatter(padded[0], "fsdp", scatter_dimension=0, tiled=True),
            lax.psum_scatter(padded[1], "fsdp", scatter_dimension=0, tiled=True),
            lax.psum_scatter(padded[2], "fsdp", scatter_dimension=0, tiled=True),
            lax.psum_scatter(padded[3], "fsdp", scatter_dimension=0, tiled=True),
            lax.psum_scatter(padded[4], "fsdp", scatter_dimension=0, tiled=True),
        )
    grad_rest = [
        jnp.stack([layer_sums[layer_index][part_index] for layer_index in range(layer_total)])
        for part_index in range(5)
    ]
    mod_joined = jnp.concatenate(mod_lows, axis=1)
    ada_full = left_product(
        lax.all_gather(cond_act, "fsdp", axis=0, tiled=True),
        lax.all_gather(mod_joined, "fsdp", axis=0, tiled=True),
    )
    own_start = lax.axis_index("fsdp") * ada_shard
    ada_rows = []
    for layer_index in range(layer_total):
        flat_layer = pad_flat(
            ada_full[:, layer_index * 6 * D : (layer_index + 1) * 6 * D], ada_shard * device_count
        )
        ada_rows.append(lax.dynamic_slice_in_dim(flat_layer, own_start, ada_shard))
    ada_grad = jnp.stack(ada_rows)
    (condition_grad,) = silu_pull(cond_total)
    return (
        latents_out,
        upstream,
        condition_grad,
        ada_grad,
        grad_rest[0],
        grad_rest[1],
        grad_rest[2],
        grad_rest[3],
        grad_rest[4],
    )


BF16 = jnp.bfloat16
F32 = jnp.float32
SLOT = 4
STEP = 1
CHUNK = 512
SEQ = 256
HALF = 7 * D
WIRE = HALF + 2 * D + 128
BIAS = 10 * D + FF
VMEM = pl.BlockSpec(memory_space=pltpu.VMEM)
SMEM = pl.BlockSpec(memory_space=pltpu.SMEM)


def params_of(grid_rank=0, megabytes=36):
    semantics = ("arbitrary",) * grid_rank if grid_rank else None
    return pltpu.CompilerParams(vmem_limit_bytes=megabytes * 2**20, dimension_semantics=semantics)


def dot_nn(left, right):
    return lax.dot_general(
        left, right, (((1,), (0,)), ((), ())), preferred_element_type=jnp.float32
    )


def pack_kernel(rows, ada_in, qkv_in, proj_in, fc1_in, fc2_in, bias_in, cond, out_left, out_right, out_last, ada, qkv, proj, fc1, fc2, bias, sems, wide):
    copies = [
        pltpu.make_async_copy(source, target, sems.at[place])
        for place, (source, target) in enumerate(
            ((ada_in, ada), (qkv_in, qkv), (proj_in, proj), (fc1_in, fc1), (fc2_in, fc2), (bias_in, bias))
        )
    ]
    for copy in copies:
        copy.start()
    wide[:, :, WIRE - 128 :] = jnp.zeros((2, 2 * rows, 128), F32)
    wide_cond = cond[...].astype(F32)
    act = (wide_cond / (1.0 + jnp.exp(-wide_cond))).astype(BF16).astype(F32)
    for part in range(3):
        wide[0, 8 + 4 * part : 12 + 4 * part, WIRE - 128 :] = act[:, part * 128 : part * 128 + 128]
    for copy in copies:
        copy.wait()

    def put(source, start, width, row, column):
        values = source[:, start : start + width].astype(F32)
        for layer in range(2):
            wide[layer, row : row + 1, column : column + width] = values[layer : layer + 1]

    for row in range(rows):
        put(ada, row * 6 * D, 6 * D, row, 0)
        put(qkv, row * 3 * D, D, row, 6 * D)
        put(qkv, row * 3 * D + D, 2 * D, rows + row, 0)
        put(proj, row * D, D, rows + row, 2 * D)
        put(fc1, row * FF, FF, rows + row, 3 * D)
    for row in range(4 * rows):
        put(fc2, row * D, D, row % (2 * rows), HALF + D * (row // (2 * rows)))
    put(bias, 0, 128, 0, WIRE - 128)
    put(bias, 128, 128, 1, WIRE - 128)
    low = wide[0].astype(BF16)
    low_last = wide[1].astype(BF16)
    for copy_index in range(out_last.shape[0]):
        out_left[copy_index] = low[:, : WIRE // 2]
        out_right[copy_index] = low[:, WIRE // 2 :]
        out_last[copy_index] = low_last


def pack(ada, qkv, proj, fc1, fc2, bias, cond, rows, copies):
    flat = (ada, qkv, proj, fc1, fc2, bias)
    return pl.pallas_call(
        functools.partial(pack_kernel, rows),
        out_shape=tuple(
            jax.ShapeDtypeStruct((copies, 2 * rows, width), BF16) for width in (WIRE // 2, WIRE // 2, WIRE)
        ),
        in_specs=[pl.BlockSpec(memory_space=pltpu.HBM)] * 6 + [VMEM],
        out_specs=(VMEM,) * 3,
        scratch_shapes=[pltpu.VMEM(array.shape, BF16) for array in flat]
        + [pltpu.SemaphoreType.DMA((6,)), pltpu.VMEM((2, 2 * rows, WIRE), F32)],
        compiler_params=params_of(0, 62),
        name="pack",
    )(*flat, cond)


def unpack_kernel(rows, spots, place, *refs):
    blocks, (left, right, down, bias, cond, wire, sems) = refs[:-7], refs[-7:]
    copies = []
    for number, (block, (side, step, level, column)) in enumerate(zip(blocks, spots, strict=True)):
        target = wire.at[
            (place[0] + side) % 2,
            place[1] ^ step,
            pl.ds(level, block.shape[0]),
            :,
            pl.ds(column, block.shape[2]),
        ]
        copies.append(pltpu.make_async_copy(block, target, sems.at[number]))
    for copy in copies:
        copy.start()
    for copy in copies:
        copy.wait()

    def of(device):
        return wire.at[device % 2, (device // 2) % 4, device // 8]

    for group in range(8):
        for half, target in ((0, left), (1, right)):
            target[4 * rows * group : 4 * rows * (group + 1), :] = jnp.concatenate(
                [of(4 * group + member)[half * rows : (half + 1) * rows, :HALF] for member in range(4)], axis=0
            )
    for device in range(32):
        for part in range(2):
            start = 4 * rows * device + 2 * rows * part
            column = HALF + D * part
            down[start : start + 2 * rows, :] = of(device)[:, column : column + D]
        tail = of(device)[:, WIRE - 128 :].astype(F32)
        for part in range(2):
            chunk = 2 * device + part
            if chunk < BIAS // 128:
                bias[0:1, chunk * 128 : chunk * 128 + 128] = tail[part : part + 1]
        for part in range(3):
            cond[device % 2, 4 * (device // 2) : 4 * (device // 2) + 4, part * 128 : part * 128 + 128] = tail[
                8 + 4 * part : 12 + 4 * part
            ]


def unpack_wire(place, held):
    blocks, spots = [block for block, _ in held], [spot for _, spot in held]
    rows = blocks[0].shape[1] // 2
    return pl.pallas_call(
        functools.partial(unpack_kernel, rows, spots),
        out_shape=(
            jax.ShapeDtypeStruct((D, HALF), BF16),
            jax.ShapeDtypeStruct((D, HALF), BF16),
            jax.ShapeDtypeStruct((FF, D), BF16),
            jax.ShapeDtypeStruct((1, BIAS), F32),
            jax.ShapeDtypeStruct((2, SLOT * 16, D), F32),
        ),
        in_specs=[SMEM] + [pl.BlockSpec(memory_space=pl.ANY)] * len(blocks),
        out_specs=(VMEM,) * 5,
        scratch_shapes=[pltpu.VMEM((2, 4, 4, 2 * rows, WIRE), BF16), pltpu.SemaphoreType.DMA((len(blocks),))],
        compiler_params=params_of(0, 24),
        name="unpack",
    )(place, *blocks)


def norm_stats(values):
    centred = values - jnp.mean(values, axis=-1, keepdims=True)
    rstd = lax.rsqrt(jnp.mean(centred * centred, axis=-1, keepdims=True) + EPSILON)
    return centred * rstd, rstd


def mod_part(mod, step, part):
    rows = [
        jnp.broadcast_to(mod[pl.ds(STEP * step + slot, 1), part * D : (part + 1) * D], (SEQ, D))
        for slot in range(STEP)
    ]
    return rows[0] if STEP == 1 else jnp.concatenate(rows, axis=0)


def put_sums(d_mod, step, part, values):
    for slot in range(STEP):
        d_mod[pl.ds(SLOT * part + STEP * step + slot, 1), :] = row_sum(values[slot * SEQ : (slot + 1) * SEQ])


def occupied(counts, step):
    rows = [
        jnp.full((SEQ, 1), jnp.where(STEP * step + slot < counts[0], 1.0, 0.0), F32) for slot in range(STEP)
    ]
    return rows[0] if STEP == 1 else jnp.concatenate(rows, axis=0)


def flat(ref):
    return ref[...].reshape(STEP * SEQ, ref.shape[2])


def gelu_and_slope(pre):
    factor, cubic = 0.7978845608028654, 0.044715
    square = pre * pre
    half = 0.5 + 0.5 * jnp.tanh(pre * (factor + (factor * cubic) * square))
    act = pre * half
    return act, half + act * (1.0 - half) * (2.0 * factor + (6.0 * factor * cubic) * square)


def row_sum(values):
    return jnp.sum(values, axis=0, keepdims=True)


def head_masks(factor):
    lane = lax.broadcasted_iota(jnp.int32, (1, 2 * HEAD), 1)
    first = jnp.where(lane < HEAD, factor, 0.0).astype(BF16)
    second = jnp.where(lane < HEAD, 0.0, factor).astype(BF16)
    return first, second


def both_heads(pair, masks):
    return jnp.concatenate([pair * masks[0], pair * masks[1]], axis=0)


def merge_heads(stack):
    lane = lax.broadcasted_iota(jnp.int32, (SEQ, 2 * HEAD), 1)
    return jnp.where(lane < HEAD, stack[:SEQ], stack[SEQ:])


def softmax_keys(scores):
    raised = jnp.exp(scores - jnp.max(scores, axis=0, keepdims=True))
    return raised * (1.0 / jnp.sum(raised, axis=0, keepdims=True))


def forward_kernel(counts, hidden, cond, left, right, down, bias, out, mod, qkv, attended, projected, middle, active, slope, branch, *, last):
    step = pl.program_id(0)

    @pl.when(step == 0)
    def _():
        wide_cond = cond[...].astype(F32)
        act = (wide_cond / (1.0 + jnp.exp(-wide_cond))).astype(BF16)
        mod[...] = dot_nn(act, left[:, : 6 * D]) + bias[:, : 6 * D]

    values = flat(hidden).astype(F32)
    normed, _ = norm_stats(values)
    normed = (normed * (1.0 + mod_part(mod, step, 1)) + mod_part(mod, step, 0)).astype(BF16)
    queries = (dot_nn(normed, left[:, 6 * D :]) + bias[:, 6 * D : 7 * D]).astype(BF16)
    mixed = dot_nn(normed, right[:, : 2 * D])
    keys = mixed[:, :D].astype(BF16)
    heads_in = (mixed[:, D:] + bias[:, 7 * D : 8 * D]).astype(BF16)
    qkv[:, :, :D] = queries.reshape(STEP, SEQ, D)
    qkv[:, :, D : 2 * D] = keys.reshape(STEP, SEQ, D)
    qkv[:, :, 2 * D :] = heads_in.reshape(STEP, SEQ, D)
    masks = head_masks(1.0 / math.sqrt(HEAD))
    joined = []
    for slot in range(STEP):
        rows = slice(slot * SEQ, (slot + 1) * SEQ)
        pairs = []
        for pair in range(HEADS // 2):
            span = slice(pair * 2 * HEAD, (pair + 1) * 2 * HEAD)
            probs = softmax_keys(right_product(keys[rows, span], both_heads(queries[rows, span], masks)))
            pairs.append(merge_heads(left_product(probs.astype(BF16), heads_in[rows, span])).astype(BF16))
        joined.append(jnp.concatenate(pairs, axis=1))
    joined = joined[0] if STEP == 1 else jnp.concatenate(joined, axis=0)
    attended[...] = joined.reshape(STEP, SEQ, D)
    proj = dot_nn(joined, right[:, 2 * D : 3 * D]) + bias[:, 8 * D : 9 * D]
    projected[...] = proj.reshape(STEP, SEQ, D)
    mid = values + mod_part(mod, step, 2) * proj
    middle[...] = mid.reshape(STEP, SEQ, D)
    normed, _ = norm_stats(mid)
    normed = (normed * (1.0 + mod_part(mod, step, 4)) + mod_part(mod, step, 3)).astype(BF16)
    ffn = bias[:, 9 * D + FF :]
    for start in range(0, FF, CHUNK):
        stop = start + CHUNK
        pre = dot_nn(normed, right[:, 3 * D + start : 3 * D + stop]) + bias[:, 9 * D + start : 9 * D + stop]
        act, rate = gelu_and_slope(pre)
        act = act.astype(BF16)
        active[:, :, start:stop] = act.reshape(STEP, SEQ, CHUNK)
        slope[:, :, start:stop] = rate.reshape(STEP, SEQ, CHUNK)
        ffn = ffn + dot_nn(act, down[start:stop, :])
    branch[...] = ffn.reshape(STEP, SEQ, D)
    result = mid + mod_part(mod, step, 5) * ffn
    if last:
        result = result * occupied(counts, step)
    out[...] = result.reshape(STEP, SEQ, D)


def per_slot(width):
    return pl.BlockSpec((STEP, SEQ, width), lambda step: (step, 0, 0))


def whole(*shape):
    return pl.BlockSpec(shape, lambda step: (0,) * len(shape))


def tokens(width, dtype):
    return jax.ShapeDtypeStruct((SLOT, SEQ, width), dtype)


def cost(flops, moved):
    return pl.CostEstimate(flops=flops, bytes_accessed=moved, transcendentals=0)


def forward_block(counts, hidden, cond, weights, last):
    left, right, down, bias = weights
    return pl.pallas_call(
        functools.partial(forward_kernel, last=last),
        grid=(SLOT // STEP,),
        out_shape=(
            tokens(D, F32),
            jax.ShapeDtypeStruct((SLOT, 6 * D), F32),
            tokens(3 * D, BF16),
            tokens(D, BF16),
            tokens(D, F32),
            tokens(D, F32),
            tokens(FF, BF16),
            tokens(FF, F32),
            tokens(D, F32),
        ),
        in_specs=[
            SMEM,
            per_slot(D),
            whole(SLOT, D),
            whole(D, HALF),
            whole(D, HALF),
            whole(FF, D),
            whole(1, BIAS),
        ],
        out_specs=(
            per_slot(D),
            whole(SLOT, 6 * D),
            per_slot(3 * D),
            per_slot(D),
            per_slot(D),
            per_slot(D),
            per_slot(FF),
            per_slot(FF),
            per_slot(D),
        ),
        compiler_params=params_of(1),
        cost_estimate=cost(5 * 10**9, 20 * 2**20),
        name="forward_block",
    )(counts, hidden, cond, left, right, down, bias)


def norm_backward(d_normed, normed, rstd, scale):
    inner = d_normed * (1.0 + scale)
    along = jnp.mean(inner * normed, axis=-1, keepdims=True)
    return rstd * (inner - jnp.mean(inner, axis=-1, keepdims=True) - normed * along)


def ffn_kernel(chips, core, counts, upstream, branch, active, slope, middle, mod, right, down, d_middle, d_mod, bias, keep, send, acc_up, acc_down, *, last):
    step = pl.program_id(0)

    @pl.when(step == 0)
    def _():
        acc_up[...] = jnp.zeros_like(acc_up)
        acc_down[...] = jnp.zeros_like(acc_down)
        bias[...] = jnp.zeros_like(bias)
        d_mod[...] = jnp.zeros_like(d_mod)

    up = flat(upstream).astype(F32)
    if last:
        up = up * occupied(counts, step)
    d_branch = up * mod_part(mod, step, 5)
    put_sums(d_mod, step, 5, up * flat(branch))
    bias[:, FF:] += row_sum(d_branch)
    low = d_branch.astype(BF16)
    normed, rstd = norm_stats(flat(middle))
    scale = mod_part(mod, step, 4)
    shifted = (normed * (1.0 + scale) + mod_part(mod, step, 3)).astype(BF16)
    d_normed = 0.0
    for start in range(0, FF, CHUNK):
        stop = start + CHUNK
        d_pre = right_product(low, down[start:stop, :]) * slope[:, :, start:stop].reshape(STEP * SEQ, CHUNK)
        acc_down[start:stop, :] += left_product(active[:, :, start:stop].reshape(STEP * SEQ, CHUNK), low)
        bias[:, start:stop] += row_sum(d_pre)
        low_pre = d_pre.astype(BF16)
        acc_up[:, start:stop] += left_product(shifted, low_pre)
        d_normed = d_normed + right_product(low_pre, right[:, 3 * D + start : 3 * D + stop])
    put_sums(d_mod, step, 3, d_normed)
    put_sums(d_mod, step, 4, d_normed * normed)
    d_middle[...] = (up + norm_backward(d_normed, normed, rstd, scale)).reshape(STEP, SEQ, D)

    @pl.when(step == SLOT // STEP - 1)
    def _():
        rows = D // chips
        is_odd = core[0] == 1
        for chip in range(chips):
            span = slice(rows * chip, rows * (chip + 1))
            even, odd = acc_up[span, : 2 * D], acc_up[span, 2 * D :]
            keep[chip, :, : 2 * D] = jnp.where(is_odd, odd, even).astype(BF16)
            send[chip, :, : 2 * D] = jnp.where(is_odd, even, odd).astype(BF16)
            for part in range(2):
                start = rows * (4 * chip + part)
                even = acc_down[start : start + rows, :]
                odd = acc_down[start + 2 * rows : start + 3 * rows, :]
                keep[chip, :, (2 + part) * D : (3 + part) * D] = jnp.where(is_odd, odd, even).astype(BF16)
                send[chip, :, (2 + part) * D : (3 + part) * D] = jnp.where(is_odd, even, odd).astype(BF16)


def ffn_backward(core, counts, upstream, record, weights, chips, last):
    _, mod, _, _, _, middle, active, slope, branch = record
    _, right, down, _ = weights
    rows = D // chips
    return pl.pallas_call(
        functools.partial(ffn_kernel, chips, last=last),
        grid=(SLOT // STEP,),
        out_shape=(
            tokens(D, F32),
            jax.ShapeDtypeStruct((24, D), F32),
            jax.ShapeDtypeStruct((1, FF + D), F32),
            jax.ShapeDtypeStruct((chips, rows, 4 * D), BF16),
            jax.ShapeDtypeStruct((chips, rows, 4 * D), BF16),
        ),
        in_specs=[
            SMEM,
            SMEM,
            per_slot(D),
            per_slot(D),
            per_slot(FF),
            per_slot(FF),
            per_slot(D),
            whole(SLOT, 6 * D),
            whole(D, HALF),
            whole(FF, D),
        ],
        out_specs=(
            per_slot(D),
            whole(24, D),
            whole(1, FF + D),
            whole(chips, rows, 4 * D),
            whole(chips, rows, 4 * D),
        ),
        scratch_shapes=[pltpu.VMEM((D, FF), F32), pltpu.VMEM((FF, D), F32)],
        compiler_params=params_of(1),
        cost_estimate=cost(8 * 10**9, 20 * 2**20),
        name="ffn_backward",
    )(core, counts, upstream, branch, active, slope, middle, mod, right, down)


def attention_kernel(chips, core, d_middle, hidden, qkv, attended, projected, mod, left, right, d_mod_in, bias_in, cond, d_cond_in, d_hidden, d_cond, keep, send, acc, acc_proj, d_mod, bias, *, first):
    step = pl.program_id(0)

    @pl.when(step == 0)
    def _():
        acc[...] = jnp.zeros_like(acc)
        acc_proj[...] = jnp.zeros_like(acc_proj)
        bias[...] = jnp.zeros_like(bias)
        d_mod[...] = d_mod_in[...]

    d_mid = flat(d_middle)
    d_proj = d_mid * mod_part(mod, step, 2)
    put_sums(d_mod, step, 2, d_mid * flat(projected))
    bias[:, 8 * D : 9 * D] += row_sum(d_proj)
    low = d_proj.astype(BF16)
    acc_proj[...] += left_product(flat(attended), low)
    d_heads = right_product(low, right[:, 2 * D : 3 * D]).astype(BF16)
    factor = 1.0 / math.sqrt(HEAD)
    masks, plain = head_masks(factor), head_masks(1.0)
    mixed = []
    for slot in range(STEP):
        rows = slice(slot * SEQ, (slot + 1) * SEQ)
        d_query, d_keys, d_values = [], [], []
        for pair in range(HEADS // 2):
            span = slice(pair * 2 * HEAD, (pair + 1) * 2 * HEAD)
            queries = both_heads(qkv[slot, :, span], masks)
            keys = qkv[slot, :, D + pair * 2 * HEAD : D + (pair + 1) * 2 * HEAD]
            heads_in = qkv[slot, :, 2 * D + pair * 2 * HEAD : 2 * D + (pair + 1) * 2 * HEAD]
            d_pair = both_heads(d_heads[rows, span], plain)
            probs = softmax_keys(right_product(keys, queries))
            d_probs = right_product(heads_in, d_pair)
            d_values.append(dot_nn(probs.astype(BF16), d_pair))
            weighted = probs * d_probs
            d_scores = (weighted - probs * jnp.sum(weighted, axis=0, keepdims=True)).astype(BF16)
            d_keys.append(dot_nn(d_scores, queries))
            d_query.append(merge_heads(left_product(d_scores, keys)) * factor)
        d_query = jnp.concatenate(d_query, axis=1)
        d_values = jnp.concatenate(d_values, axis=1)
        bias[:, 6 * D : 7 * D] += row_sum(d_query)
        bias[:, 7 * D : 8 * D] += row_sum(d_values)
        mixed.append(
            jnp.concatenate(
                [d_query.astype(BF16), jnp.concatenate(d_keys, axis=1).astype(BF16), d_values.astype(BF16)], axis=1
            )
        )
    mixed = mixed[0] if STEP == 1 else jnp.concatenate(mixed, axis=0)
    normed, rstd = norm_stats(flat(hidden).astype(F32))
    scale = mod_part(mod, step, 1)
    shifted = (normed * (1.0 + scale) + mod_part(mod, step, 0)).astype(BF16)
    acc[...] += left_product(shifted, mixed)
    d_normed = right_product(mixed[:, :D], left[:, 6 * D :]) + right_product(mixed[:, D:], right[:, : 2 * D])
    put_sums(d_mod, step, 0, d_normed)
    put_sums(d_mod, step, 1, d_normed * normed)
    d_hidden[...] = (d_mid + norm_backward(d_normed, normed, rstd, scale)).reshape(STEP, SEQ, D)

    @pl.when(step == SLOT // STEP - 1)
    def _():
        rows = D // chips
        bias[:, 9 * D :] = bias_in[...]
        total = d_cond_in[...]
        for part in range(6):
            grads = d_mod[SLOT * part : SLOT * (part + 1), :]
            bias[:, part * D : (part + 1) * D] = row_sum(grads)
            total = total + right_product(grads.astype(BF16), left[:, part * D : (part + 1) * D])
        if first:
            wide_cond = cond[...].astype(F32)
            gate = 1.0 / (1.0 + jnp.exp(-wide_cond))
            total = total * (gate * (1.0 + wide_cond * (1.0 - gate)))
        d_cond[...] = total
        low_mod = d_mod[...].astype(BF16)
        is_odd = core[0] == 1
        for chip in range(chips):
            span = slice(rows * chip, rows * (chip + 1))
            even = acc[span, : 2 * D]
            odd = jnp.concatenate([acc[span, 2 * D :], acc_proj[span, :]], axis=1)
            tails = []
            for half in range(2):
                pieces = []
                for part in range(2):
                    chunk = 4 * chip + 2 * half + part
                    if chunk < BIAS // 128:
                        pieces.append(bias[:, chunk * 128 : (chunk + 1) * 128])
                    else:
                        pieces.append(jnp.zeros((1, 128), F32))
                pieces.append(jnp.zeros((rows - 2, 128), F32))
                tails.append(jnp.concatenate(pieces, axis=0))
            keep[chip, :, : 2 * D] = jnp.where(is_odd, odd, even).astype(BF16)
            send[chip, :, : 2 * D] = jnp.where(is_odd, even, odd).astype(BF16)
            keep[chip, :, 2 * D : 2 * D + 128] = jnp.where(is_odd, tails[1], tails[0]).astype(BF16)
            send[chip, :, 2 * D : 2 * D + 128] = jnp.where(is_odd, tails[0], tails[1]).astype(BF16)
            keep[chip, :, 2 * D + 128 :] = low_mod
            send[chip, :, 2 * D + 128 :] = jnp.zeros_like(low_mod)


def attention_backward(core, d_middle, hidden, record, weights, d_mod, bias, cond, d_cond, chips, first):
    _, mod, qkv, attended, projected, *_ = record
    left, right, _, _ = weights
    rows = D // chips
    return pl.pallas_call(
        functools.partial(attention_kernel, chips, first=first),
        grid=(SLOT // STEP,),
        out_shape=(
            tokens(D, F32),
            jax.ShapeDtypeStruct((SLOT, D), F32),
            jax.ShapeDtypeStruct((chips, rows, 3 * D + 128), BF16),
            jax.ShapeDtypeStruct((chips, rows, 3 * D + 128), BF16),
        ),
        in_specs=[
            SMEM,
            per_slot(D),
            per_slot(D),
            per_slot(3 * D),
            per_slot(D),
            per_slot(D),
            whole(SLOT, 6 * D),
            whole(D, HALF),
            whole(D, HALF),
            whole(24, D),
            whole(1, FF + D),
            whole(SLOT, D),
            whole(SLOT, D),
        ],
        out_specs=(
            per_slot(D),
            whole(SLOT, D),
            whole(chips, rows, 3 * D + 128),
            whole(chips, rows, 3 * D + 128),
        ),
        scratch_shapes=[
            pltpu.VMEM((D, 3 * D), F32),
            pltpu.VMEM((D, D), F32),
            pltpu.VMEM((24, D), F32),
            pltpu.VMEM((1, BIAS), F32),
        ],
        compiler_params=params_of(1),
        cost_estimate=cost(6 * 10**9, 20 * 2**20),
        name="attention_backward",
    )(core, d_middle, hidden, qkv, attended, projected, mod, left, right, d_mod, bias, cond, d_cond)


def finish_kernel(chips, core, own_ffn, own_attn, got_ffn, got_attn, own_mod, got_mod, cond, chip, ada_out, qkv_out, proj_out, fc1_out, fc2_out, bias_out):
    rows = D // (2 * chips)
    is_odd = core[0] == 1
    mine = 2 * chip[0] + core[0]
    take = lax.broadcasted_iota(jnp.int32, (16, D), 0)
    column = lax.broadcasted_iota(jnp.int32, (16, D), 1)
    pick = ((column == rows * mine + take) & (take < rows)).astype(F32).astype(BF16)
    chosen = [right_product(pick, cond[side].astype(BF16)).astype(BF16) for side in range(2)]
    slots = SLOT * chips
    source = lax.broadcasted_iota(jnp.int32, (slots, 24 * chips), 0)
    target = lax.broadcasted_iota(jnp.int32, (slots, 24 * chips), 1)
    places = []
    for part in range(6):
        place = (target == 24 * (source // SLOT) + SLOT * part + source % SLOT).astype(F32).astype(BF16)
        places.append([dot_nn(chosen[side], place).astype(BF16) for side in range(2)])
    for layer in range(2):
        even = jnp.where(is_odd, got_mod[layer], own_mod[layer])
        odd = jnp.where(is_odd, own_mod[layer], got_mod[layer])
        for part in range(6):
            block = dot_nn(places[part][0], even) + dot_nn(places[part][1], odd)
            for row in range(rows):
                start = row * 6 * D + part * D
                ada_out[layer : layer + 1, start : start + D] = block[row : row + 1]
        own = jnp.where(is_odd, own_ffn[layer, rows:, :], own_ffn[layer, :rows, :])
        got = got_ffn[layer]
        first = jnp.where(is_odd, got, own[:, : 2 * D])
        second = jnp.where(is_odd, own[:, : 2 * D], got)
        for row in range(rows):
            fc1_out[layer : layer + 1, row * FF : row * FF + 2 * D] = first[row : row + 1]
            fc1_out[layer : layer + 1, row * FF + 2 * D : (row + 1) * FF] = second[row : row + 1]
        for row in range(4 * rows):
            column_start = (2 + row // (2 * rows)) * D
            fc2_out[layer : layer + 1, row * D : (row + 1) * D] = own_ffn[
                layer, row % (2 * rows) : row % (2 * rows) + 1, column_start : column_start + D
            ]
        own = jnp.where(is_odd, own_attn[layer, rows:, :], own_attn[layer, :rows, :])
        got = got_attn[layer]
        first = jnp.where(is_odd, got, own[:, : 2 * D])
        second = jnp.where(is_odd, own[:, : 2 * D], got)
        for row in range(rows):
            qkv_out[layer : layer + 1, row * 3 * D : row * 3 * D + 2 * D] = first[row : row + 1]
            qkv_out[layer : layer + 1, row * 3 * D + 2 * D : (row + 1) * 3 * D] = second[row : row + 1, :D]
            proj_out[layer : layer + 1, row * D : (row + 1) * D] = second[row : row + 1, D:]
        for part in range(2):
            bias_out[layer : layer + 1, part * 128 : (part + 1) * 128] = own_attn[
                layer, part : part + 1, 2 * D : 2 * D + 128
            ]


def finish(core, chip, own_ffn, own_attn, got_ffn, got_attn, own_mod, got_mod, cond, shapes, chips):
    return pl.pallas_call(
        functools.partial(finish_kernel, chips),
        out_shape=tuple(jax.ShapeDtypeStruct(shape, F32) for shape in shapes),
        in_specs=[SMEM] + [VMEM] * 7 + [SMEM],
        out_specs=(VMEM,) * 6,
        compiler_params=params_of(),
        name="finish",
    )(core, own_ffn, own_attn, got_ffn, got_attn, own_mod, got_mod, cond, chip)


def fast_body(
    latents_in, condition, counts, ada_weight, qkv_weight, proj_weight, fc1_weight, fc2_weight, biases, cotangent
):
    devices = lax.axis_size("fsdp")
    chips = devices // 2
    rows = D // devices
    index = lax.axis_index("fsdp")
    core, chip = (index % 2).reshape(1), (index // 2).reshape(1)
    pairs = [[2 * one, 2 * one + 1] for one in range(chips)]
    across = [[2 * one + side for one in range(chips)] for side in range(2)]
    swap = [(one, one ^ 1) for one in range(devices)]

    lines = [[8 * level + one for level in range(4)] for one in range(8)]
    place = jnp.stack([index % 2, (index // 2) % 4])
    tie = lax.optimization_barrier

    def along(value, bit):
        return lax.ppermute(value, "fsdp", [(one, one ^ bit) for one in range(devices)])

    def stacked(copies):
        return lax.all_to_all(copies, "fsdp", 0, 0, axis_index_groups=lines, tiled=True)

    def with_other_core(held):
        return [*held, *[(along(block, 1), (1, *spot[1:])) for block, spot in held]]

    def planes_of(stack, column):
        return [(stack if step == 0 else along(stack, 2 * step), (0, step, 0, column)) for step in range(4)]

    copies_left, copies_right, copies_last = pack(
        ada_weight, qkv_weight, proj_weight, fc1_weight, fc2_weight, biases, condition, rows, 4
    )
    stack_left, copies_right = tie((stacked(copies_left), copies_right))
    blocks, stack_right, copies_last = tie(
        ([block for block, _ in planes_of(stack_left, 0)], stacked(copies_right), copies_last)
    )
    planes_left = [(block, (0, step, 0, 0)) for step, block in enumerate(blocks)]
    planes_right = planes_of(stack_right, WIRE // 2)
    stack_last = stacked(copies_last)
    held_first = [*with_other_core(planes_left), *with_other_core(planes_right)]
    stack_last, place = tie((stack_last, place))
    *first_weights, cond_all = unpack_wire(place, held_first)
    planes_last = planes_of(stack_last, 0)
    first = forward_block(counts, latents_in, condition, first_weights, False)
    blocks, first = tie(([block for block, _ in planes_last], first))
    held_last = with_other_core([(block, spot) for block, (_, spot) in zip(blocks, planes_last, strict=True)])
    *last_weights, _ = unpack_wire(place, held_last)
    last = forward_block(counts, first[0], condition, last_weights, True)
    weights, records, hidden = [first_weights, last_weights], [first, last], [latents_in, first[0], last[0]]
    upstream = cotangent
    d_cond = jnp.zeros((SLOT, D), F32)
    reduced = [None, None]

    def paired(keep, send):
        got = lax.ppermute(send, "fsdp", swap)
        return (keep.astype(F32) + got.astype(F32)).astype(BF16)

    def exchanged(both):
        return lax.all_to_all(both, "fsdp", 0, 0, axis_index_groups=across, tiled=True)

    def summed(spread):
        return jnp.sum(spread.astype(F32), axis=0)

    d_middle, d_mod, bias, *wire = ffn_backward(core, counts, upstream, records[1], weights[1], chips, True)
    d_middle, both = tie((d_middle, paired(*wire)))
    ffn_last = exchanged(both)
    upstream, d_cond, *wire = attention_backward(
        core, d_middle, hidden[1], records[1], weights[1], d_mod, bias, condition, d_cond, chips, False
    )
    upstream, both, ffn_last = tie((upstream, paired(*wire), ffn_last))
    attn_last = exchanged(both)
    d_middle, d_mod, bias, *wire = ffn_backward(core, counts, upstream, records[0], weights[0], chips, False)
    d_middle, both, attn_last = tie((d_middle, paired(*wire), attn_last))
    ffn_first = exchanged(both)
    upstream, d_cond, *wire = attention_backward(
        core, d_middle, hidden[0], records[0], weights[0], d_mod, bias, condition, d_cond, chips, True
    )
    both, ffn_first = tie((paired(*wire), ffn_first))
    attn_first = exchanged(both)
    width = 2 * D + 128
    for layer, (ffn, attn) in enumerate(((ffn_first, attn_first), (ffn_last, attn_last))):
        reduced[layer] = (summed(ffn), summed(attn[:, :, :width]), attn[:, :, width:].reshape(24 * chips, D))
    own_ffn = jnp.stack([reduced[layer][0] for layer in range(2)])
    own_attn = jnp.stack([reduced[layer][1] for layer in range(2)])
    own_mod = jnp.stack([reduced[layer][2] for layer in range(2)])
    start = (1 - index % 2) * rows
    to_send = jnp.concatenate([own_ffn[:, :, : 2 * D], own_attn[:, :, : 2 * D]], axis=2)
    got = lax.ppermute(lax.dynamic_slice_in_dim(to_send, start, rows, axis=1), "fsdp", swap)
    got_mod = lax.ppermute(own_mod, "fsdp", swap)
    shapes = [array.shape for array in (ada_weight, qkv_weight, proj_weight, fc1_weight, fc2_weight, biases)]
    grads = finish(
        core, chip, own_ffn, own_attn, got[:, :, : 2 * D], got[:, :, 2 * D :], own_mod, got_mod, cond_all, shapes, chips
    )
    return (hidden[2], upstream, d_cond, *grads)


def choose_body(
    latents_in, condition, counts, ada_weight, qkv_weight, proj_weight, fc1_weight, fc2_weight, biases, cotangent
):
    devices = lax.axis_size("fsdp")
    rows = D // devices
    fits = (
        D % devices == 0
        and devices == 32
        and latents_in.shape == (SLOT, SEQ, D)
        and ada_weight.shape == (2, rows * 6 * D)
        and qkv_weight.shape == (2, rows * 3 * D)
        and proj_weight.shape == (2, rows * D)
        and fc1_weight.shape == (2, rows * FF)
        and fc2_weight.shape == (2, rows * FF)
        and biases.shape == (2, 256)
    )
    chosen = fast_body if fits else body
    return chosen(
        latents_in, condition, counts, ada_weight, qkv_weight, proj_weight, fc1_weight, fc2_weight, biases, cotangent
    )


def solution(mesh):
    return jax.shard_map(
        choose_body,
        mesh=mesh,
        in_specs=(
            P("fsdp", None, None),
            P("fsdp", None),
            P("fsdp"),
            P(None, "fsdp"),
            P(None, "fsdp"),
            P(None, "fsdp"),
            P(None, "fsdp"),
            P(None, "fsdp"),
            P(None, "fsdp"),
            P("fsdp", None, None),
        ),
        out_specs=(
            P("fsdp", None, None),
            P("fsdp", None, None),
            P("fsdp", None),
            P(None, "fsdp"),
            P(None, "fsdp"),
            P(None, "fsdp"),
            P(None, "fsdp"),
            P(None, "fsdp"),
            P(None, "fsdp"),
        ),
        check_vma=False,
    )
```

```python
import functools
import math

import jax
import jax.numpy as jnp
from jax import lax
from jax.experimental import pallas as pl
from jax.experimental.pallas import tpu as pltpu
from jax.sharding import PartitionSpec as P

D = 384
HEADS = 6
HEAD = 64
FF = 1536


EPSILON = 1e-06


def modulate_norm(values_in, shift_add, scale_mul):
    centred = values_in - jnp.mean(values_in, axis=-1, keepdims=True)
    variance = jnp.mean(centred * centred, axis=-1, keepdims=True)
    normed = centred * lax.rsqrt(variance + EPSILON)
    return normed * (1.0 + scale_mul[:, None, :]) + shift_add[:, None, :]


def gelu_tanh(values_in):
    return jax.nn.gelu(values_in, approximate=True)


def left_product(left, right):
    return lax.dot_general(
        left, right, (((0,), (0,)), ((), ())), preferred_element_type=jnp.float32
    )


def right_product(left, right):
    return lax.dot_general(
        left, right, (((1,), (1,)), ((), ())), preferred_element_type=jnp.float32
    )


def unpack(gathered):
    ada_flat, qkv_flat, proj_flat, fc1_flat, fc2_flat, bias_flat = gathered
    bias_wide = bias_flat.astype(jnp.float32)
    return (
        ada_flat.reshape(D, 6 * D),
        qkv_flat[: 3 * D * D].reshape(D, 3 * D),
        proj_flat[: D * D].reshape(D, D),
        fc1_flat.reshape(D, FF),
        fc2_flat.reshape(FF, D),
        bias_wide[: 6 * D],
        bias_wide[6 * D : 7 * D],
        bias_wide[7 * D : 8 * D],
        bias_wide[8 * D : 9 * D],
        bias_wide[9 * D : 9 * D + FF],
        bias_wide[9 * D + FF : 10 * D + FF],
    )


def split_modulation(modulation):
    return [modulation[:, part_index * D : (part_index + 1) * D] for part_index in range(6)]


def layer_forward(hidden, cond_act, params):
    w_ada, w_qkv, w_proj, w_fc1, w_fc2, b_ada, b_query, b_value, b_proj, b_fc1, b_fc2 = params
    slot_count, seq_len = (hidden.shape[0], hidden.shape[1])
    modulation = jnp.dot(cond_act, w_ada, preferred_element_type=jnp.float32) + b_ada
    shift_attn, scale_attn, gate_attn, shift_ffn, scale_ffn, gate_ffn = split_modulation(modulation)
    normed_attn = modulate_norm(hidden, shift_attn, scale_attn).astype(jnp.bfloat16).reshape(-1, D)
    mixed_qkv = jnp.dot(normed_attn, w_qkv, preferred_element_type=jnp.float32)
    queries = (
        (mixed_qkv[:, 0:D] + b_query).astype(jnp.bfloat16).reshape(slot_count, seq_len, HEADS, HEAD)
    )
    key_heads = (
        mixed_qkv[:, D : 2 * D].astype(jnp.bfloat16).reshape(slot_count, seq_len, HEADS, HEAD)
    )
    value_heads = (
        (mixed_qkv[:, 2 * D : 3 * D] + b_value)
        .astype(jnp.bfloat16)
        .reshape(slot_count, seq_len, HEADS, HEAD)
    )
    scores = jnp.einsum(
        "bqhd,bkhd->bhqk", queries, key_heads, preferred_element_type=jnp.float32
    ) * (1.0 / math.sqrt(HEAD))
    peak_score = jnp.max(scores, axis=-1, keepdims=True)
    exp_scores = jnp.exp(scores - peak_score)
    exp_total = jnp.sum(exp_scores, axis=-1, keepdims=True)
    logsum = peak_score + jnp.log(exp_total)
    attn_probs = (exp_scores / exp_total).astype(jnp.bfloat16)
    attended = jnp.einsum(
        "bhqk,bkhd->bqhd", attn_probs, value_heads, preferred_element_type=jnp.float32
    )
    attended = attended.astype(jnp.bfloat16).reshape(-1, D)
    projected = (jnp.dot(attended, w_proj, preferred_element_type=jnp.float32) + b_proj).reshape(
        slot_count, seq_len, D
    )
    middle = hidden + gate_attn[:, None, :] * projected
    normed_ffn = modulate_norm(middle, shift_ffn, scale_ffn).astype(jnp.bfloat16).reshape(-1, D)
    pre_act = jnp.dot(normed_ffn, w_fc1, preferred_element_type=jnp.float32) + b_fc1
    activation = gelu_tanh(pre_act).astype(jnp.bfloat16)
    branch = (jnp.dot(activation, w_fc2, preferred_element_type=jnp.float32) + b_fc2).reshape(
        slot_count, seq_len, D
    )
    result = middle + gate_ffn[:, None, :] * branch
    record = (
        hidden,
        modulation,
        normed_attn,
        queries,
        key_heads,
        value_heads,
        logsum,
        attended,
        projected,
        middle,
        normed_ffn,
        pre_act,
        activation,
        branch,
    )
    return (result, record)


def layer_backward(upstream, params, record):
    w_ada, w_qkv, w_proj, w_fc1, w_fc2, b_ada, b_query, b_value, b_proj, b_fc1, b_fc2 = params
    (
        hidden,
        modulation,
        normed_attn,
        queries,
        key_heads,
        value_heads,
        logsum,
        attended,
        projected,
        middle,
        normed_ffn,
        pre_act,
        activation,
        branch,
    ) = record
    slot_count, seq_len = (hidden.shape[0], hidden.shape[1])
    shift_attn, scale_attn, gate_attn, shift_ffn, scale_ffn, gate_ffn = split_modulation(modulation)
    d_branch = (upstream * gate_ffn[:, None, :]).reshape(-1, D)
    d_gate_ffn = jnp.sum(upstream * branch, axis=1)
    grad_b_fc2 = jnp.sum(d_branch, axis=0)
    branch_low = d_branch.astype(jnp.bfloat16)
    grad_w_fc2 = left_product(activation, branch_low)
    d_act = right_product(branch_low, w_fc2)
    gelu_out, gelu_pull = jax.vjp(gelu_tanh, pre_act)
    (d_pre,) = gelu_pull(d_act)
    grad_b_fc1 = jnp.sum(d_pre, axis=0)
    pre_low = d_pre.astype(jnp.bfloat16)
    grad_w_fc1 = left_product(normed_ffn, pre_low)
    d_normed_ffn = right_product(pre_low, w_fc1).reshape(slot_count, seq_len, D)
    norm_out, norm_pull = jax.vjp(modulate_norm, middle, shift_ffn, scale_ffn)
    middle_part, d_shift_ffn, d_scale_ffn = norm_pull(d_normed_ffn)
    d_middle = upstream + middle_part
    d_proj = (d_middle * gate_attn[:, None, :]).reshape(-1, D)
    d_gate_attn = jnp.sum(d_middle * projected, axis=1)
    grad_b_proj = jnp.sum(d_proj, axis=0)
    proj_low = d_proj.astype(jnp.bfloat16)
    grad_w_proj = left_product(attended, proj_low)
    d_attended = (
        right_product(proj_low, w_proj)
        .astype(jnp.bfloat16)
        .reshape(slot_count, seq_len, HEADS, HEAD)
    )
    scores = jnp.einsum(
        "bqhd,bkhd->bhqk", queries, key_heads, preferred_element_type=jnp.float32
    ) * (1.0 / math.sqrt(HEAD))
    attn_probs = jnp.exp(scores - logsum)
    d_probs = jnp.einsum(
        "bqhd,bkhd->bhqk", d_attended, value_heads, preferred_element_type=jnp.float32
    )
    d_values = jnp.einsum(
        "bhqk,bqhd->bkhd",
        attn_probs.astype(jnp.bfloat16),
        d_attended,
        preferred_element_type=jnp.float32,
    )
    row_inner = jnp.sum(attn_probs * d_probs, axis=-1, keepdims=True)
    d_scores = (attn_probs * (d_probs - row_inner) * (1.0 / math.sqrt(HEAD))).astype(jnp.bfloat16)
    d_query = jnp.einsum(
        "bhqk,bkhd->bqhd", d_scores, key_heads, preferred_element_type=jnp.float32
    ).reshape(-1, D)
    d_keys = jnp.einsum(
        "bhqk,bqhd->bkhd", d_scores, queries, preferred_element_type=jnp.float32
    ).reshape(-1, D)
    d_values = d_values.reshape(-1, D)
    grad_b_query = jnp.sum(d_query, axis=0)
    grad_b_value = jnp.sum(d_values, axis=0)
    mixed_low = jnp.concatenate([d_query, d_keys, d_values], axis=1).astype(jnp.bfloat16)
    grad_w_qkv = left_product(normed_attn, mixed_low)
    d_normed_attn = right_product(mixed_low, w_qkv).reshape(slot_count, seq_len, D)
    attn_out, attn_pull = jax.vjp(modulate_norm, hidden, shift_attn, scale_attn)
    hidden_part, d_shift_attn, d_scale_attn = attn_pull(d_normed_attn)
    d_hidden = d_middle + hidden_part
    d_mod = jnp.concatenate(
        [d_shift_attn, d_scale_attn, d_gate_attn, d_shift_ffn, d_scale_ffn, d_gate_ffn], axis=1
    )
    grad_b_ada = jnp.sum(d_mod, axis=0)
    mod_low = d_mod.astype(jnp.bfloat16)
    d_cond = right_product(mod_low, w_ada)
    grad_bias = jnp.concatenate(
        [grad_b_ada, grad_b_query, grad_b_value, grad_b_proj, grad_b_fc1, grad_b_fc2]
    )
    return (d_hidden, d_cond, mod_low, (grad_w_qkv, grad_w_proj, grad_w_fc1, grad_w_fc2, grad_bias))


def pad_flat(values_in, length):
    flat = values_in.reshape(-1)
    return jnp.pad(flat, (0, length - flat.shape[0]))


def body(
    latents_in,
    condition,
    counts,
    ada_weight,
    qkv_weight,
    proj_weight,
    fc1_weight,
    fc2_weight,
    biases,
    cotangent,
):
    slot_count = latents_in.shape[0]
    layer_total = ada_weight.shape[0]
    device_count = lax.axis_size("fsdp")
    rest_list = (qkv_weight, proj_weight, fc1_weight, fc2_weight, biases)
    rest_lengths = [piece.shape[1] * device_count for piece in rest_list]
    ada_shard = ada_weight.shape[1]
    occupied = (jnp.arange(slot_count) < counts[0]).astype(jnp.float32)
    cond_wide = condition.astype(jnp.float32)
    silu_out, silu_pull = jax.vjp(jax.nn.silu, cond_wide)
    cond_act = silu_out.astype(jnp.bfloat16)
    hidden = latents_in.astype(jnp.float32)
    records = []
    for layer_index in range(layer_total):
        gathered = (
            lax.all_gather(ada_weight[layer_index], "fsdp", axis=0, tiled=True),
            lax.all_gather(qkv_weight[layer_index], "fsdp", axis=0, tiled=True),
            lax.all_gather(proj_weight[layer_index], "fsdp", axis=0, tiled=True),
            lax.all_gather(fc1_weight[layer_index], "fsdp", axis=0, tiled=True),
            lax.all_gather(fc2_weight[layer_index], "fsdp", axis=0, tiled=True),
            lax.all_gather(biases[layer_index], "fsdp", axis=0, tiled=True),
        )
        params = unpack(gathered)
        hidden, record = layer_forward(hidden, cond_act, params)
        records.append(record)
    latents_out = hidden * occupied[:, None, None]
    upstream = cotangent.astype(jnp.float32) * occupied[:, None, None]
    cond_total = jnp.zeros(cond_wide.shape, jnp.float32)
    layer_sums = [None] * layer_total
    mod_lows = [None] * layer_total
    for layer_index in reversed(range(layer_total)):
        gathered = (
            lax.all_gather(ada_weight[layer_index], "fsdp", axis=0, tiled=True),
            lax.all_gather(qkv_weight[layer_index], "fsdp", axis=0, tiled=True),
            lax.all_gather(proj_weight[layer_index], "fsdp", axis=0, tiled=True),
            lax.all_gather(fc1_weight[layer_index], "fsdp", axis=0, tiled=True),
            lax.all_gather(fc2_weight[layer_index], "fsdp", axis=0, tiled=True),
            lax.all_gather(biases[layer_index], "fsdp", axis=0, tiled=True),
        )
        params = unpack(gathered)
        upstream, d_cond, mod_low, grad_parts = layer_backward(
            upstream, params, records[layer_index]
        )
        mod_lows[layer_index] = mod_low
        cond_total = cond_total + d_cond
        padded = [
            pad_flat(grad_parts[part_index], rest_lengths[part_index]) for part_index in range(5)
        ]
        layer_sums[layer_index] = (
            lax.psum_scatter(padded[0], "fsdp", scatter_dimension=0, tiled=True),
            lax.psum_scatter(padded[1], "fsdp", scatter_dimension=0, tiled=True),
            lax.psum_scatter(padded[2], "fsdp", scatter_dimension=0, tiled=True),
            lax.psum_scatter(padded[3], "fsdp", scatter_dimension=0, tiled=True),
            lax.psum_scatter(padded[4], "fsdp", scatter_dimension=0, tiled=True),
        )
    grad_rest = [
        jnp.stack([layer_sums[layer_index][part_index] for layer_index in range(layer_total)])
        for part_index in range(5)
    ]
    mod_joined = jnp.concatenate(mod_lows, axis=1)
    ada_full = left_product(
        lax.all_gather(cond_act, "fsdp", axis=0, tiled=True),
        lax.all_gather(mod_joined, "fsdp", axis=0, tiled=True),
    )
    own_start = lax.axis_index("fsdp") * ada_shard
    ada_rows = []
    for layer_index in range(layer_total):
        flat_layer = pad_flat(
            ada_full[:, layer_index * 6 * D : (layer_index + 1) * 6 * D], ada_shard * device_count
        )
        ada_rows.append(lax.dynamic_slice_in_dim(flat_layer, own_start, ada_shard))
    ada_grad = jnp.stack(ada_rows)
    (condition_grad,) = silu_pull(cond_total)
    return (
        latents_out,
        upstream,
        condition_grad,
        ada_grad,
        grad_rest[0],
        grad_rest[1],
        grad_rest[2],
        grad_rest[3],
        grad_rest[4],
    )


BF16 = jnp.bfloat16
F32 = jnp.float32
SLOT = 4
STEP = 1
CHUNK = 512
SEQ = 256
HALF = 7 * D
WIRE = HALF + 2 * D + 128
BIAS = 10 * D + FF
VMEM = pl.BlockSpec(memory_space=pltpu.VMEM)
SMEM = pl.BlockSpec(memory_space=pltpu.SMEM)


def params_of(grid_rank=0, megabytes=36):
    semantics = ("arbitrary",) * grid_rank if grid_rank else None
    return pltpu.CompilerParams(vmem_limit_bytes=megabytes * 2**20, dimension_semantics=semantics)


def dot_nn(left, right):
    return lax.dot_general(
        left, right, (((1,), (0,)), ((), ())), preferred_element_type=jnp.float32
    )


def pack_kernel(rows, ada_in, qkv_in, proj_in, fc1_in, fc2_in, bias_in, cond, out_left, out_right, out_last, ada, qkv, proj, fc1, fc2, bias, sems, wide):
    copies = [
        pltpu.make_async_copy(source, target, sems.at[place])
        for place, (source, target) in enumerate(
            ((ada_in, ada), (qkv_in, qkv), (proj_in, proj), (fc1_in, fc1), (fc2_in, fc2), (bias_in, bias))
        )
    ]
    for copy in copies:
        copy.start()
    wide[:, :, WIRE - 128 :] = jnp.zeros((2, 2 * rows, 128), F32)
    wide_cond = cond[...].astype(F32)
    act = (wide_cond / (1.0 + jnp.exp(-wide_cond))).astype(BF16).astype(F32)
    for part in range(3):
        wide[0, 8 + 4 * part : 12 + 4 * part, WIRE - 128 :] = act[:, part * 128 : part * 128 + 128]
    for copy in copies:
        copy.wait()

    def put(source, start, width, row, column):
        values = source[:, start : start + width].astype(F32)
        for layer in range(2):
            wide[layer, row : row + 1, column : column + width] = values[layer : layer + 1]

    for row in range(rows):
        put(ada, row * 6 * D, 6 * D, row, 0)
        put(qkv, row * 3 * D, D, row, 6 * D)
        put(qkv, row * 3 * D + D, 2 * D, rows + row, 0)
        put(proj, row * D, D, rows + row, 2 * D)
        put(fc1, row * FF, FF, rows + row, 3 * D)
    for row in range(4 * rows):
        put(fc2, row * D, D, row % (2 * rows), HALF + D * (row // (2 * rows)))
    put(bias, 0, 128, 0, WIRE - 128)
    put(bias, 128, 128, 1, WIRE - 128)
    low = wide[0].astype(BF16)
    low_last = wide[1].astype(BF16)
    for copy_index in range(out_last.shape[0]):
        out_left[copy_index] = low[:, : WIRE // 2]
        out_right[copy_index] = low[:, WIRE // 2 :]
        out_last[copy_index] = low_last


def pack(ada, qkv, proj, fc1, fc2, bias, cond, rows, copies):
    flat = (ada, qkv, proj, fc1, fc2, bias)
    return pl.pallas_call(
        functools.partial(pack_kernel, rows),
        out_shape=tuple(
            jax.ShapeDtypeStruct((copies, 2 * rows, width), BF16) for width in (WIRE // 2, WIRE // 2, WIRE)
        ),
        in_specs=[pl.BlockSpec(memory_space=pltpu.HBM)] * 6 + [VMEM],
        out_specs=(VMEM,) * 3,
        scratch_shapes=[pltpu.VMEM(array.shape, BF16) for array in flat]
        + [pltpu.SemaphoreType.DMA((6,)), pltpu.VMEM((2, 2 * rows, WIRE), F32)],
        compiler_params=params_of(0, 62),
        name="pack",
    )(*flat, cond)


def unpack_kernel(rows, spots, place, *refs):
    blocks, (left, right, down, bias, cond, wire, sems) = refs[:-7], refs[-7:]
    copies = []
    for number, (block, (side, step, level, column)) in enumerate(zip(blocks, spots, strict=True)):
        target = wire.at[
            (place[0] + side) % 2,
            place[1] ^ step,
            pl.ds(level, block.shape[0]),
            :,
            pl.ds(column, block.shape[2]),
        ]
        copies.append(pltpu.make_async_copy(block, target, sems.at[number]))
    for copy in copies:
        copy.start()
    for copy in copies:
        copy.wait()

    def of(device):
        return wire.at[device % 2, (device // 2) % 4, device // 8]

    for group in range(8):
        for half, target in ((0, left), (1, right)):
            target[4 * rows * group : 4 * rows * (group + 1), :] = jnp.concatenate(
                [of(4 * group + member)[half * rows : (half + 1) * rows, :HALF] for member in range(4)], axis=0
            )
    for device in range(32):
        for part in range(2):
            start = 4 * rows * device + 2 * rows * part
            column = HALF + D * part
            down[start : start + 2 * rows, :] = of(device)[:, column : column + D]
        tail = of(device)[:, WIRE - 128 :].astype(F32)
        for part in range(2):
            chunk = 2 * device + part
            if chunk < BIAS // 128:
                bias[0:1, chunk * 128 : chunk * 128 + 128] = tail[part : part + 1]
        for part in range(3):
            cond[device % 2, 4 * (device // 2) : 4 * (device // 2) + 4, part * 128 : part * 128 + 128] = tail[
                8 + 4 * part : 12 + 4 * part
            ]


def unpack_wire(place, held):
    blocks, spots = [block for block, _ in held], [spot for _, spot in held]
    rows = blocks[0].shape[1] // 2
    return pl.pallas_call(
        functools.partial(unpack_kernel, rows, spots),
        out_shape=(
            jax.ShapeDtypeStruct((D, HALF), BF16),
            jax.ShapeDtypeStruct((D, HALF), BF16),
            jax.ShapeDtypeStruct((FF, D), BF16),
            jax.ShapeDtypeStruct((1, BIAS), F32),
            jax.ShapeDtypeStruct((2, SLOT * 16, D), F32),
        ),
        in_specs=[SMEM] + [pl.BlockSpec(memory_space=pl.ANY)] * len(blocks),
        out_specs=(VMEM,) * 5,
        scratch_shapes=[pltpu.VMEM((2, 4, 4, 2 * rows, WIRE), BF16), pltpu.SemaphoreType.DMA((len(blocks),))],
        compiler_params=params_of(0, 24),
        name="unpack",
    )(place, *blocks)


def norm_stats(values):
    centred = values - jnp.mean(values, axis=-1, keepdims=True)
    rstd = lax.rsqrt(jnp.mean(centred * centred, axis=-1, keepdims=True) + EPSILON)
    return centred * rstd, rstd


def mod_part(mod, step, part):
    rows = [
        jnp.broadcast_to(mod[pl.ds(STEP * step + slot, 1), part * D : (part + 1) * D], (SEQ, D))
        for slot in range(STEP)
    ]
    return rows[0] if STEP == 1 else jnp.concatenate(rows, axis=0)


def put_sums(d_mod, step, part, values):
    for slot in range(STEP):
        d_mod[pl.ds(SLOT * part + STEP * step + slot, 1), :] = row_sum(values[slot * SEQ : (slot + 1) * SEQ])


def occupied(counts, step):
    rows = [
        jnp.full((SEQ, 1), jnp.where(STEP * step + slot < counts[0], 1.0, 0.0), F32) for slot in range(STEP)
    ]
    return rows[0] if STEP == 1 else jnp.concatenate(rows, axis=0)


def flat(ref):
    return ref[...].reshape(STEP * SEQ, ref.shape[2])


def gelu_and_slope(pre):
    factor, cubic = 0.7978845608028654, 0.044715
    square = pre * pre
    half = 0.5 + 0.5 * jnp.tanh(pre * (factor + (factor * cubic) * square))
    act = pre * half
    return act, half + act * (1.0 - half) * (2.0 * factor + (6.0 * factor * cubic) * square)


def row_sum(values):
    return jnp.sum(values, axis=0, keepdims=True)


def head_masks(factor):
    lane = lax.broadcasted_iota(jnp.int32, (1, 2 * HEAD), 1)
    first = jnp.where(lane < HEAD, factor, 0.0).astype(BF16)
    second = jnp.where(lane < HEAD, 0.0, factor).astype(BF16)
    return first, second


def both_heads(pair, masks):
    return jnp.concatenate([pair * masks[0], pair * masks[1]], axis=0)


def merge_heads(stack):
    lane = lax.broadcasted_iota(jnp.int32, (SEQ, 2 * HEAD), 1)
    return jnp.where(lane < HEAD, stack[:SEQ], stack[SEQ:])


def softmax_keys(scores):
    raised = jnp.exp(scores - jnp.max(scores, axis=0, keepdims=True))
    return raised * (1.0 / jnp.sum(raised, axis=0, keepdims=True))


def forward_kernel(counts, hidden, cond, left, right, down, bias, out, mod, qkv, attended, projected, middle, active, slope, branch, *, last):
    step = pl.program_id(0)

    @pl.when(step == 0)
    def _():
        wide_cond = cond[...].astype(F32)
        act = (wide_cond / (1.0 + jnp.exp(-wide_cond))).astype(BF16)
        mod[...] = dot_nn(act, left[:, : 6 * D]) + bias[:, : 6 * D]

    values = flat(hidden).astype(F32)
    normed, _ = norm_stats(values)
    normed = (normed * (1.0 + mod_part(mod, step, 1)) + mod_part(mod, step, 0)).astype(BF16)
    queries = (dot_nn(normed, left[:, 6 * D :]) + bias[:, 6 * D : 7 * D]).astype(BF16)
    mixed = dot_nn(normed, right[:, : 2 * D])
    keys = mixed[:, :D].astype(BF16)
    heads_in = (mixed[:, D:] + bias[:, 7 * D : 8 * D]).astype(BF16)
    qkv[:, :, :D] = queries.reshape(STEP, SEQ, D)
    qkv[:, :, D : 2 * D] = keys.reshape(STEP, SEQ, D)
    qkv[:, :, 2 * D :] = heads_in.reshape(STEP, SEQ, D)
    masks = head_masks(1.0 / math.sqrt(HEAD))
    joined = []
    for slot in range(STEP):
        rows = slice(slot * SEQ, (slot + 1) * SEQ)
        pairs = []
        for pair in range(HEADS // 2):
            span = slice(pair * 2 * HEAD, (pair + 1) * 2 * HEAD)
            probs = softmax_keys(right_product(keys[rows, span], both_heads(queries[rows, span], masks)))
            pairs.append(merge_heads(left_product(probs.astype(BF16), heads_in[rows, span])).astype(BF16))
        joined.append(jnp.concatenate(pairs, axis=1))
    joined = joined[0] if STEP == 1 else jnp.concatenate(joined, axis=0)
    attended[...] = joined.reshape(STEP, SEQ, D)
    proj = dot_nn(joined, right[:, 2 * D : 3 * D]) + bias[:, 8 * D : 9 * D]
    projected[...] = proj.reshape(STEP, SEQ, D)
    mid = values + mod_part(mod, step, 2) * proj
    middle[...] = mid.reshape(STEP, SEQ, D)
    normed, _ = norm_stats(mid)
    normed = (normed * (1.0 + mod_part(mod, step, 4)) + mod_part(mod, step, 3)).astype(BF16)
    ffn = bias[:, 9 * D + FF :]
    for start in range(0, FF, CHUNK):
        stop = start + CHUNK
        pre = dot_nn(normed, right[:, 3 * D + start : 3 * D + stop]) + bias[:, 9 * D + start : 9 * D + stop]
        act, rate = gelu_and_slope(pre)
        act = act.astype(BF16)
        active[:, :, start:stop] = act.reshape(STEP, SEQ, CHUNK)
        slope[:, :, start:stop] = rate.reshape(STEP, SEQ, CHUNK)
        ffn = ffn + dot_nn(act, down[start:stop, :])
    branch[...] = ffn.reshape(STEP, SEQ, D)
    result = mid + mod_part(mod, step, 5) * ffn
    if last:
        result = result * occupied(counts, step)
    out[...] = result.reshape(STEP, SEQ, D)


def per_slot(width):
    return pl.BlockSpec((STEP, SEQ, width), lambda step: (step, 0, 0))


def whole(*shape):
    return pl.BlockSpec(shape, lambda step: (0,) * len(shape))


def tokens(width, dtype):
    return jax.ShapeDtypeStruct((SLOT, SEQ, width), dtype)


def cost(flops, moved):
    return pl.CostEstimate(flops=flops, bytes_accessed=moved, transcendentals=0)


def forward_block(counts, hidden, cond, weights, last):
    left, right, down, bias = weights
    return pl.pallas_call(
        functools.partial(forward_kernel, last=last),
        grid=(SLOT // STEP,),
        out_shape=(
            tokens(D, F32),
            jax.ShapeDtypeStruct((SLOT, 6 * D), F32),
            tokens(3 * D, BF16),
            tokens(D, BF16),
            tokens(D, F32),
            tokens(D, F32),
            tokens(FF, BF16),
            tokens(FF, F32),
            tokens(D, F32),
        ),
        in_specs=[
            SMEM,
            per_slot(D),
            whole(SLOT, D),
            whole(D, HALF),
            whole(D, HALF),
            whole(FF, D),
            whole(1, BIAS),
        ],
        out_specs=(
            per_slot(D),
            whole(SLOT, 6 * D),
            per_slot(3 * D),
            per_slot(D),
            per_slot(D),
            per_slot(D),
            per_slot(FF),
            per_slot(FF),
            per_slot(D),
        ),
        compiler_params=params_of(1),
        cost_estimate=cost(5 * 10**9, 20 * 2**20),
        name="forward_block",
    )(counts, hidden, cond, left, right, down, bias)


def norm_backward(d_normed, normed, rstd, scale):
    inner = d_normed * (1.0 + scale)
    along = jnp.mean(inner * normed, axis=-1, keepdims=True)
    return rstd * (inner - jnp.mean(inner, axis=-1, keepdims=True) - normed * along)


def offsets(place, chip):
    return (chip // 4 + 4 - place[2]) % 4, place[1] ^ (chip % 4)


def ffn_kernel(chips, core, counts, upstream, branch, active, slope, middle, mod, right, down, d_middle, d_mod, bias, keep, send, acc_up, acc_down, *, last):
    step = pl.program_id(0)

    @pl.when(step == 0)
    def _():
        acc_up[...] = jnp.zeros_like(acc_up)
        acc_down[...] = jnp.zeros_like(acc_down)
        bias[...] = jnp.zeros_like(bias)
        d_mod[...] = jnp.zeros_like(d_mod)

    up = flat(upstream).astype(F32)
    if last:
        up = up * occupied(counts, step)
    d_branch = up * mod_part(mod, step, 5)
    put_sums(d_mod, step, 5, up * flat(branch))
    bias[:, FF:] += row_sum(d_branch)
    low = d_branch.astype(BF16)
    normed, rstd = norm_stats(flat(middle))
    scale = mod_part(mod, step, 4)
    shifted = (normed * (1.0 + scale) + mod_part(mod, step, 3)).astype(BF16)
    d_normed = 0.0
    for start in range(0, FF, CHUNK):
        stop = start + CHUNK
        d_pre = right_product(low, down[start:stop, :]) * slope[:, :, start:stop].reshape(STEP * SEQ, CHUNK)
        acc_down[start:stop, :] += left_product(active[:, :, start:stop].reshape(STEP * SEQ, CHUNK), low)
        bias[:, start:stop] += row_sum(d_pre)
        low_pre = d_pre.astype(BF16)
        acc_up[:, start:stop] += left_product(shifted, low_pre)
        d_normed = d_normed + right_product(low_pre, right[:, 3 * D + start : 3 * D + stop])
    put_sums(d_mod, step, 3, d_normed)
    put_sums(d_mod, step, 4, d_normed * normed)
    d_middle[...] = (up + norm_backward(d_normed, normed, rstd, scale)).reshape(STEP, SEQ, D)

    @pl.when(step == SLOT // STEP - 1)
    def _():
        rows = D // chips
        is_odd = core[0] == 1
        for chip in range(chips):
            span = slice(rows * chip, rows * (chip + 1))
            step_z, step_plane = offsets(core, chip)
            even, odd = acc_up[span, : 2 * D], acc_up[span, 2 * D :]
            keep[step_plane, step_z, :, : 2 * D] = jnp.where(is_odd, odd, even).astype(BF16)
            send[step_plane, step_z, :, : 2 * D] = jnp.where(is_odd, even, odd).astype(BF16)
            for part in range(2):
                start = rows * (4 * chip + part)
                even = acc_down[start : start + rows, :]
                odd = acc_down[start + 2 * rows : start + 3 * rows, :]
                columns = slice((2 + part) * D, (3 + part) * D)
                keep[step_plane, step_z, :, columns] = jnp.where(is_odd, odd, even).astype(BF16)
                send[step_plane, step_z, :, columns] = jnp.where(is_odd, even, odd).astype(BF16)


def ffn_backward(core, counts, upstream, record, weights, chips, last):
    _, mod, _, _, _, middle, active, slope, branch = record
    _, right, down, _ = weights
    rows = D // chips
    return pl.pallas_call(
        functools.partial(ffn_kernel, chips, last=last),
        grid=(SLOT // STEP,),
        out_shape=(
            tokens(D, F32),
            jax.ShapeDtypeStruct((24, D), F32),
            jax.ShapeDtypeStruct((1, FF + D), F32),
            jax.ShapeDtypeStruct((4, 4, rows, 4 * D), BF16),
            jax.ShapeDtypeStruct((4, 4, rows, 4 * D), BF16),
        ),
        in_specs=[
            SMEM,
            SMEM,
            per_slot(D),
            per_slot(D),
            per_slot(FF),
            per_slot(FF),
            per_slot(D),
            whole(SLOT, 6 * D),
            whole(D, HALF),
            whole(FF, D),
        ],
        out_specs=(
            per_slot(D),
            whole(24, D),
            whole(1, FF + D),
            whole(4, 4, rows, 4 * D),
            whole(4, 4, rows, 4 * D),
        ),
        scratch_shapes=[pltpu.VMEM((D, FF), F32), pltpu.VMEM((FF, D), F32)],
        compiler_params=params_of(1),
        cost_estimate=cost(8 * 10**9, 20 * 2**20),
        name="ffn_backward",
    )(core, counts, upstream, branch, active, slope, middle, mod, right, down)


def attention_kernel(chips, core, d_middle, hidden, qkv, attended, projected, mod, left, right, d_mod_in, bias_in, cond, d_cond_in, d_hidden, d_cond, keep, send, acc, acc_proj, d_mod, bias, *, first):
    step = pl.program_id(0)

    @pl.when(step == 0)
    def _():
        acc[...] = jnp.zeros_like(acc)
        acc_proj[...] = jnp.zeros_like(acc_proj)
        bias[...] = jnp.zeros_like(bias)
        d_mod[...] = d_mod_in[...]

    d_mid = flat(d_middle)
    d_proj = d_mid * mod_part(mod, step, 2)
    put_sums(d_mod, step, 2, d_mid * flat(projected))
    bias[:, 8 * D : 9 * D] += row_sum(d_proj)
    low = d_proj.astype(BF16)
    acc_proj[...] += left_product(flat(attended), low)
    d_heads = right_product(low, right[:, 2 * D : 3 * D]).astype(BF16)
    factor = 1.0 / math.sqrt(HEAD)
    masks, plain = head_masks(factor), head_masks(1.0)
    mixed = []
    for slot in range(STEP):
        rows = slice(slot * SEQ, (slot + 1) * SEQ)
        d_query, d_keys, d_values = [], [], []
        for pair in range(HEADS // 2):
            span = slice(pair * 2 * HEAD, (pair + 1) * 2 * HEAD)
            queries = both_heads(qkv[slot, :, span], masks)
            keys = qkv[slot, :, D + pair * 2 * HEAD : D + (pair + 1) * 2 * HEAD]
            heads_in = qkv[slot, :, 2 * D + pair * 2 * HEAD : 2 * D + (pair + 1) * 2 * HEAD]
            d_pair = both_heads(d_heads[rows, span], plain)
            probs = softmax_keys(right_product(keys, queries))
            d_probs = right_product(heads_in, d_pair)
            d_values.append(dot_nn(probs.astype(BF16), d_pair))
            weighted = probs * d_probs
            d_scores = (weighted - probs * jnp.sum(weighted, axis=0, keepdims=True)).astype(BF16)
            d_keys.append(dot_nn(d_scores, queries))
            d_query.append(merge_heads(left_product(d_scores, keys)) * factor)
        d_query = jnp.concatenate(d_query, axis=1)
        d_values = jnp.concatenate(d_values, axis=1)
        bias[:, 6 * D : 7 * D] += row_sum(d_query)
        bias[:, 7 * D : 8 * D] += row_sum(d_values)
        mixed.append(
            jnp.concatenate(
                [d_query.astype(BF16), jnp.concatenate(d_keys, axis=1).astype(BF16), d_values.astype(BF16)], axis=1
            )
        )
    mixed = mixed[0] if STEP == 1 else jnp.concatenate(mixed, axis=0)
    normed, rstd = norm_stats(flat(hidden).astype(F32))
    scale = mod_part(mod, step, 1)
    shifted = (normed * (1.0 + scale) + mod_part(mod, step, 0)).astype(BF16)
    acc[...] += left_product(shifted, mixed)
    d_normed = right_product(mixed[:, :D], left[:, 6 * D :]) + right_product(mixed[:, D:], right[:, : 2 * D])
    put_sums(d_mod, step, 0, d_normed)
    put_sums(d_mod, step, 1, d_normed * normed)
    d_hidden[...] = (d_mid + norm_backward(d_normed, normed, rstd, scale)).reshape(STEP, SEQ, D)

    @pl.when(step == SLOT // STEP - 1)
    def _():
        rows = D // chips
        bias[:, 9 * D :] = bias_in[...]
        total = d_cond_in[...]
        for part in range(6):
            grads = d_mod[SLOT * part : SLOT * (part + 1), :]
            bias[:, part * D : (part + 1) * D] = row_sum(grads)
            total = total + right_product(grads.astype(BF16), left[:, part * D : (part + 1) * D])
        if first:
            wide_cond = cond[...].astype(F32)
            gate = 1.0 / (1.0 + jnp.exp(-wide_cond))
            total = total * (gate * (1.0 + wide_cond * (1.0 - gate)))
        d_cond[...] = total
        low_mod = d_mod[...].astype(BF16)
        is_odd = core[0] == 1
        for chip in range(chips):
            span = slice(rows * chip, rows * (chip + 1))
            even = acc[span, : 2 * D]
            odd = jnp.concatenate([acc[span, 2 * D :], acc_proj[span, :]], axis=1)
            tails = []
            for half in range(2):
                pieces = []
                for part in range(2):
                    chunk = 4 * chip + 2 * half + part
                    if chunk < BIAS // 128:
                        pieces.append(bias[:, chunk * 128 : (chunk + 1) * 128])
                    else:
                        pieces.append(jnp.zeros((1, 128), F32))
                pieces.append(jnp.zeros((rows - 2, 128), F32))
                tails.append(jnp.concatenate(pieces, axis=0))
            step_z, step_plane = offsets(core, chip)
            keep[step_plane, step_z, :, : 2 * D] = jnp.where(is_odd, odd, even).astype(BF16)
            send[step_plane, step_z, :, : 2 * D] = jnp.where(is_odd, even, odd).astype(BF16)
            keep[step_plane, step_z, :, 2 * D :] = jnp.where(is_odd, tails[1], tails[0]).astype(BF16)
            send[step_plane, step_z, :, 2 * D :] = jnp.where(is_odd, tails[0], tails[1]).astype(BF16)
        for step_plane in range(4):
            keep[step_plane, 4, :, :D] = low_mod
            keep[step_plane, 4, :, D:] = jnp.zeros((24, D + 128), BF16)
            send[step_plane, 4] = jnp.zeros((24, 2 * D + 128), BF16)


def attention_backward(core, d_middle, hidden, record, weights, d_mod, bias, cond, d_cond, chips, first):
    _, mod, qkv, attended, projected, *_ = record
    left, right, _, _ = weights
    rows = D // chips
    return pl.pallas_call(
        functools.partial(attention_kernel, chips, first=first),
        grid=(SLOT // STEP,),
        out_shape=(
            tokens(D, F32),
            jax.ShapeDtypeStruct((SLOT, D), F32),
            jax.ShapeDtypeStruct((4, 5, rows, 2 * D + 128), BF16),
            jax.ShapeDtypeStruct((4, 5, rows, 2 * D + 128), BF16),
        ),
        in_specs=[
            SMEM,
            per_slot(D),
            per_slot(D),
            per_slot(3 * D),
            per_slot(D),
            per_slot(D),
            whole(SLOT, 6 * D),
            whole(D, HALF),
            whole(D, HALF),
            whole(24, D),
            whole(1, FF + D),
            whole(SLOT, D),
            whole(SLOT, D),
        ],
        out_specs=(
            per_slot(D),
            whole(SLOT, D),
            whole(4, 5, rows, 2 * D + 128),
            whole(4, 5, rows, 2 * D + 128),
        ),
        scratch_shapes=[
            pltpu.VMEM((D, 3 * D), F32),
            pltpu.VMEM((D, D), F32),
            pltpu.VMEM((24, D), F32),
            pltpu.VMEM((1, BIAS), F32),
        ],
        compiler_params=params_of(1, 52 if first else 36),
        cost_estimate=cost(6 * 10**9, 20 * 2**20),
        name="attention_backward",
    )(core, d_middle, hidden, qkv, attended, projected, mod, left, right, d_mod, bias, cond, d_cond)


def finish_kernel(chips, place, own_ffn, own_attn, got_ffn, got_attn, own_mod, got_mod, cond, ada_out, qkv_out, proj_out, fc1_out, fc2_out, bias_out):
    rows = D // (2 * chips)
    is_odd = place[0] == 1
    mine = 8 * place[2] + 2 * place[1] + place[0]
    take = lax.broadcasted_iota(jnp.int32, (16, D), 0)
    column = lax.broadcasted_iota(jnp.int32, (16, D), 1)
    pick = ((column == rows * mine + take) & (take < rows)).astype(F32).astype(BF16)
    chosen = [right_product(pick, cond[side].astype(BF16)).astype(BF16) for side in range(2)]
    slots = SLOT * chips
    source = lax.broadcasted_iota(jnp.int32, (slots, 24 * chips), 0)
    target = lax.broadcasted_iota(jnp.int32, (slots, 24 * chips), 1)
    block = target // 24
    chip = 4 * ((place[2] + 4 - block // 4) % 4) + ((block % 4) ^ place[1])
    places = []
    for part in range(6):
        spot = (source // SLOT == chip) & (target % 24 == SLOT * part + source % SLOT)
        spot = spot.astype(F32).astype(BF16)
        places.append([dot_nn(chosen[side], spot).astype(BF16) for side in range(2)])

    def in_rows(mods):
        return jnp.concatenate(
            [mods[level, :, step * D : (step + 1) * D] for level in range(4) for step in range(4)], axis=0
        )

    for layer in range(2):
        own, got = in_rows(own_mod.at[layer]), in_rows(got_mod.at[layer])
        even = jnp.where(is_odd, got, own)
        odd = jnp.where(is_odd, own, got)
        for part in range(6):
            block = dot_nn(places[part][0], even) + dot_nn(places[part][1], odd)
            for row in range(rows):
                start = row * 6 * D + part * D
                ada_out[layer : layer + 1, start : start + D] = block[row : row + 1]
        own = jnp.where(is_odd, own_ffn[layer, rows:, :], own_ffn[layer, :rows, :])
        got = got_ffn[layer]
        first = jnp.where(is_odd, got, own[:, : 2 * D])
        second = jnp.where(is_odd, own[:, : 2 * D], got)
        for row in range(rows):
            fc1_out[layer : layer + 1, row * FF : row * FF + 2 * D] = first[row : row + 1]
            fc1_out[layer : layer + 1, row * FF + 2 * D : (row + 1) * FF] = second[row : row + 1]
        for row in range(4 * rows):
            column_start = (2 + row // (2 * rows)) * D
            fc2_out[layer : layer + 1, row * D : (row + 1) * D] = own_ffn[
                layer, row % (2 * rows) : row % (2 * rows) + 1, column_start : column_start + D
            ]
        own = jnp.where(is_odd, own_attn[layer, rows:, :], own_attn[layer, :rows, :])
        got = got_attn[layer]
        first = jnp.where(is_odd, got, own[:, : 2 * D])
        second = jnp.where(is_odd, own[:, : 2 * D], got)
        for row in range(rows):
            qkv_out[layer : layer + 1, row * 3 * D : row * 3 * D + 2 * D] = first[row : row + 1]
            qkv_out[layer : layer + 1, row * 3 * D + 2 * D : (row + 1) * 3 * D] = second[row : row + 1, :D]
            proj_out[layer : layer + 1, row * D : (row + 1) * D] = second[row : row + 1, D:]
        for part in range(2):
            bias_out[layer : layer + 1, part * 128 : (part + 1) * 128] = own_attn[
                layer, part : part + 1, 2 * D : 2 * D + 128
            ]


def finish(place, own_ffn, own_attn, got_ffn, got_attn, own_mod, got_mod, cond, shapes, chips):
    return pl.pallas_call(
        functools.partial(finish_kernel, chips),
        out_shape=tuple(jax.ShapeDtypeStruct(shape, F32) for shape in shapes),
        in_specs=[SMEM] + [VMEM] * 7,
        out_specs=(VMEM,) * 6,
        compiler_params=params_of(),
        name="finish",
    )(place, own_ffn, own_attn, got_ffn, got_attn, own_mod, got_mod, cond)


def fast_body(
    latents_in, condition, counts, ada_weight, qkv_weight, proj_weight, fc1_weight, fc2_weight, biases, cotangent
):
    devices = lax.axis_size("fsdp")
    chips = devices // 2
    rows = D // devices
    index = lax.axis_index("fsdp")
    swap = [(one, one ^ 1) for one in range(devices)]

    lines = [[8 * level + one for level in range(4)] for one in range(8)]
    place = core = jnp.stack([index % 2, index // 2 % 4, index // 8])
    tie = lax.optimization_barrier

    def along(value, bit):
        return lax.ppermute(value, "fsdp", [(one, one ^ bit) for one in range(devices)])

    def stacked(copies):
        return lax.all_to_all(copies, "fsdp", 0, 0, axis_index_groups=lines, tiled=True)

    def with_other_core(held):
        return [*held, *[(along(block, 1), (1, *spot[1:])) for block, spot in held]]

    def planes_of(stack, column):
        return [(stack if step == 0 else along(stack, 2 * step), (0, step, 0, column)) for step in range(4)]

    copies_left, copies_right, copies_last = pack(
        ada_weight, qkv_weight, proj_weight, fc1_weight, fc2_weight, biases, condition, rows, 4
    )
    stack_left, copies_right = tie((stacked(copies_left), copies_right))
    stack_right, copies_last = tie((stacked(copies_right), copies_last))
    blocks, stack_right = tie(([block for block, _ in planes_of(stack_left, 0)], stack_right))
    planes_left = [(block, (0, step, 0, 0)) for step, block in enumerate(blocks)]
    planes_right = planes_of(stack_right, WIRE // 2)
    stack_last = stacked(copies_last)
    held_first = [*with_other_core(planes_left), *with_other_core(planes_right)]
    stack_last, place = tie((stack_last, place))
    *first_weights, cond_all = unpack_wire(place, held_first)
    planes_last = planes_of(stack_last, 0)
    first = forward_block(counts, latents_in, condition, first_weights, False)
    blocks, first = tie(([block for block, _ in planes_last], first))
    held_last = with_other_core([(block, spot) for block, (_, spot) in zip(blocks, planes_last, strict=True)])
    *last_weights, _ = unpack_wire(place, held_last)
    last = forward_block(counts, first[0], condition, last_weights, True)
    weights, records, hidden = [first_weights, last_weights], [first, last], [latents_in, first[0], last[0]]
    upstream = cotangent
    d_cond = jnp.zeros((SLOT, D), F32)

    def paired(keep, send):
        got = lax.ppermute(send, "fsdp", swap)
        return [(keep[step].astype(F32) + got[step].astype(F32)).astype(BF16) for step in range(4)]

    def in_plane(parts):
        return [parts[step] if step == 0 else along(parts[step], 2 * step) for step in range(4)]

    def in_line(parts):
        def shifted(value, step):
            return lax.ppermute(value, "fsdp", [(one, (one + 8 * step) % devices) for one in range(devices)])

        return [parts[step] if step == 0 else shifted(parts[step], step) for step in range(4)]

    def plane_sums(parts):
        return [sum(part[level].astype(F32) for part in parts).astype(BF16) for level in range(4)]

    def with_mods(parts):
        mods = [part[4, :, :D] for part in parts]
        return [jnp.concatenate([level, *mods], axis=1) for level in plane_sums(parts)]

    def total(parts):
        return sum(part.astype(F32) for part in parts)

    d_middle, d_mod, bias, *wire = ffn_backward(core, counts, upstream, records[1], weights[1], chips, True)
    d_middle, both = tie((d_middle, paired(*wire)))
    ffn_last = in_plane(both)
    upstream, d_cond, *wire = attention_backward(
        core, d_middle, hidden[1], records[1], weights[1], d_mod, bias, condition, d_cond, chips, False
    )
    upstream, wire, ffn_last = tie((upstream, wire, ffn_last))
    upstream, both, sums = tie((upstream, paired(*wire), plane_sums(ffn_last)))
    ffn_last, attn_last = in_line(sums), in_plane(both)
    d_middle, d_mod, bias, *wire = ffn_backward(core, counts, upstream, records[0], weights[0], chips, False)
    d_middle, wire, ffn_last, attn_last = tie((d_middle, wire, ffn_last, attn_last))
    d_middle, both, sums = tie((d_middle, paired(*wire), with_mods(attn_last)))
    attn_last, ffn_first = in_line(sums), in_plane(both)
    upstream, d_cond, *wire = attention_backward(
        core, d_middle, hidden[0], records[0], weights[0], d_mod, bias, condition, d_cond, chips, True
    )
    wire, attn_last, ffn_first = tie((wire, attn_last, ffn_first))
    attn_first = in_plane(paired(*wire))
    ffn_first = in_line(plane_sums(ffn_first))
    attn_first = in_line(with_mods(attn_first))
    width = 2 * D + 128
    own_ffn = jnp.stack([total(ffn_first), total(ffn_last)])
    own_attn = jnp.stack([total([part[:, :width] for part in parts]) for parts in (attn_first, attn_last)])
    own_mod = jnp.stack([jnp.stack([part[:, width:] for part in parts]) for parts in (attn_first, attn_last)])
    start = (1 - index % 2) * rows
    to_send = jnp.concatenate([own_ffn[:, :, : 2 * D], own_attn[:, :, : 2 * D]], axis=2)
    got = lax.ppermute(lax.dynamic_slice_in_dim(to_send, start, rows, axis=1), "fsdp", swap)
    got_mod = lax.ppermute(own_mod, "fsdp", swap)
    shapes = [array.shape for array in (ada_weight, qkv_weight, proj_weight, fc1_weight, fc2_weight, biases)]
    grads = finish(
        place, own_ffn, own_attn, got[:, :, : 2 * D], got[:, :, 2 * D :], own_mod, got_mod, cond_all, shapes, chips
    )
    return (hidden[2], upstream, d_cond, *grads)


def choose_body(
    latents_in, condition, counts, ada_weight, qkv_weight, proj_weight, fc1_weight, fc2_weight, biases, cotangent
):
    devices = lax.axis_size("fsdp")
    rows = D // devices
    fits = (
        D % devices == 0
        and devices == 32
        and latents_in.shape == (SLOT, SEQ, D)
        and ada_weight.shape == (2, rows * 6 * D)
        and qkv_weight.shape == (2, rows * 3 * D)
        and proj_weight.shape == (2, rows * D)
        and fc1_weight.shape == (2, rows * FF)
        and fc2_weight.shape == (2, rows * FF)
        and biases.shape == (2, 256)
    )
    chosen = fast_body if fits else body
    return chosen(
        latents_in, condition, counts, ada_weight, qkv_weight, proj_weight, fc1_weight, fc2_weight, biases, cotangent
    )


def solution(mesh):
    return jax.shard_map(
        choose_body,
        mesh=mesh,
        in_specs=(
            P("fsdp", None, None),
            P("fsdp", None),
            P("fsdp"),
            P(None, "fsdp"),
            P(None, "fsdp"),
            P(None, "fsdp"),
            P(None, "fsdp"),
            P(None, "fsdp"),
            P(None, "fsdp"),
            P("fsdp", None, None),
        ),
        out_specs=(
            P("fsdp", None, None),
            P("fsdp", None, None),
            P("fsdp", None),
            P(None, "fsdp"),
            P(None, "fsdp"),
            P(None, "fsdp"),
            P(None, "fsdp"),
            P(None, "fsdp"),
            P(None, "fsdp"),
        ),
        check_vma=False,
    )
```

```python
import functools
import math

import jax
import jax.numpy as jnp
from jax import lax
from jax.experimental import pallas as pl
from jax.experimental.pallas import tpu as pltpu
from jax.sharding import PartitionSpec as P

D = 384
HEADS = 6
HEAD = 64
FF = 1536


EPSILON = 1e-06


def modulate_norm(values_in, shift_add, scale_mul):
    centred = values_in - jnp.mean(values_in, axis=-1, keepdims=True)
    variance = jnp.mean(centred * centred, axis=-1, keepdims=True)
    normed = centred * lax.rsqrt(variance + EPSILON)
    return normed * (1.0 + scale_mul[:, None, :]) + shift_add[:, None, :]


def gelu_tanh(values_in):
    return jax.nn.gelu(values_in, approximate=True)


def left_product(left, right):
    return lax.dot_general(
        left, right, (((0,), (0,)), ((), ())), preferred_element_type=jnp.float32
    )


def right_product(left, right):
    return lax.dot_general(
        left, right, (((1,), (1,)), ((), ())), preferred_element_type=jnp.float32
    )


def unpack(gathered):
    ada_flat, qkv_flat, proj_flat, fc1_flat, fc2_flat, bias_flat = gathered
    bias_wide = bias_flat.astype(jnp.float32)
    return (
        ada_flat.reshape(D, 6 * D),
        qkv_flat[: 3 * D * D].reshape(D, 3 * D),
        proj_flat[: D * D].reshape(D, D),
        fc1_flat.reshape(D, FF),
        fc2_flat.reshape(FF, D),
        bias_wide[: 6 * D],
        bias_wide[6 * D : 7 * D],
        bias_wide[7 * D : 8 * D],
        bias_wide[8 * D : 9 * D],
        bias_wide[9 * D : 9 * D + FF],
        bias_wide[9 * D + FF : 10 * D + FF],
    )


def split_modulation(modulation):
    return [modulation[:, part_index * D : (part_index + 1) * D] for part_index in range(6)]


def layer_forward(hidden, cond_act, params):
    w_ada, w_qkv, w_proj, w_fc1, w_fc2, b_ada, b_query, b_value, b_proj, b_fc1, b_fc2 = params
    slot_count, seq_len = (hidden.shape[0], hidden.shape[1])
    modulation = jnp.dot(cond_act, w_ada, preferred_element_type=jnp.float32) + b_ada
    shift_attn, scale_attn, gate_attn, shift_ffn, scale_ffn, gate_ffn = split_modulation(modulation)
    normed_attn = modulate_norm(hidden, shift_attn, scale_attn).astype(jnp.bfloat16).reshape(-1, D)
    mixed_qkv = jnp.dot(normed_attn, w_qkv, preferred_element_type=jnp.float32)
    queries = (
        (mixed_qkv[:, 0:D] + b_query).astype(jnp.bfloat16).reshape(slot_count, seq_len, HEADS, HEAD)
    )
    key_heads = (
        mixed_qkv[:, D : 2 * D].astype(jnp.bfloat16).reshape(slot_count, seq_len, HEADS, HEAD)
    )
    value_heads = (
        (mixed_qkv[:, 2 * D : 3 * D] + b_value)
        .astype(jnp.bfloat16)
        .reshape(slot_count, seq_len, HEADS, HEAD)
    )
    scores = jnp.einsum(
        "bqhd,bkhd->bhqk", queries, key_heads, preferred_element_type=jnp.float32
    ) * (1.0 / math.sqrt(HEAD))
    peak_score = jnp.max(scores, axis=-1, keepdims=True)
    exp_scores = jnp.exp(scores - peak_score)
    exp_total = jnp.sum(exp_scores, axis=-1, keepdims=True)
    logsum = peak_score + jnp.log(exp_total)
    attn_probs = (exp_scores / exp_total).astype(jnp.bfloat16)
    attended = jnp.einsum(
        "bhqk,bkhd->bqhd", attn_probs, value_heads, preferred_element_type=jnp.float32
    )
    attended = attended.astype(jnp.bfloat16).reshape(-1, D)
    projected = (jnp.dot(attended, w_proj, preferred_element_type=jnp.float32) + b_proj).reshape(
        slot_count, seq_len, D
    )
    middle = hidden + gate_attn[:, None, :] * projected
    normed_ffn = modulate_norm(middle, shift_ffn, scale_ffn).astype(jnp.bfloat16).reshape(-1, D)
    pre_act = jnp.dot(normed_ffn, w_fc1, preferred_element_type=jnp.float32) + b_fc1
    activation = gelu_tanh(pre_act).astype(jnp.bfloat16)
    branch = (jnp.dot(activation, w_fc2, preferred_element_type=jnp.float32) + b_fc2).reshape(
        slot_count, seq_len, D
    )
    result = middle + gate_ffn[:, None, :] * branch
    record = (
        hidden,
        modulation,
        normed_attn,
        queries,
        key_heads,
        value_heads,
        logsum,
        attended,
        projected,
        middle,
        normed_ffn,
        pre_act,
        activation,
        branch,
    )
    return (result, record)


def layer_backward(upstream, params, record):
    w_ada, w_qkv, w_proj, w_fc1, w_fc2, b_ada, b_query, b_value, b_proj, b_fc1, b_fc2 = params
    (
        hidden,
        modulation,
        normed_attn,
        queries,
        key_heads,
        value_heads,
        logsum,
        attended,
        projected,
        middle,
        normed_ffn,
        pre_act,
        activation,
        branch,
    ) = record
    slot_count, seq_len = (hidden.shape[0], hidden.shape[1])
    shift_attn, scale_attn, gate_attn, shift_ffn, scale_ffn, gate_ffn = split_modulation(modulation)
    d_branch = (upstream * gate_ffn[:, None, :]).reshape(-1, D)
    d_gate_ffn = jnp.sum(upstream * branch, axis=1)
    grad_b_fc2 = jnp.sum(d_branch, axis=0)
    branch_low = d_branch.astype(jnp.bfloat16)
    grad_w_fc2 = left_product(activation, branch_low)
    d_act = right_product(branch_low, w_fc2)
    gelu_out, gelu_pull = jax.vjp(gelu_tanh, pre_act)
    (d_pre,) = gelu_pull(d_act)
    grad_b_fc1 = jnp.sum(d_pre, axis=0)
    pre_low = d_pre.astype(jnp.bfloat16)
    grad_w_fc1 = left_product(normed_ffn, pre_low)
    d_normed_ffn = right_product(pre_low, w_fc1).reshape(slot_count, seq_len, D)
    norm_out, norm_pull = jax.vjp(modulate_norm, middle, shift_ffn, scale_ffn)
    middle_part, d_shift_ffn, d_scale_ffn = norm_pull(d_normed_ffn)
    d_middle = upstream + middle_part
    d_proj = (d_middle * gate_attn[:, None, :]).reshape(-1, D)
    d_gate_attn = jnp.sum(d_middle * projected, axis=1)
    grad_b_proj = jnp.sum(d_proj, axis=0)
    proj_low = d_proj.astype(jnp.bfloat16)
    grad_w_proj = left_product(attended, proj_low)
    d_attended = (
        right_product(proj_low, w_proj)
        .astype(jnp.bfloat16)
        .reshape(slot_count, seq_len, HEADS, HEAD)
    )
    scores = jnp.einsum(
        "bqhd,bkhd->bhqk", queries, key_heads, preferred_element_type=jnp.float32
    ) * (1.0 / math.sqrt(HEAD))
    attn_probs = jnp.exp(scores - logsum)
    d_probs = jnp.einsum(
        "bqhd,bkhd->bhqk", d_attended, value_heads, preferred_element_type=jnp.float32
    )
    d_values = jnp.einsum(
        "bhqk,bqhd->bkhd",
        attn_probs.astype(jnp.bfloat16),
        d_attended,
        preferred_element_type=jnp.float32,
    )
    row_inner = jnp.sum(attn_probs * d_probs, axis=-1, keepdims=True)
    d_scores = (attn_probs * (d_probs - row_inner) * (1.0 / math.sqrt(HEAD))).astype(jnp.bfloat16)
    d_query = jnp.einsum(
        "bhqk,bkhd->bqhd", d_scores, key_heads, preferred_element_type=jnp.float32
    ).reshape(-1, D)
    d_keys = jnp.einsum(
        "bhqk,bqhd->bkhd", d_scores, queries, preferred_element_type=jnp.float32
    ).reshape(-1, D)
    d_values = d_values.reshape(-1, D)
    grad_b_query = jnp.sum(d_query, axis=0)
    grad_b_value = jnp.sum(d_values, axis=0)
    mixed_low = jnp.concatenate([d_query, d_keys, d_values], axis=1).astype(jnp.bfloat16)
    grad_w_qkv = left_product(normed_attn, mixed_low)
    d_normed_attn = right_product(mixed_low, w_qkv).reshape(slot_count, seq_len, D)
    attn_out, attn_pull = jax.vjp(modulate_norm, hidden, shift_attn, scale_attn)
    hidden_part, d_shift_attn, d_scale_attn = attn_pull(d_normed_attn)
    d_hidden = d_middle + hidden_part
    d_mod = jnp.concatenate(
        [d_shift_attn, d_scale_attn, d_gate_attn, d_shift_ffn, d_scale_ffn, d_gate_ffn], axis=1
    )
    grad_b_ada = jnp.sum(d_mod, axis=0)
    mod_low = d_mod.astype(jnp.bfloat16)
    d_cond = right_product(mod_low, w_ada)
    grad_bias = jnp.concatenate(
        [grad_b_ada, grad_b_query, grad_b_value, grad_b_proj, grad_b_fc1, grad_b_fc2]
    )
    return (d_hidden, d_cond, mod_low, (grad_w_qkv, grad_w_proj, grad_w_fc1, grad_w_fc2, grad_bias))


def pad_flat(values_in, length):
    flat = values_in.reshape(-1)
    return jnp.pad(flat, (0, length - flat.shape[0]))


def body(
    latents_in,
    condition,
    counts,
    ada_weight,
    qkv_weight,
    proj_weight,
    fc1_weight,
    fc2_weight,
    biases,
    cotangent,
):
    slot_count = latents_in.shape[0]
    layer_total = ada_weight.shape[0]
    device_count = lax.axis_size("fsdp")
    rest_list = (qkv_weight, proj_weight, fc1_weight, fc2_weight, biases)
    rest_lengths = [piece.shape[1] * device_count for piece in rest_list]
    ada_shard = ada_weight.shape[1]
    occupied = (jnp.arange(slot_count) < counts[0]).astype(jnp.float32)
    cond_wide = condition.astype(jnp.float32)
    silu_out, silu_pull = jax.vjp(jax.nn.silu, cond_wide)
    cond_act = silu_out.astype(jnp.bfloat16)
    hidden = latents_in.astype(jnp.float32)
    records = []
    for layer_index in range(layer_total):
        gathered = (
            lax.all_gather(ada_weight[layer_index], "fsdp", axis=0, tiled=True),
            lax.all_gather(qkv_weight[layer_index], "fsdp", axis=0, tiled=True),
            lax.all_gather(proj_weight[layer_index], "fsdp", axis=0, tiled=True),
            lax.all_gather(fc1_weight[layer_index], "fsdp", axis=0, tiled=True),
            lax.all_gather(fc2_weight[layer_index], "fsdp", axis=0, tiled=True),
            lax.all_gather(biases[layer_index], "fsdp", axis=0, tiled=True),
        )
        params = unpack(gathered)
        hidden, record = layer_forward(hidden, cond_act, params)
        records.append(record)
    latents_out = hidden * occupied[:, None, None]
    upstream = cotangent.astype(jnp.float32) * occupied[:, None, None]
    cond_total = jnp.zeros(cond_wide.shape, jnp.float32)
    layer_sums = [None] * layer_total
    mod_lows = [None] * layer_total
    for layer_index in reversed(range(layer_total)):
        gathered = (
            lax.all_gather(ada_weight[layer_index], "fsdp", axis=0, tiled=True),
            lax.all_gather(qkv_weight[layer_index], "fsdp", axis=0, tiled=True),
            lax.all_gather(proj_weight[layer_index], "fsdp", axis=0, tiled=True),
            lax.all_gather(fc1_weight[layer_index], "fsdp", axis=0, tiled=True),
            lax.all_gather(fc2_weight[layer_index], "fsdp", axis=0, tiled=True),
            lax.all_gather(biases[layer_index], "fsdp", axis=0, tiled=True),
        )
        params = unpack(gathered)
        upstream, d_cond, mod_low, grad_parts = layer_backward(
            upstream, params, records[layer_index]
        )
        mod_lows[layer_index] = mod_low
        cond_total = cond_total + d_cond
        padded = [
            pad_flat(grad_parts[part_index], rest_lengths[part_index]) for part_index in range(5)
        ]
        layer_sums[layer_index] = (
            lax.psum_scatter(padded[0], "fsdp", scatter_dimension=0, tiled=True),
            lax.psum_scatter(padded[1], "fsdp", scatter_dimension=0, tiled=True),
            lax.psum_scatter(padded[2], "fsdp", scatter_dimension=0, tiled=True),
            lax.psum_scatter(padded[3], "fsdp", scatter_dimension=0, tiled=True),
            lax.psum_scatter(padded[4], "fsdp", scatter_dimension=0, tiled=True),
        )
    grad_rest = [
        jnp.stack([layer_sums[layer_index][part_index] for layer_index in range(layer_total)])
        for part_index in range(5)
    ]
    mod_joined = jnp.concatenate(mod_lows, axis=1)
    ada_full = left_product(
        lax.all_gather(cond_act, "fsdp", axis=0, tiled=True),
        lax.all_gather(mod_joined, "fsdp", axis=0, tiled=True),
    )
    own_start = lax.axis_index("fsdp") * ada_shard
    ada_rows = []
    for layer_index in range(layer_total):
        flat_layer = pad_flat(
            ada_full[:, layer_index * 6 * D : (layer_index + 1) * 6 * D], ada_shard * device_count
        )
        ada_rows.append(lax.dynamic_slice_in_dim(flat_layer, own_start, ada_shard))
    ada_grad = jnp.stack(ada_rows)
    (condition_grad,) = silu_pull(cond_total)
    return (
        latents_out,
        upstream,
        condition_grad,
        ada_grad,
        grad_rest[0],
        grad_rest[1],
        grad_rest[2],
        grad_rest[3],
        grad_rest[4],
    )


BF16 = jnp.bfloat16
F32 = jnp.float32
SLOT = 4
STEP = 1
CHUNK = 512
SEQ = 256
HALF = 7 * D
WIRE = HALF + 2 * D + 128
BIAS = 10 * D + FF
VMEM = pl.BlockSpec(memory_space=pltpu.VMEM)
SMEM = pl.BlockSpec(memory_space=pltpu.SMEM)


def params_of(grid_rank=0, megabytes=36):
    semantics = ("arbitrary",) * grid_rank if grid_rank else None
    return pltpu.CompilerParams(vmem_limit_bytes=megabytes * 2**20, dimension_semantics=semantics)


def dot_nn(left, right):
    return lax.dot_general(
        left, right, (((1,), (0,)), ((), ())), preferred_element_type=jnp.float32
    )


def pack_kernel(rows, ada_in, qkv_in, proj_in, fc1_in, fc2_in, bias_in, cond, out_left, out_right, out_last, ada, qkv, proj, fc1, fc2, bias, sems, wide):
    copies = [
        pltpu.make_async_copy(source, target, sems.at[place])
        for place, (source, target) in enumerate(
            ((ada_in, ada), (qkv_in, qkv), (proj_in, proj), (fc1_in, fc1), (fc2_in, fc2), (bias_in, bias))
        )
    ]
    for copy in copies:
        copy.start()
    wide[:, :, WIRE - 128 :] = jnp.zeros((2, 2 * rows, 128), F32)
    wide_cond = cond[...].astype(F32)
    act = (wide_cond / (1.0 + jnp.exp(-wide_cond))).astype(BF16).astype(F32)
    for part in range(3):
        wide[0, 8 + 4 * part : 12 + 4 * part, WIRE - 128 :] = act[:, part * 128 : part * 128 + 128]
    for copy in copies:
        copy.wait()

    def put(source, start, width, row, column):
        values = source[:, start : start + width].astype(F32)
        for layer in range(2):
            wide[layer, row : row + 1, column : column + width] = values[layer : layer + 1]

    for row in range(rows):
        put(ada, row * 6 * D, 6 * D, row, 0)
        put(qkv, row * 3 * D, D, row, 6 * D)
        put(qkv, row * 3 * D + D, 2 * D, rows + row, 0)
        put(proj, row * D, D, rows + row, 2 * D)
        put(fc1, row * FF, FF, rows + row, 3 * D)
    for row in range(4 * rows):
        put(fc2, row * D, D, row % (2 * rows), HALF + D * (row // (2 * rows)))
    put(bias, 0, 128, 0, WIRE - 128)
    put(bias, 128, 128, 1, WIRE - 128)
    low = wide[0].astype(BF16)
    low_last = wide[1].astype(BF16)
    for copy_index in range(out_last.shape[0]):
        out_left[copy_index] = low[:, : WIRE // 2]
        out_right[copy_index] = low[:, WIRE // 2 :]
        out_last[copy_index] = low_last


def pack(ada, qkv, proj, fc1, fc2, bias, cond, rows, copies):
    flat = (ada, qkv, proj, fc1, fc2, bias)
    return pl.pallas_call(
        functools.partial(pack_kernel, rows),
        out_shape=tuple(
            jax.ShapeDtypeStruct((copies, 2 * rows, width), BF16) for width in (WIRE // 2, WIRE // 2, WIRE)
        ),
        in_specs=[pl.BlockSpec(memory_space=pltpu.HBM)] * 6 + [VMEM],
        out_specs=(VMEM,) * 3,
        scratch_shapes=[pltpu.VMEM(array.shape, BF16) for array in flat]
        + [pltpu.SemaphoreType.DMA((6,)), pltpu.VMEM((2, 2 * rows, WIRE), F32)],
        compiler_params=params_of(0, 62),
        name="pack",
    )(*flat, cond)


def unpack_kernel(rows, spots, place, *refs):
    blocks, (left, right, down, bias, cond, wire, sems) = refs[:-7], refs[-7:]
    copies = []
    for number, (block, (side, step, level, column)) in enumerate(zip(blocks, spots, strict=True)):
        target = wire.at[
            (place[0] + side) % 2,
            place[1] ^ step,
            pl.ds(level, block.shape[0]),
            :,
            pl.ds(column, block.shape[2]),
        ]
        copies.append(pltpu.make_async_copy(block, target, sems.at[number]))
    for copy in copies:
        copy.start()
    for copy in copies:
        copy.wait()

    def of(device):
        return wire.at[device % 2, (device // 2) % 4, device // 8]

    for group in range(8):
        for half, target in ((0, left), (1, right)):
            target[4 * rows * group : 4 * rows * (group + 1), :] = jnp.concatenate(
                [of(4 * group + member)[half * rows : (half + 1) * rows, :HALF] for member in range(4)], axis=0
            )
    for device in range(32):
        for part in range(2):
            start = 4 * rows * device + 2 * rows * part
            column = HALF + D * part
            down[start : start + 2 * rows, :] = of(device)[:, column : column + D]
        tail = of(device)[:, WIRE - 128 :].astype(F32)
        for part in range(2):
            chunk = 2 * device + part
            if chunk < BIAS // 128:
                bias[0:1, chunk * 128 : chunk * 128 + 128] = tail[part : part + 1]
        for part in range(3):
            cond[device % 2, 4 * (device // 2) : 4 * (device // 2) + 4, part * 128 : part * 128 + 128] = tail[
                8 + 4 * part : 12 + 4 * part
            ]


def unpack_wire(place, held):
    blocks, spots = [block for block, _ in held], [spot for _, spot in held]
    rows = blocks[0].shape[1] // 2
    return pl.pallas_call(
        functools.partial(unpack_kernel, rows, spots),
        out_shape=(
            jax.ShapeDtypeStruct((D, HALF), BF16),
            jax.ShapeDtypeStruct((D, HALF), BF16),
            jax.ShapeDtypeStruct((FF, D), BF16),
            jax.ShapeDtypeStruct((1, BIAS), F32),
            jax.ShapeDtypeStruct((2, SLOT * 16, D), F32),
        ),
        in_specs=[SMEM] + [pl.BlockSpec(memory_space=pl.ANY)] * len(blocks),
        out_specs=(VMEM,) * 5,
        scratch_shapes=[pltpu.VMEM((2, 4, 4, 2 * rows, WIRE), BF16), pltpu.SemaphoreType.DMA((len(blocks),))],
        compiler_params=params_of(0, 24),
        name="unpack",
    )(place, *blocks)


def norm_stats(values):
    centred = values - jnp.mean(values, axis=-1, keepdims=True)
    rstd = lax.rsqrt(jnp.mean(centred * centred, axis=-1, keepdims=True) + EPSILON)
    return centred * rstd, rstd


def mod_part(mod, step, part):
    rows = [
        jnp.broadcast_to(mod[pl.ds(STEP * step + slot, 1), part * D : (part + 1) * D], (SEQ, D))
        for slot in range(STEP)
    ]
    return rows[0] if STEP == 1 else jnp.concatenate(rows, axis=0)


def put_sums(d_mod, step, part, values):
    for slot in range(STEP):
        d_mod[pl.ds(SLOT * part + STEP * step + slot, 1), :] = row_sum(values[slot * SEQ : (slot + 1) * SEQ])


def occupied(counts, step):
    rows = [
        jnp.full((SEQ, 1), jnp.where(STEP * step + slot < counts[0], 1.0, 0.0), F32) for slot in range(STEP)
    ]
    return rows[0] if STEP == 1 else jnp.concatenate(rows, axis=0)


def flat(ref):
    return ref[...].reshape(STEP * SEQ, ref.shape[2])


def gelu_and_slope(pre):
    factor, cubic = 0.7978845608028654, 0.044715
    square = pre * pre
    half = 0.5 + 0.5 * jnp.tanh(pre * (factor + (factor * cubic) * square))
    act = pre * half
    return act, half + act * (1.0 - half) * (2.0 * factor + (6.0 * factor * cubic) * square)


def row_sum(values):
    return jnp.sum(values, axis=0, keepdims=True)


def head_masks(factor):
    lane = lax.broadcasted_iota(jnp.int32, (1, 2 * HEAD), 1)
    first = jnp.where(lane < HEAD, factor, 0.0).astype(BF16)
    second = jnp.where(lane < HEAD, 0.0, factor).astype(BF16)
    return first, second


def both_heads(pair, masks):
    return jnp.concatenate([pair * masks[0], pair * masks[1]], axis=0)


def merge_heads(stack):
    lane = lax.broadcasted_iota(jnp.int32, (SEQ, 2 * HEAD), 1)
    return jnp.where(lane < HEAD, stack[:SEQ], stack[SEQ:])


def softmax_keys(scores):
    raised = jnp.exp(scores - jnp.max(scores, axis=0, keepdims=True))
    return raised * (1.0 / jnp.sum(raised, axis=0, keepdims=True))


def forward_kernel(counts, hidden, cond, left, right, down, bias, out, mod, qkv, attended, projected, middle, active, slope, branch, *, last):
    step = pl.program_id(0)

    @pl.when(step == 0)
    def _():
        wide_cond = cond[...].astype(F32)
        act = (wide_cond / (1.0 + jnp.exp(-wide_cond))).astype(BF16)
        mod[...] = dot_nn(act, left[:, : 6 * D]) + bias[:, : 6 * D]

    values = flat(hidden).astype(F32)
    normed, _ = norm_stats(values)
    normed = (normed * (1.0 + mod_part(mod, step, 1)) + mod_part(mod, step, 0)).astype(BF16)
    queries = (dot_nn(normed, left[:, 6 * D :]) + bias[:, 6 * D : 7 * D]).astype(BF16)
    mixed = dot_nn(normed, right[:, : 2 * D])
    keys = mixed[:, :D].astype(BF16)
    heads_in = (mixed[:, D:] + bias[:, 7 * D : 8 * D]).astype(BF16)
    qkv[:, :, :D] = queries.reshape(STEP, SEQ, D)
    qkv[:, :, D : 2 * D] = keys.reshape(STEP, SEQ, D)
    qkv[:, :, 2 * D :] = heads_in.reshape(STEP, SEQ, D)
    masks = head_masks(1.0 / math.sqrt(HEAD))
    joined = []
    for slot in range(STEP):
        rows = slice(slot * SEQ, (slot + 1) * SEQ)
        pairs = []
        for pair in range(HEADS // 2):
            span = slice(pair * 2 * HEAD, (pair + 1) * 2 * HEAD)
            probs = softmax_keys(right_product(keys[rows, span], both_heads(queries[rows, span], masks)))
            pairs.append(merge_heads(left_product(probs.astype(BF16), heads_in[rows, span])).astype(BF16))
        joined.append(jnp.concatenate(pairs, axis=1))
    joined = joined[0] if STEP == 1 else jnp.concatenate(joined, axis=0)
    attended[...] = joined.reshape(STEP, SEQ, D)
    proj = dot_nn(joined, right[:, 2 * D : 3 * D]) + bias[:, 8 * D : 9 * D]
    projected[...] = proj.reshape(STEP, SEQ, D)
    mid = values + mod_part(mod, step, 2) * proj
    middle[...] = mid.reshape(STEP, SEQ, D)
    normed, _ = norm_stats(mid)
    normed = (normed * (1.0 + mod_part(mod, step, 4)) + mod_part(mod, step, 3)).astype(BF16)
    ffn = bias[:, 9 * D + FF :]
    for start in range(0, FF, CHUNK):
        stop = start + CHUNK
        pre = dot_nn(normed, right[:, 3 * D + start : 3 * D + stop]) + bias[:, 9 * D + start : 9 * D + stop]
        act, rate = gelu_and_slope(pre)
        act = act.astype(BF16)
        active[:, :, start:stop] = act.reshape(STEP, SEQ, CHUNK)
        slope[:, :, start:stop] = rate.reshape(STEP, SEQ, CHUNK)
        ffn = ffn + dot_nn(act, down[start:stop, :])
    branch[...] = ffn.reshape(STEP, SEQ, D)
    result = mid + mod_part(mod, step, 5) * ffn
    if last:
        result = result * occupied(counts, step)
    out[...] = result.reshape(STEP, SEQ, D)


def per_slot(width):
    return pl.BlockSpec((STEP, SEQ, width), lambda step: (step, 0, 0))


def whole(*shape):
    return pl.BlockSpec(shape, lambda step: (0,) * len(shape))


def tokens(width, dtype):
    return jax.ShapeDtypeStruct((SLOT, SEQ, width), dtype)


def cost(flops, moved):
    return pl.CostEstimate(flops=flops, bytes_accessed=moved, transcendentals=0)


def forward_block(counts, hidden, cond, weights, last):
    left, right, down, bias = weights
    return pl.pallas_call(
        functools.partial(forward_kernel, last=last),
        grid=(SLOT // STEP,),
        out_shape=(
            tokens(D, F32),
            jax.ShapeDtypeStruct((SLOT, 6 * D), F32),
            tokens(3 * D, BF16),
            tokens(D, BF16),
            tokens(D, F32),
            tokens(D, F32),
            tokens(FF, BF16),
            tokens(FF, F32),
            tokens(D, F32),
        ),
        in_specs=[
            SMEM,
            per_slot(D),
            whole(SLOT, D),
            whole(D, HALF),
            whole(D, HALF),
            whole(FF, D),
            whole(1, BIAS),
        ],
        out_specs=(
            per_slot(D),
            whole(SLOT, 6 * D),
            per_slot(3 * D),
            per_slot(D),
            per_slot(D),
            per_slot(D),
            per_slot(FF),
            per_slot(FF),
            per_slot(D),
        ),
        compiler_params=params_of(1, 36),
        cost_estimate=cost(5 * 10**9, 20 * 2**20),
        name="forward_block",
    )(counts, hidden, cond, left, right, down, bias)


def norm_backward(d_normed, normed, rstd, scale):
    inner = d_normed * (1.0 + scale)
    along = jnp.mean(inner * normed, axis=-1, keepdims=True)
    return rstd * (inner - jnp.mean(inner, axis=-1, keepdims=True) - normed * along)


def offsets(place, chip):
    return (chip // 4 + 4 - place[2]) % 4, place[1] ^ (chip % 4)


def ffn_kernel(chips, core, counts, upstream, branch, active, slope, middle, mod, right, down, d_middle, d_mod, bias, keep, send, acc_up, acc_down, *, last):
    step = pl.program_id(0)

    @pl.when(step == 0)
    def _():
        acc_up[...] = jnp.zeros_like(acc_up)
        acc_down[...] = jnp.zeros_like(acc_down)
        bias[...] = jnp.zeros_like(bias)
        d_mod[...] = jnp.zeros_like(d_mod)

    up = flat(upstream).astype(F32)
    if last:
        up = up * occupied(counts, step)
    d_branch = up * mod_part(mod, step, 5)
    put_sums(d_mod, step, 5, up * flat(branch))
    bias[:, FF:] += row_sum(d_branch)
    low = d_branch.astype(BF16)
    normed, rstd = norm_stats(flat(middle))
    scale = mod_part(mod, step, 4)
    shifted = (normed * (1.0 + scale) + mod_part(mod, step, 3)).astype(BF16)
    d_normed = 0.0
    for start in range(0, FF, CHUNK):
        stop = start + CHUNK
        d_pre = right_product(low, down[start:stop, :]) * slope[:, :, start:stop].reshape(STEP * SEQ, CHUNK)
        acc_down[start:stop, :] += left_product(active[:, :, start:stop].reshape(STEP * SEQ, CHUNK), low)
        bias[:, start:stop] += row_sum(d_pre)
        low_pre = d_pre.astype(BF16)
        acc_up[:, start:stop] += left_product(shifted, low_pre)
        d_normed = d_normed + right_product(low_pre, right[:, 3 * D + start : 3 * D + stop])
    put_sums(d_mod, step, 3, d_normed)
    put_sums(d_mod, step, 4, d_normed * normed)
    d_middle[...] = (up + norm_backward(d_normed, normed, rstd, scale)).reshape(STEP, SEQ, D)

    @pl.when(step == SLOT // STEP - 1)
    def _():
        rows = D // chips
        is_odd = core[0] == 1
        for chip in range(chips):
            span = slice(rows * chip, rows * (chip + 1))
            step_z, step_plane = offsets(core, chip)
            even, odd = acc_up[span, : 2 * D], acc_up[span, 2 * D :]
            keep[step_plane, step_z, :, : 2 * D] = jnp.where(is_odd, odd, even).astype(BF16)
            send[step_plane, step_z, :, : 2 * D] = jnp.where(is_odd, even, odd).astype(BF16)
            for part in range(2):
                start = rows * (4 * chip + part)
                even = acc_down[start : start + rows, :]
                odd = acc_down[start + 2 * rows : start + 3 * rows, :]
                columns = slice((2 + part) * D, (3 + part) * D)
                keep[step_plane, step_z, :, columns] = jnp.where(is_odd, odd, even).astype(BF16)
                send[step_plane, step_z, :, columns] = jnp.where(is_odd, even, odd).astype(BF16)


def ffn_backward(core, counts, upstream, record, weights, chips, last):
    _, mod, _, _, _, middle, active, slope, branch = record
    _, right, down, _ = weights
    rows = D // chips
    return pl.pallas_call(
        functools.partial(ffn_kernel, chips, last=last),
        grid=(SLOT // STEP,),
        out_shape=(
            tokens(D, F32),
            jax.ShapeDtypeStruct((24, D), F32),
            jax.ShapeDtypeStruct((1, FF + D), F32),
            jax.ShapeDtypeStruct((4, 4, rows, 4 * D), BF16),
            jax.ShapeDtypeStruct((4, 4, rows, 4 * D), BF16),
        ),
        in_specs=[
            SMEM,
            SMEM,
            per_slot(D),
            per_slot(D),
            per_slot(FF),
            per_slot(FF),
            per_slot(D),
            whole(SLOT, 6 * D),
            whole(D, HALF),
            whole(FF, D),
        ],
        out_specs=(
            per_slot(D),
            whole(24, D),
            whole(1, FF + D),
            whole(4, 4, rows, 4 * D),
            whole(4, 4, rows, 4 * D),
        ),
        scratch_shapes=[pltpu.VMEM((D, FF), F32), pltpu.VMEM((FF, D), F32)],
        compiler_params=params_of(1, 36),
        cost_estimate=cost(8 * 10**9, 20 * 2**20),
        name="ffn_backward",
    )(core, counts, upstream, branch, active, slope, middle, mod, right, down)


def attention_kernel(chips, core, d_middle, hidden, qkv, attended, projected, mod, left, right, d_mod_in, bias_in, cond, d_cond_in, d_hidden, d_cond, keep, send, acc, acc_proj, d_mod, bias, *, first):
    step = pl.program_id(0)

    @pl.when(step == 0)
    def _():
        acc[...] = jnp.zeros_like(acc)
        acc_proj[...] = jnp.zeros_like(acc_proj)
        bias[...] = jnp.zeros_like(bias)
        d_mod[...] = d_mod_in[...]

    d_mid = flat(d_middle)
    d_proj = d_mid * mod_part(mod, step, 2)
    put_sums(d_mod, step, 2, d_mid * flat(projected))
    bias[:, 8 * D : 9 * D] += row_sum(d_proj)
    low = d_proj.astype(BF16)
    acc_proj[...] += left_product(flat(attended), low)
    d_heads = right_product(low, right[:, 2 * D : 3 * D]).astype(BF16)
    factor = 1.0 / math.sqrt(HEAD)
    masks, plain = head_masks(factor), head_masks(1.0)
    mixed = []
    for slot in range(STEP):
        rows = slice(slot * SEQ, (slot + 1) * SEQ)
        d_query, d_keys, d_values = [], [], []
        for pair in range(HEADS // 2):
            span = slice(pair * 2 * HEAD, (pair + 1) * 2 * HEAD)
            queries = both_heads(qkv[slot, :, span], masks)
            keys = qkv[slot, :, D + pair * 2 * HEAD : D + (pair + 1) * 2 * HEAD]
            heads_in = qkv[slot, :, 2 * D + pair * 2 * HEAD : 2 * D + (pair + 1) * 2 * HEAD]
            d_pair = both_heads(d_heads[rows, span], plain)
            probs = softmax_keys(right_product(keys, queries))
            d_probs = right_product(heads_in, d_pair)
            d_values.append(dot_nn(probs.astype(BF16), d_pair))
            weighted = probs * d_probs
            d_scores = (weighted - probs * jnp.sum(weighted, axis=0, keepdims=True)).astype(BF16)
            d_keys.append(dot_nn(d_scores, queries))
            d_query.append(merge_heads(left_product(d_scores, keys)) * factor)
        d_query = jnp.concatenate(d_query, axis=1)
        d_values = jnp.concatenate(d_values, axis=1)
        bias[:, 6 * D : 7 * D] += row_sum(d_query)
        bias[:, 7 * D : 8 * D] += row_sum(d_values)
        mixed.append(
            jnp.concatenate(
                [d_query.astype(BF16), jnp.concatenate(d_keys, axis=1).astype(BF16), d_values.astype(BF16)], axis=1
            )
        )
    mixed = mixed[0] if STEP == 1 else jnp.concatenate(mixed, axis=0)
    normed, rstd = norm_stats(flat(hidden).astype(F32))
    scale = mod_part(mod, step, 1)
    shifted = (normed * (1.0 + scale) + mod_part(mod, step, 0)).astype(BF16)
    acc[...] += left_product(shifted, mixed)
    d_normed = right_product(mixed[:, :D], left[:, 6 * D :]) + right_product(mixed[:, D:], right[:, : 2 * D])
    put_sums(d_mod, step, 0, d_normed)
    put_sums(d_mod, step, 1, d_normed * normed)
    d_hidden[...] = (d_mid + norm_backward(d_normed, normed, rstd, scale)).reshape(STEP, SEQ, D)

    @pl.when(step == SLOT // STEP - 1)
    def _():
        rows = D // chips
        bias[:, 9 * D :] = bias_in[...]
        total = d_cond_in[...]
        for part in range(6):
            grads = d_mod[SLOT * part : SLOT * (part + 1), :]
            bias[:, part * D : (part + 1) * D] = row_sum(grads)
            total = total + right_product(grads.astype(BF16), left[:, part * D : (part + 1) * D])
        if first:
            wide_cond = cond[...].astype(F32)
            gate = 1.0 / (1.0 + jnp.exp(-wide_cond))
            total = total * (gate * (1.0 + wide_cond * (1.0 - gate)))
        d_cond[...] = total
        low_mod = d_mod[...].astype(BF16)
        is_odd = core[0] == 1
        for chip in range(chips):
            span = slice(rows * chip, rows * (chip + 1))
            even = acc[span, : 2 * D]
            odd = jnp.concatenate([acc[span, 2 * D :], acc_proj[span, :]], axis=1)
            tails = []
            for half in range(2):
                pieces = []
                for part in range(2):
                    chunk = 4 * chip + 2 * half + part
                    if chunk < BIAS // 128:
                        pieces.append(bias[:, chunk * 128 : (chunk + 1) * 128])
                    else:
                        pieces.append(jnp.zeros((1, 128), F32))
                pieces.append(jnp.zeros((rows - 2, 128), F32))
                tails.append(jnp.concatenate(pieces, axis=0))
            step_z, step_plane = offsets(core, chip)
            keep[step_plane, step_z, :, : 2 * D] = jnp.where(is_odd, odd, even).astype(BF16)
            send[step_plane, step_z, :, : 2 * D] = jnp.where(is_odd, even, odd).astype(BF16)
            keep[step_plane, step_z, :, 2 * D :] = jnp.where(is_odd, tails[1], tails[0]).astype(BF16)
            send[step_plane, step_z, :, 2 * D :] = jnp.where(is_odd, tails[0], tails[1]).astype(BF16)
        for step_plane in range(4):
            keep[step_plane, 4, :, :D] = low_mod
            keep[step_plane, 4, :, D:] = jnp.zeros((24, D + 128), BF16)
            send[step_plane, 4] = jnp.zeros((24, 2 * D + 128), BF16)


def attention_backward(core, d_middle, hidden, record, weights, d_mod, bias, cond, d_cond, chips, first):
    _, mod, qkv, attended, projected, *_ = record
    left, right, _, _ = weights
    rows = D // chips
    return pl.pallas_call(
        functools.partial(attention_kernel, chips, first=first),
        grid=(SLOT // STEP,),
        out_shape=(
            tokens(D, F32),
            jax.ShapeDtypeStruct((SLOT, D), F32),
            jax.ShapeDtypeStruct((4, 5, rows, 2 * D + 128), BF16),
            jax.ShapeDtypeStruct((4, 5, rows, 2 * D + 128), BF16),
        ),
        in_specs=[
            SMEM,
            per_slot(D),
            per_slot(D),
            per_slot(3 * D),
            per_slot(D),
            per_slot(D),
            whole(SLOT, 6 * D),
            whole(D, HALF),
            whole(D, HALF),
            whole(24, D),
            whole(1, FF + D),
            whole(SLOT, D),
            whole(SLOT, D),
        ],
        out_specs=(
            per_slot(D),
            whole(SLOT, D),
            whole(4, 5, rows, 2 * D + 128),
            whole(4, 5, rows, 2 * D + 128),
        ),
        scratch_shapes=[
            pltpu.VMEM((D, 3 * D), F32),
            pltpu.VMEM((D, D), F32),
            pltpu.VMEM((24, D), F32),
            pltpu.VMEM((1, BIAS), F32),
        ],
        compiler_params=params_of(1, 52 if first else 36),
        cost_estimate=cost(6 * 10**9, 20 * 2**20),
        name="attention_backward",
    )(core, d_middle, hidden, qkv, attended, projected, mod, left, right, d_mod, bias, cond, d_cond)


def finish_kernel(chips, place, own_ffn, own_attn, got_ffn, got_attn, own_mod, got_mod, cond, ada_out, qkv_out, proj_out, fc1_out, fc2_out, bias_out):
    rows = D // (2 * chips)
    is_odd = place[0] == 1
    mine = 8 * place[2] + 2 * place[1] + place[0]
    take = lax.broadcasted_iota(jnp.int32, (16, D), 0)
    column = lax.broadcasted_iota(jnp.int32, (16, D), 1)
    pick = ((column == rows * mine + take) & (take < rows)).astype(F32).astype(BF16)
    chosen = [right_product(pick, cond[side].astype(BF16)).astype(BF16) for side in range(2)]
    slots = SLOT * chips
    source = lax.broadcasted_iota(jnp.int32, (slots, 24 * chips), 0)
    target = lax.broadcasted_iota(jnp.int32, (slots, 24 * chips), 1)
    block = target // 24
    chip = 4 * ((place[2] + 4 - block // 4) % 4) + ((block % 4) ^ place[1])
    places = []
    for part in range(6):
        spot = (source // SLOT == chip) & (target % 24 == SLOT * part + source % SLOT)
        spot = spot.astype(F32).astype(BF16)
        places.append([dot_nn(chosen[side], spot).astype(BF16) for side in range(2)])

    def in_rows(mods):
        return jnp.concatenate(
            [mods[level, :, step * D : (step + 1) * D] for level in range(4) for step in range(4)], axis=0
        )

    for layer in range(2):
        own, got = in_rows(own_mod.at[layer]), in_rows(got_mod.at[layer])
        even = jnp.where(is_odd, got, own)
        odd = jnp.where(is_odd, own, got)
        for part in range(6):
            block = dot_nn(places[part][0], even) + dot_nn(places[part][1], odd)
            for row in range(rows):
                start = row * 6 * D + part * D
                ada_out[layer : layer + 1, start : start + D] = block[row : row + 1]
        own = jnp.where(is_odd, own_ffn[layer, rows:, :], own_ffn[layer, :rows, :])
        got = got_ffn[layer]
        first = jnp.where(is_odd, got, own[:, : 2 * D])
        second = jnp.where(is_odd, own[:, : 2 * D], got)
        for row in range(rows):
            fc1_out[layer : layer + 1, row * FF : row * FF + 2 * D] = first[row : row + 1]
            fc1_out[layer : layer + 1, row * FF + 2 * D : (row + 1) * FF] = second[row : row + 1]
        for row in range(4 * rows):
            column_start = (2 + row // (2 * rows)) * D
            fc2_out[layer : layer + 1, row * D : (row + 1) * D] = own_ffn[
                layer, row % (2 * rows) : row % (2 * rows) + 1, column_start : column_start + D
            ]
        own = jnp.where(is_odd, own_attn[layer, rows:, :], own_attn[layer, :rows, :])
        got = got_attn[layer]
        first = jnp.where(is_odd, got, own[:, : 2 * D])
        second = jnp.where(is_odd, own[:, : 2 * D], got)
        for row in range(rows):
            qkv_out[layer : layer + 1, row * 3 * D : row * 3 * D + 2 * D] = first[row : row + 1]
            qkv_out[layer : layer + 1, row * 3 * D + 2 * D : (row + 1) * 3 * D] = second[row : row + 1, :D]
            proj_out[layer : layer + 1, row * D : (row + 1) * D] = second[row : row + 1, D:]
        for part in range(2):
            bias_out[layer : layer + 1, part * 128 : (part + 1) * 128] = own_attn[
                layer, part : part + 1, 2 * D : 2 * D + 128
            ]


def finish(place, own_ffn, own_attn, got_ffn, got_attn, own_mod, got_mod, cond, shapes, chips):
    return pl.pallas_call(
        functools.partial(finish_kernel, chips),
        out_shape=tuple(jax.ShapeDtypeStruct(shape, F32) for shape in shapes),
        in_specs=[SMEM] + [VMEM] * 7,
        out_specs=(VMEM,) * 6,
        compiler_params=params_of(),
        name="finish",
    )(place, own_ffn, own_attn, got_ffn, got_attn, own_mod, got_mod, cond)


def fast_body(
    latents_in, condition, counts, ada_weight, qkv_weight, proj_weight, fc1_weight, fc2_weight, biases, cotangent
):
    devices = lax.axis_size("fsdp")
    chips = devices // 2
    rows = D // devices
    index = lax.axis_index("fsdp")
    swap = [(one, one ^ 1) for one in range(devices)]

    lines = [[8 * level + one for level in range(4)] for one in range(8)]
    place = core = jnp.stack([index % 2, index // 2 % 4, index // 8])
    tie = lax.optimization_barrier

    def along(value, bit):
        return lax.ppermute(value, "fsdp", [(one, one ^ bit) for one in range(devices)])

    def stacked(copies):
        return lax.all_to_all(copies, "fsdp", 0, 0, axis_index_groups=lines, tiled=True)

    def with_other_core(held):
        return [*held, *[(along(block, 1), (1, *spot[1:])) for block, spot in held]]

    def planes_of(stack, column):
        return [(stack if step == 0 else along(stack, 2 * step), (0, step, 0, column)) for step in range(4)]

    copies_left, copies_right, copies_last = pack(
        ada_weight, qkv_weight, proj_weight, fc1_weight, fc2_weight, biases, condition, rows, 4
    )
    stack_left, copies_right = tie((stacked(copies_left), copies_right))
    stack_right, copies_last = tie((stacked(copies_right), copies_last))
    blocks, stack_right = tie(([block for block, _ in planes_of(stack_left, 0)], stack_right))
    planes_left = [(block, (0, step, 0, 0)) for step, block in enumerate(blocks)]
    planes_right = planes_of(stack_right, WIRE // 2)
    stack_last = stacked(copies_last)
    held_first = [*with_other_core(planes_left), *with_other_core(planes_right)]
    stack_last, place = tie((stack_last, place))
    *first_weights, cond_all = unpack_wire(place, held_first)
    planes_last = planes_of(stack_last, 0)
    first = forward_block(counts, latents_in, condition, first_weights, False)
    blocks, first = tie(([block for block, _ in planes_last], first))
    held_last = with_other_core([(block, spot) for block, (_, spot) in zip(blocks, planes_last, strict=True)])
    *last_weights, _ = unpack_wire(place, held_last)
    last = forward_block(counts, first[0], condition, last_weights, True)
    weights, records, hidden = [first_weights, last_weights], [first, last], [latents_in, first[0], last[0]]
    upstream = cotangent
    d_cond = jnp.zeros((SLOT, D), F32)

    def paired(keep, send):
        got = lax.ppermute(send, "fsdp", swap)
        return [(keep[step].astype(F32) + got[step].astype(F32)).astype(BF16) for step in range(4)]

    def in_plane(parts):
        return [parts[step] if step == 0 else along(parts[step], 2 * step) for step in range(4)]

    def in_line(parts):
        def shifted(value, step):
            return lax.ppermute(value, "fsdp", [(one, (one + 8 * step) % devices) for one in range(devices)])

        return [parts[step] if step == 0 else shifted(parts[step], step) for step in range(4)]

    def plane_sums(parts):
        return [sum(part[level].astype(F32) for part in parts).astype(BF16) for level in range(4)]

    def with_mods(parts):
        mods = [part[4, :, :D] for part in parts]
        return [jnp.concatenate([level, *mods], axis=1) for level in plane_sums(parts)]

    def total(parts):
        return sum(part.astype(F32) for part in parts)

    d_middle, d_mod, bias, *wire = ffn_backward(core, counts, upstream, records[1], weights[1], chips, True)
    d_middle, both = tie((d_middle, paired(*wire)))
    ffn_last = in_plane(both)
    upstream, d_cond, *wire = attention_backward(
        core, d_middle, hidden[1], records[1], weights[1], d_mod, bias, condition, d_cond, chips, False
    )
    upstream, wire, ffn_last = tie((upstream, wire, ffn_last))
    upstream, both, sums = tie((upstream, paired(*wire), plane_sums(ffn_last)))
    ffn_last, attn_last = in_line(sums), in_plane(both)
    d_middle, d_mod, bias, *wire = ffn_backward(core, counts, upstream, records[0], weights[0], chips, False)
    d_middle, wire, ffn_last, attn_last = tie((d_middle, wire, ffn_last, attn_last))
    d_middle, both, sums = tie((d_middle, paired(*wire), with_mods(attn_last)))
    attn_last, ffn_first = in_line(sums), in_plane(both)
    upstream, d_cond, *wire = attention_backward(
        core, d_middle, hidden[0], records[0], weights[0], d_mod, bias, condition, d_cond, chips, True
    )
    wire, attn_last, ffn_first = tie((wire, attn_last, ffn_first))
    both, sums = tie((paired(*wire), plane_sums(ffn_first)))
    attn_first, ffn_first = in_plane(both), in_line(sums)
    attn_first = in_line(with_mods(attn_first))
    width = 2 * D + 128
    own_ffn = jnp.stack([total(ffn_first), total(ffn_last)])
    own_attn = jnp.stack([total([part[:, :width] for part in parts]) for parts in (attn_first, attn_last)])
    own_mod = jnp.stack([jnp.stack([part[:, width:] for part in parts]) for parts in (attn_first, attn_last)])
    start = (1 - index % 2) * rows
    to_send = jnp.concatenate([own_ffn[:, :, : 2 * D], own_attn[:, :, : 2 * D]], axis=2)
    got = lax.ppermute(lax.dynamic_slice_in_dim(to_send, start, rows, axis=1), "fsdp", swap)
    got_mod = lax.ppermute(own_mod, "fsdp", swap)
    shapes = [array.shape for array in (ada_weight, qkv_weight, proj_weight, fc1_weight, fc2_weight, biases)]
    grads = finish(
        place, own_ffn, own_attn, got[:, :, : 2 * D], got[:, :, 2 * D :], own_mod, got_mod, cond_all, shapes, chips
    )
    return (hidden[2], upstream, d_cond, *grads)


def choose_body(
    latents_in, condition, counts, ada_weight, qkv_weight, proj_weight, fc1_weight, fc2_weight, biases, cotangent
):
    devices = lax.axis_size("fsdp")
    rows = D // devices
    fits = (
        D % devices == 0
        and devices == 32
        and latents_in.shape == (SLOT, SEQ, D)
        and ada_weight.shape == (2, rows * 6 * D)
        and qkv_weight.shape == (2, rows * 3 * D)
        and proj_weight.shape == (2, rows * D)
        and fc1_weight.shape == (2, rows * FF)
        and fc2_weight.shape == (2, rows * FF)
        and biases.shape == (2, 256)
    )
    chosen = fast_body if fits else body
    return chosen(
        latents_in, condition, counts, ada_weight, qkv_weight, proj_weight, fc1_weight, fc2_weight, biases, cotangent
    )


def solution(mesh):
    return jax.shard_map(
        choose_body,
        mesh=mesh,
        in_specs=(
            P("fsdp", None, None),
            P("fsdp", None),
            P("fsdp"),
            P(None, "fsdp"),
            P(None, "fsdp"),
            P(None, "fsdp"),
            P(None, "fsdp"),
            P(None, "fsdp"),
            P(None, "fsdp"),
            P("fsdp", None, None),
        ),
        out_specs=(
            P("fsdp", None, None),
            P("fsdp", None, None),
            P("fsdp", None),
            P(None, "fsdp"),
            P(None, "fsdp"),
            P(None, "fsdp"),
            P(None, "fsdp"),
            P(None, "fsdp"),
            P(None, "fsdp"),
        ),
        check_vma=False,
    )
```

```python
import functools
import math

import jax
import jax.numpy as jnp
from jax import lax
from jax.experimental import pallas as pl
from jax.experimental.pallas import tpu as pltpu
from jax.sharding import PartitionSpec as P

D = 384
HEADS = 6
HEAD = 64
FF = 1536


EPSILON = 1e-06


def modulate_norm(values_in, shift_add, scale_mul):
    centred = values_in - jnp.mean(values_in, axis=-1, keepdims=True)
    variance = jnp.mean(centred * centred, axis=-1, keepdims=True)
    normed = centred * lax.rsqrt(variance + EPSILON)
    return normed * (1.0 + scale_mul[:, None, :]) + shift_add[:, None, :]


def gelu_tanh(values_in):
    return jax.nn.gelu(values_in, approximate=True)


def left_product(left, right):
    return lax.dot_general(
        left, right, (((0,), (0,)), ((), ())), preferred_element_type=jnp.float32
    )


def right_product(left, right):
    return lax.dot_general(
        left, right, (((1,), (1,)), ((), ())), preferred_element_type=jnp.float32
    )


def unpack(gathered):
    ada_flat, qkv_flat, proj_flat, fc1_flat, fc2_flat, bias_flat = gathered
    bias_wide = bias_flat.astype(jnp.float32)
    return (
        ada_flat.reshape(D, 6 * D),
        qkv_flat[: 3 * D * D].reshape(D, 3 * D),
        proj_flat[: D * D].reshape(D, D),
        fc1_flat.reshape(D, FF),
        fc2_flat.reshape(FF, D),
        bias_wide[: 6 * D],
        bias_wide[6 * D : 7 * D],
        bias_wide[7 * D : 8 * D],
        bias_wide[8 * D : 9 * D],
        bias_wide[9 * D : 9 * D + FF],
        bias_wide[9 * D + FF : 10 * D + FF],
    )


def split_modulation(modulation):
    return [modulation[:, part_index * D : (part_index + 1) * D] for part_index in range(6)]


def layer_forward(hidden, cond_act, params):
    w_ada, w_qkv, w_proj, w_fc1, w_fc2, b_ada, b_query, b_value, b_proj, b_fc1, b_fc2 = params
    slot_count, seq_len = (hidden.shape[0], hidden.shape[1])
    modulation = jnp.dot(cond_act, w_ada, preferred_element_type=jnp.float32) + b_ada
    shift_attn, scale_attn, gate_attn, shift_ffn, scale_ffn, gate_ffn = split_modulation(modulation)
    normed_attn = modulate_norm(hidden, shift_attn, scale_attn).astype(jnp.bfloat16).reshape(-1, D)
    mixed_qkv = jnp.dot(normed_attn, w_qkv, preferred_element_type=jnp.float32)
    queries = (
        (mixed_qkv[:, 0:D] + b_query).astype(jnp.bfloat16).reshape(slot_count, seq_len, HEADS, HEAD)
    )
    key_heads = (
        mixed_qkv[:, D : 2 * D].astype(jnp.bfloat16).reshape(slot_count, seq_len, HEADS, HEAD)
    )
    value_heads = (
        (mixed_qkv[:, 2 * D : 3 * D] + b_value)
        .astype(jnp.bfloat16)
        .reshape(slot_count, seq_len, HEADS, HEAD)
    )
    scores = jnp.einsum(
        "bqhd,bkhd->bhqk", queries, key_heads, preferred_element_type=jnp.float32
    ) * (1.0 / math.sqrt(HEAD))
    peak_score = jnp.max(scores, axis=-1, keepdims=True)
    exp_scores = jnp.exp(scores - peak_score)
    exp_total = jnp.sum(exp_scores, axis=-1, keepdims=True)
    logsum = peak_score + jnp.log(exp_total)
    attn_probs = (exp_scores / exp_total).astype(jnp.bfloat16)
    attended = jnp.einsum(
        "bhqk,bkhd->bqhd", attn_probs, value_heads, preferred_element_type=jnp.float32
    )
    attended = attended.astype(jnp.bfloat16).reshape(-1, D)
    projected = (jnp.dot(attended, w_proj, preferred_element_type=jnp.float32) + b_proj).reshape(
        slot_count, seq_len, D
    )
    middle = hidden + gate_attn[:, None, :] * projected
    normed_ffn = modulate_norm(middle, shift_ffn, scale_ffn).astype(jnp.bfloat16).reshape(-1, D)
    pre_act = jnp.dot(normed_ffn, w_fc1, preferred_element_type=jnp.float32) + b_fc1
    activation = gelu_tanh(pre_act).astype(jnp.bfloat16)
    branch = (jnp.dot(activation, w_fc2, preferred_element_type=jnp.float32) + b_fc2).reshape(
        slot_count, seq_len, D
    )
    result = middle + gate_ffn[:, None, :] * branch
    record = (
        hidden,
        modulation,
        normed_attn,
        queries,
        key_heads,
        value_heads,
        logsum,
        attended,
        projected,
        middle,
        normed_ffn,
        pre_act,
        activation,
        branch,
    )
    return (result, record)


def layer_backward(upstream, params, record):
    w_ada, w_qkv, w_proj, w_fc1, w_fc2, b_ada, b_query, b_value, b_proj, b_fc1, b_fc2 = params
    (
        hidden,
        modulation,
        normed_attn,
        queries,
        key_heads,
        value_heads,
        logsum,
        attended,
        projected,
        middle,
        normed_ffn,
        pre_act,
        activation,
        branch,
    ) = record
    slot_count, seq_len = (hidden.shape[0], hidden.shape[1])
    shift_attn, scale_attn, gate_attn, shift_ffn, scale_ffn, gate_ffn = split_modulation(modulation)
    d_branch = (upstream * gate_ffn[:, None, :]).reshape(-1, D)
    d_gate_ffn = jnp.sum(upstream * branch, axis=1)
    grad_b_fc2 = jnp.sum(d_branch, axis=0)
    branch_low = d_branch.astype(jnp.bfloat16)
    grad_w_fc2 = left_product(activation, branch_low)
    d_act = right_product(branch_low, w_fc2)
    gelu_out, gelu_pull = jax.vjp(gelu_tanh, pre_act)
    (d_pre,) = gelu_pull(d_act)
    grad_b_fc1 = jnp.sum(d_pre, axis=0)
    pre_low = d_pre.astype(jnp.bfloat16)
    grad_w_fc1 = left_product(normed_ffn, pre_low)
    d_normed_ffn = right_product(pre_low, w_fc1).reshape(slot_count, seq_len, D)
    norm_out, norm_pull = jax.vjp(modulate_norm, middle, shift_ffn, scale_ffn)
    middle_part, d_shift_ffn, d_scale_ffn = norm_pull(d_normed_ffn)
    d_middle = upstream + middle_part
    d_proj = (d_middle * gate_attn[:, None, :]).reshape(-1, D)
    d_gate_attn = jnp.sum(d_middle * projected, axis=1)
    grad_b_proj = jnp.sum(d_proj, axis=0)
    proj_low = d_proj.astype(jnp.bfloat16)
    grad_w_proj = left_product(attended, proj_low)
    d_attended = (
        right_product(proj_low, w_proj)
        .astype(jnp.bfloat16)
        .reshape(slot_count, seq_len, HEADS, HEAD)
    )
    scores = jnp.einsum(
        "bqhd,bkhd->bhqk", queries, key_heads, preferred_element_type=jnp.float32
    ) * (1.0 / math.sqrt(HEAD))
    attn_probs = jnp.exp(scores - logsum)
    d_probs = jnp.einsum(
        "bqhd,bkhd->bhqk", d_attended, value_heads, preferred_element_type=jnp.float32
    )
    d_values = jnp.einsum(
        "bhqk,bqhd->bkhd",
        attn_probs.astype(jnp.bfloat16),
        d_attended,
        preferred_element_type=jnp.float32,
    )
    row_inner = jnp.sum(attn_probs * d_probs, axis=-1, keepdims=True)
    d_scores = (attn_probs * (d_probs - row_inner) * (1.0 / math.sqrt(HEAD))).astype(jnp.bfloat16)
    d_query = jnp.einsum(
        "bhqk,bkhd->bqhd", d_scores, key_heads, preferred_element_type=jnp.float32
    ).reshape(-1, D)
    d_keys = jnp.einsum(
        "bhqk,bqhd->bkhd", d_scores, queries, preferred_element_type=jnp.float32
    ).reshape(-1, D)
    d_values = d_values.reshape(-1, D)
    grad_b_query = jnp.sum(d_query, axis=0)
    grad_b_value = jnp.sum(d_values, axis=0)
    mixed_low = jnp.concatenate([d_query, d_keys, d_values], axis=1).astype(jnp.bfloat16)
    grad_w_qkv = left_product(normed_attn, mixed_low)
    d_normed_attn = right_product(mixed_low, w_qkv).reshape(slot_count, seq_len, D)
    attn_out, attn_pull = jax.vjp(modulate_norm, hidden, shift_attn, scale_attn)
    hidden_part, d_shift_attn, d_scale_attn = attn_pull(d_normed_attn)
    d_hidden = d_middle + hidden_part
    d_mod = jnp.concatenate(
        [d_shift_attn, d_scale_attn, d_gate_attn, d_shift_ffn, d_scale_ffn, d_gate_ffn], axis=1
    )
    grad_b_ada = jnp.sum(d_mod, axis=0)
    mod_low = d_mod.astype(jnp.bfloat16)
    d_cond = right_product(mod_low, w_ada)
    grad_bias = jnp.concatenate(
        [grad_b_ada, grad_b_query, grad_b_value, grad_b_proj, grad_b_fc1, grad_b_fc2]
    )
    return (d_hidden, d_cond, mod_low, (grad_w_qkv, grad_w_proj, grad_w_fc1, grad_w_fc2, grad_bias))


def pad_flat(values_in, length):
    flat = values_in.reshape(-1)
    return jnp.pad(flat, (0, length - flat.shape[0]))


def body(
    latents_in,
    condition,
    counts,
    ada_weight,
    qkv_weight,
    proj_weight,
    fc1_weight,
    fc2_weight,
    biases,
    cotangent,
):
    slot_count = latents_in.shape[0]
    layer_total = ada_weight.shape[0]
    device_count = lax.axis_size("fsdp")
    rest_list = (qkv_weight, proj_weight, fc1_weight, fc2_weight, biases)
    rest_lengths = [piece.shape[1] * device_count for piece in rest_list]
    ada_shard = ada_weight.shape[1]
    occupied = (jnp.arange(slot_count) < counts[0]).astype(jnp.float32)
    cond_wide = condition.astype(jnp.float32)
    silu_out, silu_pull = jax.vjp(jax.nn.silu, cond_wide)
    cond_act = silu_out.astype(jnp.bfloat16)
    hidden = latents_in.astype(jnp.float32)
    records = []
    for layer_index in range(layer_total):
        gathered = (
            lax.all_gather(ada_weight[layer_index], "fsdp", axis=0, tiled=True),
            lax.all_gather(qkv_weight[layer_index], "fsdp", axis=0, tiled=True),
            lax.all_gather(proj_weight[layer_index], "fsdp", axis=0, tiled=True),
            lax.all_gather(fc1_weight[layer_index], "fsdp", axis=0, tiled=True),
            lax.all_gather(fc2_weight[layer_index], "fsdp", axis=0, tiled=True),
            lax.all_gather(biases[layer_index], "fsdp", axis=0, tiled=True),
        )
        params = unpack(gathered)
        hidden, record = layer_forward(hidden, cond_act, params)
        records.append(record)
    latents_out = hidden * occupied[:, None, None]
    upstream = cotangent.astype(jnp.float32) * occupied[:, None, None]
    cond_total = jnp.zeros(cond_wide.shape, jnp.float32)
    layer_sums = [None] * layer_total
    mod_lows = [None] * layer_total
    for layer_index in reversed(range(layer_total)):
        gathered = (
            lax.all_gather(ada_weight[layer_index], "fsdp", axis=0, tiled=True),
            lax.all_gather(qkv_weight[layer_index], "fsdp", axis=0, tiled=True),
            lax.all_gather(proj_weight[layer_index], "fsdp", axis=0, tiled=True),
            lax.all_gather(fc1_weight[layer_index], "fsdp", axis=0, tiled=True),
            lax.all_gather(fc2_weight[layer_index], "fsdp", axis=0, tiled=True),
            lax.all_gather(biases[layer_index], "fsdp", axis=0, tiled=True),
        )
        params = unpack(gathered)
        upstream, d_cond, mod_low, grad_parts = layer_backward(
            upstream, params, records[layer_index]
        )
        mod_lows[layer_index] = mod_low
        cond_total = cond_total + d_cond
        padded = [
            pad_flat(grad_parts[part_index], rest_lengths[part_index]) for part_index in range(5)
        ]
        layer_sums[layer_index] = (
            lax.psum_scatter(padded[0], "fsdp", scatter_dimension=0, tiled=True),
            lax.psum_scatter(padded[1], "fsdp", scatter_dimension=0, tiled=True),
            lax.psum_scatter(padded[2], "fsdp", scatter_dimension=0, tiled=True),
            lax.psum_scatter(padded[3], "fsdp", scatter_dimension=0, tiled=True),
            lax.psum_scatter(padded[4], "fsdp", scatter_dimension=0, tiled=True),
        )
    grad_rest = [
        jnp.stack([layer_sums[layer_index][part_index] for layer_index in range(layer_total)])
        for part_index in range(5)
    ]
    mod_joined = jnp.concatenate(mod_lows, axis=1)
    ada_full = left_product(
        lax.all_gather(cond_act, "fsdp", axis=0, tiled=True),
        lax.all_gather(mod_joined, "fsdp", axis=0, tiled=True),
    )
    own_start = lax.axis_index("fsdp") * ada_shard
    ada_rows = []
    for layer_index in range(layer_total):
        flat_layer = pad_flat(
            ada_full[:, layer_index * 6 * D : (layer_index + 1) * 6 * D], ada_shard * device_count
        )
        ada_rows.append(lax.dynamic_slice_in_dim(flat_layer, own_start, ada_shard))
    ada_grad = jnp.stack(ada_rows)
    (condition_grad,) = silu_pull(cond_total)
    return (
        latents_out,
        upstream,
        condition_grad,
        ada_grad,
        grad_rest[0],
        grad_rest[1],
        grad_rest[2],
        grad_rest[3],
        grad_rest[4],
    )


BF16 = jnp.bfloat16
F32 = jnp.float32
SLOT = 4
STEP = 1
CHUNK = 512
SEQ = 256
HALF = 7 * D
WIRE = HALF + 2 * D + 128
BIAS = 10 * D + FF
VMEM = pl.BlockSpec(memory_space=pltpu.VMEM)
SMEM = pl.BlockSpec(memory_space=pltpu.SMEM)


def params_of(grid_rank=0, megabytes=36):
    semantics = ("arbitrary",) * grid_rank if grid_rank else None
    return pltpu.CompilerParams(vmem_limit_bytes=megabytes * 2**20, dimension_semantics=semantics)


def dot_nn(left, right):
    return lax.dot_general(
        left, right, (((1,), (0,)), ((), ())), preferred_element_type=jnp.float32
    )


def pack_kernel(rows, ada_in, qkv_in, proj_in, fc1_in, fc2_in, bias_in, cond, out_left, out_right, out_last, ada, qkv, proj, fc1, fc2, bias, sems, wide):
    copies = [
        pltpu.make_async_copy(source, target, sems.at[place])
        for place, (source, target) in enumerate(
            ((ada_in, ada), (qkv_in, qkv), (proj_in, proj), (fc1_in, fc1), (fc2_in, fc2), (bias_in, bias))
        )
    ]
    for copy in copies:
        copy.start()
    wide[:, :, WIRE - 128 :] = jnp.zeros((2, 2 * rows, 128), F32)
    wide_cond = cond[...].astype(F32)
    act = (wide_cond / (1.0 + jnp.exp(-wide_cond))).astype(BF16).astype(F32)
    for part in range(3):
        wide[0, 8 + 4 * part : 12 + 4 * part, WIRE - 128 :] = act[:, part * 128 : part * 128 + 128]
    for copy in copies:
        copy.wait()

    def put(source, start, width, row, column):
        values = source[:, start : start + width].astype(F32)
        for layer in range(2):
            wide[layer, row : row + 1, column : column + width] = values[layer : layer + 1]

    for row in range(rows):
        put(ada, row * 6 * D, 6 * D, row, 0)
        put(qkv, row * 3 * D, D, row, 6 * D)
        put(qkv, row * 3 * D + D, 2 * D, rows + row, 0)
        put(proj, row * D, D, rows + row, 2 * D)
        put(fc1, row * FF, FF, rows + row, 3 * D)
    for row in range(4 * rows):
        put(fc2, row * D, D, row % (2 * rows), HALF + D * (row // (2 * rows)))
    put(bias, 0, 128, 0, WIRE - 128)
    put(bias, 128, 128, 1, WIRE - 128)
    low = wide[0].astype(BF16)
    low_last = wide[1].astype(BF16)
    for copy_index in range(out_last.shape[0]):
        out_left[copy_index] = low[:, : WIRE // 2]
        out_right[copy_index] = low[:, WIRE // 2 :]
        out_last[copy_index] = low_last


def pack(ada, qkv, proj, fc1, fc2, bias, cond, rows, copies):
    flat = (ada, qkv, proj, fc1, fc2, bias)
    return pl.pallas_call(
        functools.partial(pack_kernel, rows),
        out_shape=tuple(
            jax.ShapeDtypeStruct((copies, 2 * rows, width), BF16) for width in (WIRE // 2, WIRE // 2, WIRE)
        ),
        in_specs=[pl.BlockSpec(memory_space=pltpu.HBM)] * 6 + [VMEM],
        out_specs=(VMEM,) * 3,
        scratch_shapes=[pltpu.VMEM(array.shape, BF16) for array in flat]
        + [pltpu.SemaphoreType.DMA((6,)), pltpu.VMEM((2, 2 * rows, WIRE), F32)],
        compiler_params=params_of(0, 62),
        name="pack",
    )(*flat, cond)


def unpack_kernel(rows, spots, place, *refs):
    blocks, (left, right, down, bias, cond, wire, sems) = refs[:-7], refs[-7:]
    copies = []
    for number, (block, (side, step, level, column)) in enumerate(zip(blocks, spots, strict=True)):
        target = wire.at[
            (place[0] + side) % 2,
            place[1] ^ step,
            pl.ds(level, block.shape[0]),
            :,
            pl.ds(column, block.shape[2]),
        ]
        copies.append(pltpu.make_async_copy(block, target, sems.at[number]))
    for copy in copies:
        copy.start()
    for copy in copies:
        copy.wait()

    def of(device):
        return wire.at[device % 2, (device // 2) % 4, device // 8]

    for group in range(8):
        for half, target in ((0, left), (1, right)):
            target[4 * rows * group : 4 * rows * (group + 1), :] = jnp.concatenate(
                [of(4 * group + member)[half * rows : (half + 1) * rows, :HALF] for member in range(4)], axis=0
            )
    for device in range(32):
        for part in range(2):
            start = 4 * rows * device + 2 * rows * part
            column = HALF + D * part
            down[start : start + 2 * rows, :] = of(device)[:, column : column + D]
        tail = of(device)[:, WIRE - 128 :].astype(F32)
        for part in range(2):
            chunk = 2 * device + part
            if chunk < BIAS // 128:
                bias[0:1, chunk * 128 : chunk * 128 + 128] = tail[part : part + 1]
        for part in range(3):
            cond[device % 2, 4 * (device // 2) : 4 * (device // 2) + 4, part * 128 : part * 128 + 128] = tail[
                8 + 4 * part : 12 + 4 * part
            ]


def unpack_wire(place, held):
    blocks, spots = [block for block, _ in held], [spot for _, spot in held]
    rows = blocks[0].shape[1] // 2
    return pl.pallas_call(
        functools.partial(unpack_kernel, rows, spots),
        out_shape=(
            jax.ShapeDtypeStruct((D, HALF), BF16),
            jax.ShapeDtypeStruct((D, HALF), BF16),
            jax.ShapeDtypeStruct((FF, D), BF16),
            jax.ShapeDtypeStruct((1, BIAS), F32),
            jax.ShapeDtypeStruct((2, SLOT * 16, D), F32),
        ),
        in_specs=[SMEM] + [pl.BlockSpec(memory_space=pl.ANY)] * len(blocks),
        out_specs=(VMEM,) * 5,
        scratch_shapes=[pltpu.VMEM((2, 4, 4, 2 * rows, WIRE), BF16), pltpu.SemaphoreType.DMA((len(blocks),))],
        compiler_params=params_of(0, 24),
        name="unpack",
    )(place, *blocks)


def norm_stats(values):
    centred = values - jnp.mean(values, axis=-1, keepdims=True)
    rstd = lax.rsqrt(jnp.mean(centred * centred, axis=-1, keepdims=True) + EPSILON)
    return centred * rstd, rstd


def mod_part(mod, step, part):
    rows = [
        jnp.broadcast_to(mod[pl.ds(STEP * step + slot, 1), part * D : (part + 1) * D], (SEQ, D))
        for slot in range(STEP)
    ]
    return rows[0] if STEP == 1 else jnp.concatenate(rows, axis=0)


def put_sums(d_mod, step, part, values):
    for slot in range(STEP):
        d_mod[pl.ds(SLOT * part + STEP * step + slot, 1), :] = row_sum(values[slot * SEQ : (slot + 1) * SEQ])


def occupied(counts, step):
    rows = [
        jnp.full((SEQ, 1), jnp.where(STEP * step + slot < counts[0], 1.0, 0.0), F32) for slot in range(STEP)
    ]
    return rows[0] if STEP == 1 else jnp.concatenate(rows, axis=0)


def flat(ref):
    return ref[...].reshape(STEP * SEQ, ref.shape[2])


def gelu_and_slope(pre):
    factor, cubic = 0.7978845608028654, 0.044715
    square = pre * pre
    half = 0.5 + 0.5 * jnp.tanh(pre * (factor + (factor * cubic) * square))
    act = pre * half
    return act, half + act * (1.0 - half) * (2.0 * factor + (6.0 * factor * cubic) * square)


def row_sum(values):
    return jnp.sum(values, axis=0, keepdims=True)


def head_masks(factor):
    lane = lax.broadcasted_iota(jnp.int32, (1, 2 * HEAD), 1)
    first = jnp.where(lane < HEAD, factor, 0.0).astype(BF16)
    second = jnp.where(lane < HEAD, 0.0, factor).astype(BF16)
    return first, second


def both_heads(pair, masks):
    return jnp.concatenate([pair * masks[0], pair * masks[1]], axis=0)


def merge_heads(stack):
    lane = lax.broadcasted_iota(jnp.int32, (SEQ, 2 * HEAD), 1)
    return jnp.where(lane < HEAD, stack[:SEQ], stack[SEQ:])


def softmax_keys(scores):
    raised = jnp.exp(scores - jnp.max(scores, axis=0, keepdims=True))
    return raised * (1.0 / jnp.sum(raised, axis=0, keepdims=True))


def forward_kernel(counts, hidden, cond, left, right, down, bias, out, mod, qkv, attended, projected, middle, active, slope, branch, *, last):
    step = pl.program_id(0)

    @pl.when(step == 0)
    def _():
        wide_cond = cond[...].astype(F32)
        act = (wide_cond / (1.0 + jnp.exp(-wide_cond))).astype(BF16)
        mod[...] = dot_nn(act, left[:, : 6 * D]) + bias[:, : 6 * D]

    values = flat(hidden).astype(F32)
    normed, _ = norm_stats(values)
    normed = (normed * (1.0 + mod_part(mod, step, 1)) + mod_part(mod, step, 0)).astype(BF16)
    queries = (dot_nn(normed, left[:, 6 * D :]) + bias[:, 6 * D : 7 * D]).astype(BF16)
    mixed = dot_nn(normed, right[:, : 2 * D])
    keys = mixed[:, :D].astype(BF16)
    heads_in = (mixed[:, D:] + bias[:, 7 * D : 8 * D]).astype(BF16)
    qkv[:, :, :D] = queries.reshape(STEP, SEQ, D)
    qkv[:, :, D : 2 * D] = keys.reshape(STEP, SEQ, D)
    qkv[:, :, 2 * D :] = heads_in.reshape(STEP, SEQ, D)
    masks = head_masks(1.0 / math.sqrt(HEAD))
    joined = []
    for slot in range(STEP):
        rows = slice(slot * SEQ, (slot + 1) * SEQ)
        pairs = []
        for pair in range(HEADS // 2):
            span = slice(pair * 2 * HEAD, (pair + 1) * 2 * HEAD)
            probs = softmax_keys(right_product(keys[rows, span], both_heads(queries[rows, span], masks)))
            pairs.append(merge_heads(left_product(probs.astype(BF16), heads_in[rows, span])).astype(BF16))
        joined.append(jnp.concatenate(pairs, axis=1))
    joined = joined[0] if STEP == 1 else jnp.concatenate(joined, axis=0)
    attended[...] = joined.reshape(STEP, SEQ, D)
    proj = dot_nn(joined, right[:, 2 * D : 3 * D]) + bias[:, 8 * D : 9 * D]
    projected[...] = proj.reshape(STEP, SEQ, D)
    mid = values + mod_part(mod, step, 2) * proj
    middle[...] = mid.reshape(STEP, SEQ, D)
    normed, _ = norm_stats(mid)
    normed = (normed * (1.0 + mod_part(mod, step, 4)) + mod_part(mod, step, 3)).astype(BF16)
    ffn = bias[:, 9 * D + FF :]
    for start in range(0, FF, CHUNK):
        stop = start + CHUNK
        pre = dot_nn(normed, right[:, 3 * D + start : 3 * D + stop]) + bias[:, 9 * D + start : 9 * D + stop]
        act, rate = gelu_and_slope(pre)
        act = act.astype(BF16)
        active[:, :, start:stop] = act.reshape(STEP, SEQ, CHUNK)
        slope[:, :, start:stop] = rate.reshape(STEP, SEQ, CHUNK)
        ffn = ffn + dot_nn(act, down[start:stop, :])
    branch[...] = ffn.reshape(STEP, SEQ, D)
    result = mid + mod_part(mod, step, 5) * ffn
    if last:
        result = result * occupied(counts, step)
    out[...] = result.reshape(STEP, SEQ, D)


def per_slot(width):
    return pl.BlockSpec((STEP, SEQ, width), lambda step: (step, 0, 0))


def whole(*shape):
    return pl.BlockSpec(shape, lambda step: (0,) * len(shape))


def tokens(width, dtype):
    return jax.ShapeDtypeStruct((SLOT, SEQ, width), dtype)


def cost(flops, moved):
    return pl.CostEstimate(flops=flops, bytes_accessed=moved, transcendentals=0)


def forward_block(counts, hidden, cond, weights, last):
    left, right, down, bias = weights
    return pl.pallas_call(
        functools.partial(forward_kernel, last=last),
        grid=(SLOT // STEP,),
        out_shape=(
            tokens(D, F32),
            jax.ShapeDtypeStruct((SLOT, 6 * D), F32),
            tokens(3 * D, BF16),
            tokens(D, BF16),
            tokens(D, F32),
            tokens(D, F32),
            tokens(FF, BF16),
            tokens(FF, F32),
            tokens(D, F32),
        ),
        in_specs=[
            SMEM,
            per_slot(D),
            whole(SLOT, D),
            whole(D, HALF),
            whole(D, HALF),
            whole(FF, D),
            whole(1, BIAS),
        ],
        out_specs=(
            per_slot(D),
            whole(SLOT, 6 * D),
            per_slot(3 * D),
            per_slot(D),
            per_slot(D),
            per_slot(D),
            per_slot(FF),
            per_slot(FF),
            per_slot(D),
        ),
        compiler_params=params_of(1, 36),
        cost_estimate=cost(5 * 10**9, 20 * 2**20),
        name="forward_block",
    )(counts, hidden, cond, left, right, down, bias)


def norm_backward(d_normed, normed, rstd, scale):
    inner = d_normed * (1.0 + scale)
    along = jnp.mean(inner * normed, axis=-1, keepdims=True)
    return rstd * (inner - jnp.mean(inner, axis=-1, keepdims=True) - normed * along)


def offsets(place, chip):
    return (chip // 4 + 4 - place[2]) % 4, place[1] ^ (chip % 4)


def ffn_kernel(chips, core, counts, upstream, branch, active, slope, middle, mod, right, down, d_middle, d_mod, bias, keep, send, acc_up, acc_down, *, last):
    step = pl.program_id(0)

    @pl.when(step == 0)
    def _():
        acc_up[...] = jnp.zeros_like(acc_up)
        acc_down[...] = jnp.zeros_like(acc_down)
        bias[...] = jnp.zeros_like(bias)
        d_mod[...] = jnp.zeros_like(d_mod)

    up = flat(upstream).astype(F32)
    if last:
        up = up * occupied(counts, step)
    d_branch = up * mod_part(mod, step, 5)
    put_sums(d_mod, step, 5, up * flat(branch))
    bias[:, FF:] += row_sum(d_branch)
    low = d_branch.astype(BF16)
    normed, rstd = norm_stats(flat(middle))
    scale = mod_part(mod, step, 4)
    shifted = (normed * (1.0 + scale) + mod_part(mod, step, 3)).astype(BF16)
    d_normed = 0.0
    for start in range(0, FF, CHUNK):
        stop = start + CHUNK
        d_pre = right_product(low, down[start:stop, :]) * slope[:, :, start:stop].reshape(STEP * SEQ, CHUNK)
        acc_down[start:stop, :] += left_product(active[:, :, start:stop].reshape(STEP * SEQ, CHUNK), low)
        bias[:, start:stop] += row_sum(d_pre)
        low_pre = d_pre.astype(BF16)
        acc_up[:, start:stop] += left_product(shifted, low_pre)
        d_normed = d_normed + right_product(low_pre, right[:, 3 * D + start : 3 * D + stop])
    put_sums(d_mod, step, 3, d_normed)
    put_sums(d_mod, step, 4, d_normed * normed)
    d_middle[...] = (up + norm_backward(d_normed, normed, rstd, scale)).reshape(STEP, SEQ, D)

    @pl.when(step == SLOT // STEP - 1)
    def _():
        rows = D // chips
        is_odd = core[0] == 1
        for chip in range(chips):
            span = slice(rows * chip, rows * (chip + 1))
            step_z, step_plane = offsets(core, chip)
            even, odd = acc_up[span, : 2 * D], acc_up[span, 2 * D :]
            keep[step_plane, step_z, :, : 2 * D] = jnp.where(is_odd, odd, even).astype(BF16)
            send[step_plane, step_z, :, : 2 * D] = jnp.where(is_odd, even, odd).astype(BF16)
            for part in range(2):
                start = rows * (4 * chip + part)
                even = acc_down[start : start + rows, :]
                odd = acc_down[start + 2 * rows : start + 3 * rows, :]
                columns = slice((2 + part) * D, (3 + part) * D)
                keep[step_plane, step_z, :, columns] = jnp.where(is_odd, odd, even).astype(BF16)
                send[step_plane, step_z, :, columns] = jnp.where(is_odd, even, odd).astype(BF16)


def ffn_backward(core, counts, upstream, record, weights, chips, last):
    _, mod, _, _, _, middle, active, slope, branch = record
    _, right, down, _ = weights
    rows = D // chips
    return pl.pallas_call(
        functools.partial(ffn_kernel, chips, last=last),
        grid=(SLOT // STEP,),
        out_shape=(
            tokens(D, F32),
            jax.ShapeDtypeStruct((24, D), F32),
            jax.ShapeDtypeStruct((1, FF + D), F32),
            jax.ShapeDtypeStruct((4, 4, rows, 4 * D), BF16),
            jax.ShapeDtypeStruct((4, 4, rows, 4 * D), BF16),
        ),
        in_specs=[
            SMEM,
            SMEM,
            per_slot(D),
            per_slot(D),
            per_slot(FF),
            per_slot(FF),
            per_slot(D),
            whole(SLOT, 6 * D),
            whole(D, HALF),
            whole(FF, D),
        ],
        out_specs=(
            per_slot(D),
            whole(24, D),
            whole(1, FF + D),
            whole(4, 4, rows, 4 * D),
            whole(4, 4, rows, 4 * D),
        ),
        scratch_shapes=[pltpu.VMEM((D, FF), F32), pltpu.VMEM((FF, D), F32)],
        compiler_params=params_of(1, 36),
        cost_estimate=cost(8 * 10**9, 20 * 2**20),
        name="ffn_backward",
    )(core, counts, upstream, branch, active, slope, middle, mod, right, down)


def attention_kernel(chips, core, d_middle, hidden, qkv, attended, projected, mod, left, right, d_mod_in, bias_in, cond, d_cond_in, d_hidden, d_cond, keep, send, acc, acc_proj, d_mod, bias, *, first):
    step = pl.program_id(0)

    @pl.when(step == 0)
    def _():
        acc[...] = jnp.zeros_like(acc)
        acc_proj[...] = jnp.zeros_like(acc_proj)
        bias[...] = jnp.zeros_like(bias)
        d_mod[...] = d_mod_in[...]

    d_mid = flat(d_middle)
    d_proj = d_mid * mod_part(mod, step, 2)
    put_sums(d_mod, step, 2, d_mid * flat(projected))
    bias[:, 8 * D : 9 * D] += row_sum(d_proj)
    low = d_proj.astype(BF16)
    acc_proj[...] += left_product(flat(attended), low)
    d_heads = right_product(low, right[:, 2 * D : 3 * D]).astype(BF16)
    factor = 1.0 / math.sqrt(HEAD)
    masks, plain = head_masks(factor), head_masks(1.0)
    mixed = []
    for slot in range(STEP):
        rows = slice(slot * SEQ, (slot + 1) * SEQ)
        d_query, d_keys, d_values = [], [], []
        for pair in range(HEADS // 2):
            span = slice(pair * 2 * HEAD, (pair + 1) * 2 * HEAD)
            queries = both_heads(qkv[slot, :, span], masks)
            keys = qkv[slot, :, D + pair * 2 * HEAD : D + (pair + 1) * 2 * HEAD]
            heads_in = qkv[slot, :, 2 * D + pair * 2 * HEAD : 2 * D + (pair + 1) * 2 * HEAD]
            d_pair = both_heads(d_heads[rows, span], plain)
            probs = softmax_keys(right_product(keys, queries))
            d_probs = right_product(heads_in, d_pair)
            d_values.append(dot_nn(probs.astype(BF16), d_pair))
            weighted = probs * d_probs
            d_scores = (weighted - probs * jnp.sum(weighted, axis=0, keepdims=True)).astype(BF16)
            d_keys.append(dot_nn(d_scores, queries))
            d_query.append(merge_heads(left_product(d_scores, keys)) * factor)
        d_query = jnp.concatenate(d_query, axis=1)
        d_values = jnp.concatenate(d_values, axis=1)
        bias[:, 6 * D : 7 * D] += row_sum(d_query)
        bias[:, 7 * D : 8 * D] += row_sum(d_values)
        mixed.append(
            jnp.concatenate(
                [d_query.astype(BF16), jnp.concatenate(d_keys, axis=1).astype(BF16), d_values.astype(BF16)], axis=1
            )
        )
    mixed = mixed[0] if STEP == 1 else jnp.concatenate(mixed, axis=0)
    normed, rstd = norm_stats(flat(hidden).astype(F32))
    scale = mod_part(mod, step, 1)
    shifted = (normed * (1.0 + scale) + mod_part(mod, step, 0)).astype(BF16)
    acc[...] += left_product(shifted, mixed)
    d_normed = right_product(mixed[:, :D], left[:, 6 * D :]) + right_product(mixed[:, D:], right[:, : 2 * D])
    put_sums(d_mod, step, 0, d_normed)
    put_sums(d_mod, step, 1, d_normed * normed)
    d_hidden[...] = (d_mid + norm_backward(d_normed, normed, rstd, scale)).reshape(STEP, SEQ, D)

    @pl.when(step == SLOT // STEP - 1)
    def _():
        rows = D // chips
        bias[:, 9 * D :] = bias_in[...]
        total = d_cond_in[...]
        for part in range(6):
            grads = d_mod[SLOT * part : SLOT * (part + 1), :]
            bias[:, part * D : (part + 1) * D] = row_sum(grads)
            total = total + right_product(grads.astype(BF16), left[:, part * D : (part + 1) * D])
        if first:
            wide_cond = cond[...].astype(F32)
            gate = 1.0 / (1.0 + jnp.exp(-wide_cond))
            total = total * (gate * (1.0 + wide_cond * (1.0 - gate)))
        d_cond[...] = total
        low_mod = d_mod[...].astype(BF16)
        is_odd = core[0] == 1
        for chip in range(chips):
            span = slice(rows * chip, rows * (chip + 1))
            even = acc[span, : 2 * D]
            odd = jnp.concatenate([acc[span, 2 * D :], acc_proj[span, :]], axis=1)
            tails = []
            for half in range(2):
                pieces = []
                for part in range(2):
                    chunk = 4 * chip + 2 * half + part
                    if chunk < BIAS // 128:
                        pieces.append(bias[:, chunk * 128 : (chunk + 1) * 128])
                    else:
                        pieces.append(jnp.zeros((1, 128), F32))
                pieces.append(jnp.zeros((rows - 2, 128), F32))
                tails.append(jnp.concatenate(pieces, axis=0))
            step_z, step_plane = offsets(core, chip)
            keep[step_plane, step_z, :, : 2 * D] = jnp.where(is_odd, odd, even).astype(BF16)
            send[step_plane, step_z, :, : 2 * D] = jnp.where(is_odd, even, odd).astype(BF16)
            keep[step_plane, step_z, :, 2 * D :] = jnp.where(is_odd, tails[1], tails[0]).astype(BF16)
            send[step_plane, step_z, :, 2 * D :] = jnp.where(is_odd, tails[0], tails[1]).astype(BF16)
        for step_plane in range(4):
            keep[step_plane, 4, :, :D] = low_mod
            keep[step_plane, 4, :, D:] = jnp.zeros((24, D + 128), BF16)
            send[step_plane, 4] = jnp.zeros((24, 2 * D + 128), BF16)


def attention_backward(core, d_middle, hidden, record, weights, d_mod, bias, cond, d_cond, chips, first):
    _, mod, qkv, attended, projected, *_ = record
    left, right, _, _ = weights
    rows = D // chips
    return pl.pallas_call(
        functools.partial(attention_kernel, chips, first=first),
        grid=(SLOT // STEP,),
        out_shape=(
            tokens(D, F32),
            jax.ShapeDtypeStruct((SLOT, D), F32),
            jax.ShapeDtypeStruct((4, 5, rows, 2 * D + 128), BF16),
            jax.ShapeDtypeStruct((4, 5, rows, 2 * D + 128), BF16),
        ),
        in_specs=[
            SMEM,
            per_slot(D),
            per_slot(D),
            per_slot(3 * D),
            per_slot(D),
            per_slot(D),
            whole(SLOT, 6 * D),
            whole(D, HALF),
            whole(D, HALF),
            whole(24, D),
            whole(1, FF + D),
            whole(SLOT, D),
            whole(SLOT, D),
        ],
        out_specs=(
            per_slot(D),
            whole(SLOT, D),
            whole(4, 5, rows, 2 * D + 128),
            whole(4, 5, rows, 2 * D + 128),
        ),
        scratch_shapes=[
            pltpu.VMEM((D, 3 * D), F32),
            pltpu.VMEM((D, D), F32),
            pltpu.VMEM((24, D), F32),
            pltpu.VMEM((1, BIAS), F32),
        ],
        compiler_params=params_of(1, 52 if first else 36),
        cost_estimate=cost(6 * 10**9, 20 * 2**20),
        name="attention_backward",
    )(core, d_middle, hidden, qkv, attended, projected, mod, left, right, d_mod, bias, cond, d_cond)


def finish_kernel(chips, place, own_ffn, own_attn, got_ffn, got_attn, own_mod, got_mod, cond, ada_out, qkv_out, proj_out, fc1_out, fc2_out, bias_out):
    rows = D // (2 * chips)
    is_odd = place[0] == 1
    mine = 8 * place[2] + 2 * place[1] + place[0]
    take = lax.broadcasted_iota(jnp.int32, (16, D), 0)
    column = lax.broadcasted_iota(jnp.int32, (16, D), 1)
    pick = ((column == rows * mine + take) & (take < rows)).astype(F32).astype(BF16)
    chosen = [right_product(pick, cond[side].astype(BF16)).astype(BF16) for side in range(2)]
    slots = SLOT * chips
    source = lax.broadcasted_iota(jnp.int32, (slots, 24 * chips), 0)
    target = lax.broadcasted_iota(jnp.int32, (slots, 24 * chips), 1)
    block = target // 24
    chip = 4 * ((place[2] + 4 - block // 4) % 4) + ((block % 4) ^ place[1])
    places = []
    for part in range(6):
        spot = (source // SLOT == chip) & (target % 24 == SLOT * part + source % SLOT)
        spot = spot.astype(F32).astype(BF16)
        places.append([dot_nn(chosen[side], spot).astype(BF16) for side in range(2)])

    def in_rows(mods):
        return jnp.concatenate(
            [mods[level, :, step * D : (step + 1) * D] for level in range(4) for step in range(4)], axis=0
        )

    for layer in range(2):
        own, got = in_rows(own_mod.at[layer]), in_rows(got_mod.at[layer])
        even = jnp.where(is_odd, got, own)
        odd = jnp.where(is_odd, own, got)
        for part in range(6):
            block = dot_nn(places[part][0], even) + dot_nn(places[part][1], odd)
            for row in range(rows):
                start = row * 6 * D + part * D
                ada_out[layer : layer + 1, start : start + D] = block[row : row + 1]
        own = jnp.where(is_odd, own_ffn[layer, rows:, :], own_ffn[layer, :rows, :])
        got = got_ffn[layer]
        first = jnp.where(is_odd, got, own[:, : 2 * D])
        second = jnp.where(is_odd, own[:, : 2 * D], got)
        for row in range(rows):
            fc1_out[layer : layer + 1, row * FF : row * FF + 2 * D] = first[row : row + 1]
            fc1_out[layer : layer + 1, row * FF + 2 * D : (row + 1) * FF] = second[row : row + 1]
        for row in range(4 * rows):
            column_start = (2 + row // (2 * rows)) * D
            fc2_out[layer : layer + 1, row * D : (row + 1) * D] = own_ffn[
                layer, row % (2 * rows) : row % (2 * rows) + 1, column_start : column_start + D
            ]
        own = jnp.where(is_odd, own_attn[layer, rows:, :], own_attn[layer, :rows, :])
        got = got_attn[layer]
        first = jnp.where(is_odd, got, own[:, : 2 * D])
        second = jnp.where(is_odd, own[:, : 2 * D], got)
        for row in range(rows):
            qkv_out[layer : layer + 1, row * 3 * D : row * 3 * D + 2 * D] = first[row : row + 1]
            qkv_out[layer : layer + 1, row * 3 * D + 2 * D : (row + 1) * 3 * D] = second[row : row + 1, :D]
            proj_out[layer : layer + 1, row * D : (row + 1) * D] = second[row : row + 1, D:]
        for part in range(2):
            bias_out[layer : layer + 1, part * 128 : (part + 1) * 128] = own_attn[
                layer, part : part + 1, 2 * D : 2 * D + 128
            ]


def finish(place, own_ffn, own_attn, got_ffn, got_attn, own_mod, got_mod, cond, shapes, chips):
    return pl.pallas_call(
        functools.partial(finish_kernel, chips),
        out_shape=tuple(jax.ShapeDtypeStruct(shape, F32) for shape in shapes),
        in_specs=[SMEM] + [VMEM] * 7,
        out_specs=(VMEM,) * 6,
        compiler_params=params_of(),
        name="finish",
    )(place, own_ffn, own_attn, got_ffn, got_attn, own_mod, got_mod, cond)


def fast_body(
    latents_in, condition, counts, ada_weight, qkv_weight, proj_weight, fc1_weight, fc2_weight, biases, cotangent
):
    devices = lax.axis_size("fsdp")
    chips = devices // 2
    rows = D // devices
    index = lax.axis_index("fsdp")
    swap = [(one, one ^ 1) for one in range(devices)]

    lines = [[8 * level + one for level in range(4)] for one in range(8)]
    place = core = jnp.stack([index % 2, index // 2 % 4, index // 8])
    tie = lax.optimization_barrier

    def along(value, bit):
        return lax.ppermute(value, "fsdp", [(one, one ^ bit) for one in range(devices)])

    def stacked(copies):
        return lax.all_to_all(copies, "fsdp", 0, 0, axis_index_groups=lines, tiled=True)

    def with_other_core(held):
        return [*held, *[(along(block, 1), (1, *spot[1:])) for block, spot in held]]

    def planes_of(stack, column):
        return [(stack if step == 0 else along(stack, 2 * step), (0, step, 0, column)) for step in range(4)]

    copies_left, copies_right, copies_last = pack(
        ada_weight, qkv_weight, proj_weight, fc1_weight, fc2_weight, biases, condition, rows, 4
    )
    stack_left, copies_right = tie((stacked(copies_left), copies_right))
    stack_right, copies_last = tie((stacked(copies_right), copies_last))
    blocks, stack_right = tie(([block for block, _ in planes_of(stack_left, 0)], stack_right))
    planes_left = [(block, (0, step, 0, 0)) for step, block in enumerate(blocks)]
    planes_right = planes_of(stack_right, WIRE // 2)
    stack_last = stacked(copies_last)
    held_first = [*with_other_core(planes_left), *with_other_core(planes_right)]
    stack_last, place = tie((stack_last, place))
    *first_weights, cond_all = unpack_wire(place, held_first)
    planes_last = planes_of(stack_last, 0)
    first = forward_block(counts, latents_in, condition, first_weights, False)
    blocks, first = tie(([block for block, _ in planes_last], first))
    held_last = with_other_core([(block, spot) for block, (_, spot) in zip(blocks, planes_last, strict=True)])
    *last_weights, _ = unpack_wire(place, held_last)
    last = forward_block(counts, first[0], condition, last_weights, True)
    weights, records, hidden = [first_weights, last_weights], [first, last], [latents_in, first[0], last[0]]
    upstream = cotangent
    d_cond = jnp.zeros((SLOT, D), F32)

    def paired(keep, send):
        got = lax.ppermute(send, "fsdp", swap)
        return [(keep[step].astype(F32) + got[step].astype(F32)).astype(BF16) for step in range(4)]

    def in_plane(parts):
        return [parts[step] if step == 0 else along(parts[step], 2 * step) for step in range(4)]

    def in_line(parts):
        def shifted(value, step):
            return lax.ppermute(value, "fsdp", [(one, (one + 8 * step) % devices) for one in range(devices)])

        return [parts[step] if step == 0 else shifted(parts[step], step) for step in range(4)]

    def plane_sums(parts):
        return [sum(part[level].astype(F32) for part in parts).astype(BF16) for level in range(4)]

    def with_mods(parts):
        mods = [part[4, :, :D] for part in parts]
        return [jnp.concatenate([level, *mods], axis=1) for level in plane_sums(parts)]

    def total(parts):
        return sum(part.astype(F32) for part in parts)

    d_middle, d_mod, bias, *wire = ffn_backward(core, counts, upstream, records[1], weights[1], chips, True)
    d_middle, both = tie((d_middle, paired(*wire)))
    ffn_last = in_plane(both)
    upstream, d_cond, *wire = attention_backward(
        core, d_middle, hidden[1], records[1], weights[1], d_mod, bias, condition, d_cond, chips, False
    )
    upstream, wire, ffn_last = tie((upstream, wire, ffn_last))
    upstream, both, sums = tie((upstream, paired(*wire), plane_sums(ffn_last)))
    ffn_last, attn_last = in_line(sums), in_plane(both)
    d_middle, d_mod, bias, *wire = ffn_backward(core, counts, upstream, records[0], weights[0], chips, False)
    d_middle, wire, ffn_last, attn_last = tie((d_middle, wire, ffn_last, attn_last))
    d_middle, both, sums = tie((d_middle, paired(*wire), with_mods(attn_last)))
    attn_last, ffn_first = in_line(sums), in_plane(both)
    upstream, d_cond, *wire = attention_backward(
        core, d_middle, hidden[0], records[0], weights[0], d_mod, bias, condition, d_cond, chips, True
    )
    wire, attn_last, ffn_first = tie((wire, attn_last, ffn_first))
    both, sums = tie((paired(*wire), plane_sums(ffn_first)))
    attn_first = in_plane(both)
    attn_first[1], sums = tie((attn_first[1], sums))
    ffn_first = in_line(sums)
    attn_first = in_line(with_mods(attn_first))
    width = 2 * D + 128
    own_ffn = jnp.stack([total(ffn_first), total(ffn_last)])
    own_attn = jnp.stack([total([part[:, :width] for part in parts]) for parts in (attn_first, attn_last)])
    own_mod = jnp.stack([jnp.stack([part[:, width:] for part in parts]) for parts in (attn_first, attn_last)])
    start = (1 - index % 2) * rows
    to_send = jnp.concatenate([own_ffn[:, :, : 2 * D], own_attn[:, :, : 2 * D]], axis=2)
    got = lax.ppermute(lax.dynamic_slice_in_dim(to_send, start, rows, axis=1), "fsdp", swap)
    got_mod = lax.ppermute(own_mod, "fsdp", swap)
    shapes = [array.shape for array in (ada_weight, qkv_weight, proj_weight, fc1_weight, fc2_weight, biases)]
    grads = finish(
        place, own_ffn, own_attn, got[:, :, : 2 * D], got[:, :, 2 * D :], own_mod, got_mod, cond_all, shapes, chips
    )
    return (hidden[2], upstream, d_cond, *grads)


def choose_body(
    latents_in, condition, counts, ada_weight, qkv_weight, proj_weight, fc1_weight, fc2_weight, biases, cotangent
):
    devices = lax.axis_size("fsdp")
    rows = D // devices
    fits = (
        D % devices == 0
        and devices == 32
        and latents_in.shape == (SLOT, SEQ, D)
        and ada_weight.shape == (2, rows * 6 * D)
        and qkv_weight.shape == (2, rows * 3 * D)
        and proj_weight.shape == (2, rows * D)
        and fc1_weight.shape == (2, rows * FF)
        and fc2_weight.shape == (2, rows * FF)
        and biases.shape == (2, 256)
    )
    chosen = fast_body if fits else body
    return chosen(
        latents_in, condition, counts, ada_weight, qkv_weight, proj_weight, fc1_weight, fc2_weight, biases, cotangent
    )


def solution(mesh):
    return jax.shard_map(
        choose_body,
        mesh=mesh,
        in_specs=(
            P("fsdp", None, None),
            P("fsdp", None),
            P("fsdp"),
            P(None, "fsdp"),
            P(None, "fsdp"),
            P(None, "fsdp"),
            P(None, "fsdp"),
            P(None, "fsdp"),
            P(None, "fsdp"),
            P("fsdp", None, None),
        ),
        out_specs=(
            P("fsdp", None, None),
            P("fsdp", None, None),
            P("fsdp", None),
            P(None, "fsdp"),
            P(None, "fsdp"),
            P(None, "fsdp"),
            P(None, "fsdp"),
            P(None, "fsdp"),
            P(None, "fsdp"),
        ),
        check_vma=False,
    )
```
